32 devices in a mesh: rows: 16 (over z, y, x), heads: 2 (over core).
Axes of the slice: x: 2, y: 2, z: 4, core: 2. Of those that a mesh axis runs over, the one named last changes fastest.
Arguments:
- tokens: bfloat16 [32768, 768], P(('rows', 'heads')), may hold values from -6 to 6
- prompt: bfloat16 [100, 768], replicated, may hold values from -6 to 6
- segment_ids: int32 [32, 1024], P('rows'), may hold values from 0 to 3, as said below
- gain_attn: float32 [768], replicated, may hold values from 0.25 to 1.75
- w_query: bfloat16 [768, 768], P(None, 'heads'), may hold values from -0.09375 to 0.09375
- w_key: bfloat16 [768, 768], P(None, 'heads'), may hold values from -0.09375 to 0.09375
- w_value: bfloat16 [768, 768], P(None, 'heads'), may hold values from -0.21875 to 0.21875
- w_attn_out: bfloat16 [768, 768], P('heads'), may hold values from -1 to 1
- bias_table: bfloat16 [32, 12], P(None, 'heads'), may hold values from -4 to 4
- gain_ff: float32 [768], replicated, may hold values from 0.25 to 1.75
- w_in: bfloat16 [768, 3072], P(None, 'heads'), may hold values from -0.21875 to 0.21875
- w_out: bfloat16 [3072, 768], P('heads'), may hold values from -0.15625 to 0.15625
- out_grad: bfloat16 [32768, 768], P(('rows', 'heads')), may hold values from -6 to 6
Outputs:
- result: bfloat16 [32768, 768], P(('rows', 'heads'))
- grad_tokens: bfloat16 [32768, 768], P(('rows', 'heads'))
- grad_prompt: float32 [100, 768], replicated
- grad_gain_attn: float32 [768], replicated
- grad_w_query: float32 [768, 768], P(None, 'heads')
- grad_w_key: float32 [768, 768], P(None, 'heads')
- grad_w_value: float32 [768, 768], P(None, 'heads')
- grad_w_attn_out: float32 [768, 768], P('heads')
- grad_bias_table: float32 [32, 12], P(None, 'heads')
- grad_gain_ff: float32 [768], replicated
- grad_w_in: float32 [768, 3072], P(None, 'heads')
- grad_w_out: float32 [3072, 768], P('heads')
The draws below stay inside these ranges and needn't reach their ends.
Inputs may be any that keep to these rules, and one draw needn't show every extreme that they name: `segment_ids`: in each packed row of 1024 tokens the ids run from 0 to 3 in order, never falling; every segment holds 128 tokens or more, and one segment of every row exactly 128.
All inputs are finite; a program needn't handle non-finite values.
Results may differ from the reference program's by a relative error of at most 0.015.
Values may be sent and summed in bfloat16 or wider, within the bound.
A program may use at most 448 MiB of HBM per device.

```python
import jax
import jax.numpy as jnp
from jax import lax

D = 768
H = 12
DH = 64
FF = 3072
NB = 32
ROW_LEN = 1024
PROMPT = 100
NSEG = 4
MIN_SEG = 128
ROWS_ALL = 32
TOKENS = 32768


def draw_segment_ids(key, part):
    spare = ROW_LEN - NSEG * MIN_SEG
    key_cuts, key_pick = jax.random.split(key)
    cuts = jnp.sort(jax.random.randint(key_cuts, (ROWS_ALL, NSEG - 2), 0, spare + 1, dtype=jnp.int32), axis=1)
    bounds = jnp.concatenate([jnp.zeros((ROWS_ALL, 1), jnp.int32), cuts, jnp.full((ROWS_ALL, 1), spare, jnp.int32)], axis=1)
    others = (bounds[:, 1:] - bounds[:, :-1]).astype(jnp.int32)
    chosen = jax.random.randint(key_pick, (ROWS_ALL, 1), 0, NSEG, dtype=jnp.int32)
    slots = jnp.arange(NSEG, dtype=jnp.int32)[None, :]
    source = jnp.clip(slots - (slots > chosen).astype(jnp.int32), 0, NSEG - 2).astype(jnp.int32)
    source = jnp.broadcast_to(source, (ROWS_ALL, NSEG))
    extra = jnp.where(slots == chosen, 0, jnp.take_along_axis(others, source, axis=1)).astype(jnp.int32)
    lengths = (MIN_SEG + extra).astype(jnp.int32)
    ends = jnp.cumsum(lengths, axis=1).astype(jnp.int32)
    places = jnp.arange(ROW_LEN, dtype=jnp.int32)
    return jnp.sum((places[None, :, None] >= ends[:, None, :NSEG - 1]).astype(jnp.int32), axis=2).astype(jnp.int32)


def shard_levels(stream_key, shape, pieces, smallest, top_value):
    factor_of = 1.0
    for dim, parts in pieces:
        heights = jax.random.uniform(jax.random.fold_in(jax.random.fold_in(stream_key, 6), dim), (parts,), jnp.float32, smallest / len(pieces), top_value / len(pieces))
        factor_of = factor_of * jnp.repeat(jnp.exp(heights), shape[dim] // parts).reshape((-1,) + (1,) * (len(shape) - 1 - dim))
    return factor_of


def centred(key, extent, width, reach, shards=(), kind=jnp.bfloat16):
    drawn = width * jax.random.normal(key, extent, jnp.float32)
    if shards:
        drawn = drawn * shard_levels(key, extent, shards, -0.22, 0.18)
    return jnp.clip(drawn, -reach, reach).astype(kind)


def setup_inputs(seed: int = 0) -> dict:
    seeds = jax.random.split(jax.random.key(seed), 14)
    return {
        "tokens": centred(seeds[0], (TOKENS, D), 1.0, 6.0, ((0, 32),)),
        "prompt": centred(seeds[1], (PROMPT, D), 1.0, 6.0),
        "segment_ids": draw_segment_ids(jax.random.fold_in(seeds[13], 71), 0),
        "gain_attn": jnp.clip(1.0 + 0.15 * jax.random.normal(seeds[3], (D,), jnp.float32), 0.25, 1.75),
        "w_query": centred(seeds[4], (D, H * DH), (6 * D) ** -0.5, 0.09375, ((1, 2),)),
        "w_key": centred(seeds[5], (D, H * DH), (6 * D) ** -0.5, 0.09375, ((1, 2),)),
        "w_value": centred(seeds[6], (D, H * DH), D ** -0.5, 0.21875, ((1, 2),)),
        "w_attn_out": centred(seeds[7], (H * DH, D), (max(D // 24, 32)) ** -0.5, 1.0, ((0, 2),)),
        "bias_table": centred(seeds[8], (NB, H), 0.7, 4.0, ((1, 2),)),
        "gain_ff": jnp.clip(1.0 + 0.15 * jax.random.normal(seeds[9], (D,), jnp.float32), 0.25, 1.75),
        "w_in": centred(seeds[10], (D, FF), D ** -0.5, 0.21875, ((1, 2),)),
        "w_out": centred(seeds[11], (FF, D), (FF // 2) ** -0.5, 0.15625, ((0, 2),)),
        "out_grad": centred(seeds[12], (TOKENS, D), 1.0, 6.0, ((0, 32),)),
    }


@jax.custom_vjp
def low(v):
    return lax.optimization_barrier(v.astype(jnp.bfloat16)).astype(jnp.float32)

@jax.custom_vjp
def low_back(v):
    return v

def low_keep(v):
    return (low(v), None)

def low_pass(kept, grad):
    return (grad,)

def back_keep(v):
    return (v, None)

def back_low(kept, grad):
    return (low(grad),)
low.defvjp(low_keep, low_pass)
low_back.defvjp(back_keep, back_low)
bucket_edges = (12, 16, 23, 32, 46, 64, 91)
eps_norm = 1e-06
neg_fill = -1e+30
highest = lax.Precision.HIGHEST

def bucket_of(offset):
    distance = jnp.abs(offset).astype(jnp.int32)
    far_bucket = jnp.full(distance.shape, 8, jnp.int32)
    for boundary in bucket_edges:
        far_bucket = (far_bucket + (distance >= boundary).astype(jnp.int32)).astype(jnp.int32)
    near = jnp.where(distance < 8, distance, far_bucket).astype(jnp.int32)
    return (near + 16 * (offset > 0).astype(jnp.int32)).astype(jnp.int32)

def row_positions(segment_rows):
    marks = (segment_rows[:, :, None] == jnp.arange(NSEG, dtype=jnp.int32)[None, None, :]).astype(jnp.int32)
    counts = lax.optimization_barrier(jnp.sum(marks, axis=1)).astype(jnp.int32)
    starts = (jnp.cumsum(counts, axis=1).astype(jnp.int32) - counts).astype(jnp.int32)
    first_token = lax.optimization_barrier(jnp.sum(marks * starts[:, None, :], axis=2)).astype(jnp.int32)
    return (jnp.arange(ROW_LEN, dtype=jnp.int32)[None, :] - first_token).astype(jnp.int32)

def product(left, right):
    return jnp.dot(left, right, precision=highest, preferred_element_type=jnp.float32)

def normed(value, gain):
    return value * lax.rsqrt(lax.optimization_barrier(jnp.mean(value * value, axis=-1, keepdims=True)) + eps_norm) * gain

def attend_row(table_wide, buckets, queries, keys, values, segment_row):
    head_shape = (ROW_LEN, H, DH)
    bias = jnp.transpose(table_wide[buckets], (2, 0, 1))
    raw = jnp.einsum('qhd,khd->hqk', queries.reshape(head_shape), keys.reshape(head_shape), precision=highest)
    same = segment_row[:, None] == segment_row[None, :]
    scores = jnp.where(same[None], low_back(raw) + bias, neg_fill)
    shares = jax.nn.softmax(scores, axis=-1)
    mixed = jnp.einsum('hqk,khd->qhd', low(shares), values.reshape(head_shape), precision=highest)
    return mixed.reshape(ROW_LEN, H * DH)

def reference(tokens, prompt, segment_ids, gain_attn, w_query, w_key, w_value, w_attn_out, bias_table, gain_ff, w_in, w_out, out_grad):
    positions = row_positions(segment_ids.astype(jnp.int32)).reshape(TOKENS)
    is_prompt = positions < PROMPT
    picks = (positions[:, None] == jnp.arange(PROMPT, dtype=jnp.int32)[None, :]).astype(jnp.float32)
    offsets = (jnp.arange(ROW_LEN, dtype=jnp.int32)[None, :] - jnp.arange(ROW_LEN, dtype=jnp.int32)[:, None]).astype(jnp.int32)
    buckets = bucket_of(offsets)
    rows_shape = (ROWS_ALL, ROW_LEN, H * DH)
    row_step = jax.checkpoint(attend_row)

    def layer_forward(tokens_wide, prompt_wide, gain_one, query_weight, key_weight, value_weight, out_weight, table_wide, gain_two, inner_weight, outer_weight):
        looked = product(picks, prompt_wide)
        start = jnp.where(is_prompt[:, None], looked, tokens_wide)
        normed_attn = low(normed(start, gain_one))
        queries = low(low_back(product(normed_attn, query_weight)))
        keys = low(low_back(product(normed_attn, key_weight)))
        values = low(low_back(product(normed_attn, value_weight)))

        def map_row(items):
            return row_step(table_wide, buckets, items[0], items[1], items[2], items[3])
        mixed = lax.map(map_row, (queries.reshape(rows_shape), keys.reshape(rows_shape), values.reshape(rows_shape), segment_ids))
        mixed = low_back(low(mixed.reshape(TOKENS, H * DH)))
        attn = low_back(product(mixed, out_weight))
        middle = start + attn
        normed_ff = low(normed(middle, gain_two))
        pre = low_back(product(normed_ff, inner_weight))
        active = low(jax.nn.gelu(pre, approximate=False))
        feed = low_back(product(active, outer_weight))
        return middle + feed
    wide = jnp.float32
    output, pull = jax.vjp(layer_forward, tokens.astype(wide), prompt.astype(wide), gain_attn.astype(wide), w_query.astype(wide), w_key.astype(wide), w_value.astype(wide), w_attn_out.astype(wide), bias_table.astype(wide), gain_ff.astype(wide), w_in.astype(wide), w_out.astype(wide))
    grads = pull(out_grad.astype(wide))
    return (output.astype(jnp.bfloat16), grads[0].astype(jnp.bfloat16), grads[1], grads[2], grads[3], grads[4], grads[5], grads[6], grads[7], grads[8], grads[9], grads[10])
```

```python
from functools import partial
import math

import jax
import jax.numpy as jnp
from jax import lax
from jax.experimental import pallas as pl
from jax.experimental.pallas import tpu as pltpu
from jax.sharding import PartitionSpec as P

D = 768
DH = 64
NB = 32
ROW = 1024
PROMPT = 100
BIG = 1e30
EDGES = (12, 16, 23, 32, 46, 64, 91)
EPS = 1e-06
ROOT_HALF = 1.0 / math.sqrt(2.0)
DENSITY = 1.0 / math.sqrt(2.0 * math.pi)
F32 = jnp.float32
BF16 = jnp.bfloat16
FFC = 128
CH = 768
QB = 256
HOLES = 4
BT = 128
NBLK = ROW // BT


def dot_nn(a, b):
    return lax.dot_general(a, b, (((1,), (0,)), ((), ())), preferred_element_type=F32)


def dot_nt(a, b):
    return lax.dot_general(a, b, (((1,), (1,)), ((), ())), preferred_element_type=F32)


def dot_tn(a, b):
    return lax.dot_general(a, b, (((0,), (0,)), ((), ())), preferred_element_type=F32)


def iota(shape, dim):
    return lax.broadcasted_iota(jnp.int32, shape, dim)


def bucket_of(offset):
    distance = jnp.abs(offset)
    far = jnp.full(distance.shape, 8, jnp.int32)
    for edge in EDGES:
        far = far + (distance >= edge).astype(jnp.int32)
    near = jnp.where(distance < 8, distance, far)
    return near + jnp.where(offset > 0, 16, 0)


def picks_t(seg):
    lane = iota((1, ROW), 1)
    first = jnp.zeros((1, ROW), jnp.int32)
    for s in range(1, 4):
        count = jnp.sum((seg < s).astype(F32), axis=1, keepdims=True).astype(jnp.int32)
        first = jnp.where(seg == s, count, first)
    pos = lane - first
    return (iota((128, ROW), 0) == pos).astype(F32).astype(BF16)


def offset_picks(rows):
    return (bucket_of(256 - iota((rows, 512), 1)) == iota((rows, 512), 0)).astype(F32)


def key_marks(seg):
    i = iota((16, ROW), 0)
    block = iota((16, ROW), 1) // BT
    return jnp.where(i < 8, (seg == i).astype(F32), (block == i - 8).astype(F32)).astype(BF16)


def query_marks(seg, left, right):
    i = iota((16, ROW), 0)
    block = iota((16, ROW), 1) // BT
    excluded = jnp.where(jnp.logical_or(seg == i, i >= 4), 0.0, -BIG)
    j = i - 8
    far = jnp.where(j <= block - 2, left, jnp.where(j >= block + 2, right, 0.0))
    return jnp.where(i < 8, excluded, far).astype(BF16)


def attend_head(h, seg, table_f, qkv_ref, kaug, qaug, near, scores, pt_ref, mixed_ref):
    rows = pl.ds(pl.multiple_of(h * DH, DH), DH)
    values = table_f[pl.ds(h, 1), :]
    near[...] = pltpu.roll(jnp.broadcast_to(values, (BT, 512)), 0, 1, stride=1, stride_axis=0)
    qaug[0:DH, :] = qkv_ref[0, rows, :]
    kaug[0:DH, :] = qkv_ref[1, rows, :]
    qaug[DH : DH + 16, :] = query_marks(seg, values[:, 511:512], values[:, 1:2])
    vt = qkv_ref[2, rows, :]
    ka = kaug[...]
    for b in range(ROW // QB):
        cols = slice(b * QB, (b + 1) * QB)
        sc = scores.at[b % 2]
        sc[...] = dot_tn(ka, qaug[:, cols])
        for u in range(QB // BT):
            qb = b * (QB // BT) + u
            for d in (-1, 0, 1):
                kb = qb + d
                if 0 <= kb < NBLK:
                    sc[kb * BT : (kb + 1) * BT, u * BT : (u + 1) * BT] += near[
                        :, 256 - 128 * d : 384 - 128 * d
                    ]
        s = sc[...]
        peak = jnp.max(s, axis=0, keepdims=True)
        e = jnp.exp(s - peak)
        total = jnp.sum(e, axis=0, keepdims=True)
        p = (e * (1.0 / total)).astype(BF16)
        pt_ref[0, :, cols] = p
        mixed_ref[rows, cols] = dot_nn(vt, p).astype(BF16)


def project_t(w_refs, yt, qkv_ref):
    for m in range(3):
        qkv_ref[m] = dot_tn(w_refs[m][...], yt).astype(BF16)


def head_setup(seg, tab_ref, table_f, kaug):
    picks = offset_picks(NB).astype(BF16)
    table_f[...] = dot_nn(tab_ref[...], picks)
    kaug[DH : DH + 16, :] = key_marks(seg)


def forward_first(
    seg_ref, tok_ref, prompt_ref, gain_ref, wq, wk, wv, tab_ref,
    start_ref, yt_ref, qkv_ref, pt_ref, mixed_ref,
    table_f, kaug, qaug, near, scores,
):
    h = pl.program_id(0)
    seg = seg_ref[...]

    @pl.when(h == 0)
    def _():
        looked = dot_tn(picks_t(seg), prompt_ref[...])
        here = looked[:, D : D + 128] > 0.5
        tok = tok_ref[...].astype(F32)
        start = jnp.concatenate(
            [
                jnp.where(here, looked[:, c : c + 128], tok[:, c : c + 128])
                for c in range(0, D, 128)
            ],
            axis=1,
        )
        start_ref[...] = start.astype(BF16)
        inv = lax.rsqrt(jnp.mean(start * start, axis=1, keepdims=True) + EPS)
        yt = (start * inv * gain_ref[...]).astype(BF16).T
        yt_ref[...] = yt
        project_t((wq, wk, wv), yt, qkv_ref)
        head_setup(seg, tab_ref, table_f, kaug)

    attend_head(h, seg, table_f, qkv_ref, kaug, qaug, near, scores, pt_ref, mixed_ref)


def forward_second(
    seg_ref, start_ref, yt_ref, gain_ref, wq, wk, wv, tab_ref, mixed_own, wo_own, wo_oth,
    qkv_ref, pt_ref, mixed_ref, middle_ref, x_ref, xt_ref,
    table_f, kaug, qaug, near, scores,
):
    h = pl.program_id(0)
    seg = seg_ref[...]

    @pl.when(h == 0)
    def _():
        project_t((wq, wk, wv), yt_ref[...], qkv_ref)
        head_setup(seg, tab_ref, table_f, kaug)

    attend_head(h, seg, table_f, qkv_ref, kaug, qaug, near, scores, pt_ref, mixed_ref)

    @pl.when(h == pl.num_programs(0) - 1)
    def _():
        attn = dot_tn(mixed_own[...], wo_own[...]) + dot_tn(mixed_ref[...], wo_oth[...])
        middle = start_ref[...].astype(F32) + attn
        middle_ref[...] = middle
        inv = lax.rsqrt(jnp.mean(middle * middle, axis=1, keepdims=True) + EPS)
        x = (middle * inv * gain_ref[...]).astype(BF16)
        x_ref[...] = x
        xt_ref[...] = x.T


def plan_flows(n_rows):
    me = lax.axis_index("rows")
    n_bits = n_rows.bit_length() - 1
    bits = [(me // (1 << b)) % 2 for b in range(n_bits)]
    peers = [me + (1 - 2 * bits[b]) * (1 << b) for b in range(n_bits)]
    rest = list(range(3, n_bits))
    orders = [[0, 2, 1] + rest, [1, 2, 0] + rest]
    share = CH // len(orders)
    flows = []
    for f, order in enumerate(orders):
        size, base, slot = share, f * share, 0
        stages, halved = [], []
        for j, b in enumerate(order):
            if j < n_bits - 1 and size % 32 == 0:
                size = size // 2
                keep = pl.multiple_of(base + bits[b] * size, 16)
                give = pl.multiple_of(base + (1 - bits[b]) * size, 16)
                stages.append(("halve", b, give, size, keep, slot))
                halved.append((b, keep, give, size))
                base = keep
            else:
                stages.append(("swap", b, base, size, base, slot))
            slot += size
        for b, keep, give, n in reversed(halved):
            stages.append(("gather", b, keep, n, give, slot))
            slot += n
        flows.append(stages)
    return flows, peers


def ring_rows(n_rows):
    n_bits = n_rows.bit_length() - 1
    size, total = CH // 2, 0
    for j in range(n_bits):
        if j < n_bits - 1 and size % 32 == 0:
            size = size // 2
            total += size
        total += size
    return total


def whole(shape):
    n = len(shape)
    return pl.BlockSpec(shape, lambda *_: (0,) * n, pipeline_mode=pl.Buffered(1))


def whole_out(shape):
    n = len(shape)
    return pl.BlockSpec(shape, lambda *_: (0,) * n)


def sds(shape, dtype):
    return jax.ShapeDtypeStruct(shape, dtype)


def forward_scratch():
    return [
        pltpu.VMEM((8, 512), F32),
        pltpu.VMEM((DH + 16, ROW), BF16),
        pltpu.VMEM((DH + 16, ROW), BF16),
        pltpu.VMEM((BT, 512), F32),
        pltpu.VMEM((2, ROW, QB), F32),
    ]


PARAMS = dict(vmem_limit_bytes=56 * 1024 * 1024)


def run_first(seg, tok, prompt, gain, wq, wk, wv, tab):
    cols = wq.shape[1]
    heads = cols // DH
    return pl.pallas_call(
        forward_first,
        grid=(heads,),
        in_specs=[whole(a.shape) for a in (seg, tok, prompt, gain, wq, wk, wv, tab)],
        out_specs=[
            whole_out((ROW, D)),
            whole_out((D, ROW)),
            whole_out((3, cols, ROW)),
            pl.BlockSpec((1, ROW, ROW), lambda h: (h, 0, 0)),
            whole_out((cols, ROW)),
        ],
        out_shape=[
            sds((ROW, D), BF16),
            sds((D, ROW), BF16),
            sds((3, cols, ROW), BF16),
            sds((heads, ROW, ROW), BF16),
            sds((cols, ROW), BF16),
        ],
        scratch_shapes=forward_scratch(),
        compiler_params=pltpu.CompilerParams(**PARAMS),
        name="attend_own",
    )(seg, tok, prompt, gain, wq, wk, wv, tab)


def run_second(seg, start, yt, gain, wq, wk, wv, tab, mixed_own, wo_own, wo_oth):
    cols = wq.shape[1]
    heads = cols // DH
    ins = (seg, start, yt, gain, wq, wk, wv, tab, mixed_own, wo_own, wo_oth)
    return pl.pallas_call(
        forward_second,
        grid=(heads,),
        in_specs=[whole(a.shape) for a in ins],
        out_specs=[
            whole_out((3, cols, ROW)),
            pl.BlockSpec((1, ROW, ROW), lambda h: (h, 0, 0)),
            whole_out((cols, ROW)),
            whole_out((ROW, D)),
            whole_out((ROW, D)),
            whole_out((D, ROW)),
        ],
        out_shape=[
            sds((3, cols, ROW), BF16),
            sds((heads, ROW, ROW), BF16),
            sds((cols, ROW), BF16),
            sds((ROW, D), F32),
            sds((ROW, D), BF16),
            sds((D, ROW), BF16),
        ],
        scratch_shapes=forward_scratch(),
        compiler_params=pltpu.CompilerParams(**PARAMS),
        name="attend_other",
    )(*ins)


def norm_back(value, gain, grad):
    inv = lax.rsqrt(jnp.mean(value * value, axis=1, keepdims=True) + EPS)
    scaled = grad * gain
    inner = jnp.mean(scaled * value, axis=1, keepdims=True)
    back = inv * scaled - value * (inv * inv * inv * inner)
    return back, jnp.sum(grad * (value * inv), axis=0, keepdims=True)


def backward(
    n_ff, n_heads, n_rows,
    seg_ref, gain_a_ref, gain_f_ref, win_own, win_oth, wout_own, wout_oth, pt_own, pt_oth,
    x_hbm, xt_hbm, og_hbm, mid_hbm, start_hbm, yt_hbm, qkv_own_hbm, qkv_oth_hbm,
    mix_own_hbm, mix_oth_hbm, wq_own_hbm, wk_own_hbm, wv_own_hbm, wq_oth_hbm, wk_oth_hbm,
    wv_oth_hbm, wo_own_hbm, wo_oth_hbm,
    result_ref, gtok_ref, out_in, out_out, out_q, out_k, out_v, out_o, out_small,
    x, xt, og, mid, qkv, mix, gmix, wqkv, wo, feed, gnf, gnat, dst, dqkv, kaug, vaug, doaug,
    tacc, gvec, gains, ptb, g, xsend, xrecv, ring, load_sem, late_sem, pt_sem, out_sem, xs_sem, xr_sem,
    send_sem, recv_sem,
):
    s = pl.program_id(0)
    heads_half = n_heads // 2
    cols = heads_half * DH
    me = lax.axis_index("heads")
    early = [(x_hbm, x), (xt_hbm, xt), (og_hbm, og)]
    later = [
        (mid_hbm, mid),
        (qkv_own_hbm, qkv.at[0]),
        (qkv_oth_hbm, qkv.at[1]),
        (mix_own_hbm, mix.at[0]),
        (mix_oth_hbm, mix.at[1]),
        (wq_own_hbm, wqkv.at[0, 0]),
        (wk_own_hbm, wqkv.at[0, 1]),
        (wv_own_hbm, wqkv.at[0, 2]),
        (wq_oth_hbm, wqkv.at[1, 0]),
        (wk_oth_hbm, wqkv.at[1, 1]),
        (wv_oth_hbm, wqkv.at[1, 2]),
        (wo_own_hbm, wo.at[0]),
        (wo_oth_hbm, wo.at[1]),
    ]
    n_early = len(early)
    loads = [
        pltpu.make_async_copy(a, b, load_sem.at[i]) for i, (a, b) in enumerate(early + later)
    ]
    late = [
        pltpu.make_async_copy(start_hbm, x, late_sem.at[0]),
        pltpu.make_async_copy(yt_hbm, xt, late_sem.at[1]),
    ]

    def pt_start(i):
        hh = 2 * (i // 4) + i % 2
        for o, ref in enumerate((pt_own, pt_oth)):

            @pl.when((i % 4) // 2 == o)
            def _():
                pltpu.make_async_copy(ref.at[hh], ptb.at[i % 2], pt_sem.at[i % 2]).start()

    n_out = cols // 128
    n_chunks = 2 * n_ff + 4 * n_out + 1
    flows, peers = plan_flows(n_rows)
    n_stages = max(len(f) for f in flows)
    core = {"heads": 1 - me}

    def swap(slot):
        return pltpu.make_async_remote_copy(
            src_ref=xsend.at[slot],
            dst_ref=xrecv.at[slot],
            send_sem=xs_sem.at[slot],
            recv_sem=xr_sem.at[slot],
            device_id=core,
            device_id_type=pl.DeviceIdType.MESH,
        )

    def emit(c, slot, own, oth):
        for blocks, ref in ((own, g.at[c]), (oth, xsend.at[slot])):
            for b, block in enumerate(blocks):
                n = block.shape[0]
                ref[b * n : (b + 1) * n, :] = block.astype(BF16)
        swap(slot).start()

    def collect(c, slot):
        swap(slot).wait()
        g[c] = (g[c].astype(F32) + xrecv[slot].astype(F32)).astype(BF16)

    def stage_copy(f, k, c):
        kind, bit, src, n, keep, slot = flows[f][k]
        par = c % 2
        here = g.at[c, pl.ds(src, n), :]
        return pltpu.make_async_remote_copy(
            src_ref=here,
            dst_ref=ring.at[par, f, slot : slot + n, :],
            send_sem=send_sem.at[f, k, par],
            recv_sem=recv_sem.at[f, k, par],
            device_id={"rows": peers[bit]},
            device_id_type=pl.DeviceIdType.MESH,
        )

    def stage_end(f, k, c):
        kind, bit, src, n, keep, slot = flows[f][k]
        stage_copy(f, k, c).wait()
        part = ring[c % 2, f, slot : slot + n, :]
        if kind != "gather":
            part = (g[c, pl.ds(keep, n), :].astype(F32) + part.astype(F32)).astype(BF16)
        g[c, pl.ds(keep, n), :] = part

    def out_wait(par):
        pltpu.make_async_copy(g.at[0], out_in.at[:, 0:128], out_sem.at[par]).wait()

    def out_start(c):
        par = c % 2

        @pl.when(c >= 2)
        def _():
            out_wait(par)

        def wide(ref, col):
            dst = ref.at[:, pl.ds(pl.multiple_of(col * 128, 128), 128)]
            pltpu.make_async_copy(g.at[c], dst, out_sem.at[par]).start()

        def tall(ref, row):
            for b in range(D // 128):
                dst = ref.at[
                    pl.ds(pl.multiple_of(row * 128, 128), 128), b * 128 : (b + 1) * 128
                ]
                src = g.at[c, b * 128 : (b + 1) * 128, :]
                pltpu.make_async_copy(src, dst, out_sem.at[par]).start()

        base = 2 * n_ff + n_out

        @pl.when(jnp.logical_and(c < 2 * n_ff, c % 2 == 0))
        def _():
            wide(out_in, c // 2)

        @pl.when(jnp.logical_and(c < 2 * n_ff, c % 2 == 1))
        def _():
            tall(out_out, c // 2)

        @pl.when(jnp.logical_and(c >= 2 * n_ff, c < base))
        def _():
            tall(out_o, c - 2 * n_ff)

        for m, ref in enumerate((out_q, out_k, out_v)):

            @pl.when(jnp.logical_and(jnp.logical_and(c >= base, c < n_chunks - 1), (c - base) % 3 == m))
            def _():
                wide(ref, (c - base) // 3)

        @pl.when(c == n_chunks - 1)
        def _():
            tall(out_small, 0)

    hole = n_chunks - 4

    def tick(t):
        for k in range(n_stages, -1, -1):
            v = t - k
            c = jnp.where(v >= hole + HOLES, v - HOLES, v)
            valid = jnp.logical_and(c >= 0, c < n_chunks)
            valid = jnp.logical_and(valid, jnp.logical_or(v < hole, v >= hole + HOLES))

            @pl.when(valid)
            def _():
                for f in range(len(flows)):
                    if 0 < k <= len(flows[f]):
                        stage_end(f, k - 1, c)
                    if k < len(flows[f]):
                        stage_copy(f, k, c).start()
                if k == n_stages:
                    out_start(c)

    def lanes(a):
        return [a[:, k : k + 128] for k in range(0, a.shape[1], 128)]

    @pl.when(s == 0)
    def _():
        for copy in loads:
            copy.start()
        barrier = pltpu.get_barrier_semaphore()
        for peer in [{"rows": p} for p in peers] + [core]:
            pl.semaphore_signal(
                barrier, inc=1, device_id=peer, device_id_type=pl.DeviceIdType.MESH
            )
        pl.semaphore_wait(barrier, len(peers) + 1)
        for copy in loads[:n_early]:
            copy.wait()
        feed[...] = jnp.zeros(feed.shape, F32)
        gnf[...] = jnp.zeros(gnf.shape, F32)

    @pl.when(jnp.logical_and(s >= 1, s <= n_ff))
    def _():
        for j in range(2):
            collect(2 * (s - 1) + j, 3 * ((s - 1) % 2) + j)
        tick(s - 1)

    @pl.when(s < n_ff)
    def _():
        wi = jnp.concatenate([win_own[...], win_oth[...]], axis=1)
        wout = jnp.concatenate([wout_own[...], wout_oth[...]], axis=0)
        pre = dot_nn(x[...], wi)
        cdf = 0.5 * (1.0 + lax.erf(pre * ROOT_HALF))
        active = (pre * cdf).astype(BF16)
        slope = cdf + pre * jnp.exp(-0.5 * pre * pre) * DENSITY
        gact = dot_nt(og[...], wout)
        gpre = (gact * slope).astype(BF16)
        feed[...] += dot_nn(active, wout)
        gnf[...] += dot_nt(gpre, wi)
        dwin = dot_nn(xt[...], gpre)
        dwout = dot_tn(active, og[...])
        emit(2 * s, 3 * (s % 2), [dwin[:, :FFC]], [dwin[:, FFC:]])
        emit(2 * s + 1, 3 * (s % 2) + 1, lanes(dwout[:FFC]), lanes(dwout[FFC:]))

    @pl.when(s == n_ff)
    def _():
        for copy in late:
            copy.start()
        pt_start(0)
        for copy in loads[n_early:]:
            copy.wait()
        middle = mid[...]
        result_ref[...] = (middle + feed[...]).astype(BF16)
        back, gain_grad = norm_back(middle, gain_f_ref[...], gnf[...])
        gmid = og[...].astype(F32) + back
        gains[0:1, :] = gain_grad
        mid[...] = gmid
        ga = gmid.astype(BF16)
        dwo = [dot_nn(mix[o], ga) for o in range(2)]
        for j in range(n_out):
            rows = slice(j * 128, (j + 1) * 128)
            emit(2 * n_ff + j, 3 * (n_ff % 2) + j, lanes(dwo[0][rows]), lanes(dwo[1][rows]))
        for o in range(2):
            gmix[o] = dot_nt(wo[o], ga).astype(BF16)
        gnat[...] = jnp.zeros(gnat.shape, F32)
        kaug[DH:, :] = key_marks(seg_ref[...])
        vaug[DH:, :] = (iota((16, ROW), 0) < 3).astype(F32).astype(BF16)
        gvec[...] = jnp.zeros(gvec.shape, F32)
        for copy in late:
            copy.wait()

    i = s - (n_ff + 1)

    def head_back(o, pt_ref):
        hh = 2 * (i // 4) + i % 2
        rows = pl.ds(pl.multiple_of(hh * DH, DH), DH)
        dot_ = gmix[o, rows, :]
        delta = jnp.sum(dot_.astype(F32) * mix[o, rows, :].astype(F32), axis=0, keepdims=True)
        d1 = delta.astype(BF16).astype(F32)
        d2 = (delta - d1).astype(BF16).astype(F32)
        d3 = delta - d1 - d2
        k = iota((16, ROW), 0)
        vaug[0:DH, :] = qkv[o, 2, rows, :]
        kaug[0:DH, :] = qkv[o, 1, rows, :]
        doaug[0:DH, :] = dot_
        doaug[DH:, :] = jnp.where(
            k == 0, -d1, jnp.where(k == 1, -d2, jnp.where(k == 2, -d3, 0.0))
        ).astype(BF16)
        va = vaug[...]
        ka = kaug[...]
        out_rows = pl.ds(pl.multiple_of(o * 128 + (i % 2) * DH, DH), DH)
        tacc[...] = jnp.zeros(tacc.shape, F32)
        left = jnp.zeros((1, QB), F32)
        right = jnp.zeros((1, QB), F32)
        for b in range(ROW // QB):
            qs = slice(b * QB, (b + 1) * QB)
            dp = dot_tn(va, doaug[:, qs])
            ds = pt_ref[:, qs].astype(F32) * dp
            for u in range(QB // BT):
                qb = b * (QB // BT) + u
                for d in (-1, 0, 1):
                    kb = qb + d
                    if 0 <= kb < NBLK:
                        tacc[:, 256 - 128 * d : 384 - 128 * d] += ds[
                            kb * BT : (kb + 1) * BT, u * BT : (u + 1) * BT
                        ]
            dsb = ds.astype(BF16)
            dst[:, qs] = dsb
            r = dot_nn(ka, dsb)
            dqkv[0, out_rows, qs] = r[:DH].astype(BF16)
            sums = r[DH + 8 :]
            j = iota((8, QB), 0)
            block = b * (QB // BT) + iota((8, QB), 1) // BT
            left = left + jnp.sum(jnp.where(j <= block - 2, sums, 0.0), axis=0, keepdims=True)
            right = right + jnp.sum(jnp.where(j >= block + 2, sums, 0.0), axis=0, keepdims=True)
        dqkv[1, out_rows, :] = dot_nt(qkv[o, 0, rows, :], dst[...]).astype(BF16)
        dqkv[2, out_rows, :] = dot_nt(dot_, pt_ref[...]).astype(BF16)
        flip = (iota((BT, BT), 0) + iota((BT, BT), 1) == BT - 1).astype(F32).astype(BF16)
        near = tacc[...]
        high = near.astype(BF16)
        low = (near - high.astype(F32)).astype(BF16)
        turned = dot_nn(flip, high) + dot_nn(flip, low)
        skew = pltpu.roll(turned, 0, 1, stride=1, stride_axis=0)
        vec = pltpu.roll(jnp.sum(skew, axis=0, keepdims=True), 512 - (BT - 1), 1)
        lane = iota((1, 512), 1)
        vec = vec + jnp.where(lane == 511, jnp.sum(left, axis=1, keepdims=True), 0.0)
        vec = vec + jnp.where(lane == 1, jnp.sum(right, axis=1, keepdims=True), 0.0)
        owner = me + o * (1 - 2 * me)
        gvec[pl.ds(owner * heads_half + hh, 1), :] = vec

    in_heads = jnp.logical_and(i >= 0, i < n_heads)

    @pl.when(i == 0)
    def _():
        for j in range(n_out):
            collect(2 * n_ff + j, 3 * (n_ff % 2) + j)

    after_group = jnp.logical_and(jnp.logical_and(i > 0, i <= n_heads), i % 4 == 0)

    @pl.when(after_group)
    def _():
        e = i // 4 - 1
        for m in range(3):
            collect(2 * n_ff + n_out + 3 * e + m, 3 * ((n_ff + 1 + e) % 2) + m)

    @pl.when(in_heads)
    def _():
        tick(n_ff + 2 * i)
        tick(n_ff + 2 * i + 1)

    @pl.when(in_heads)
    def _():
        @pl.when(i + 1 < n_heads)
        def _():
            pt_start(i + 1)

        pltpu.make_async_copy(pt_own.at[0], ptb.at[i % 2], pt_sem.at[i % 2]).wait()
        head_back((i % 4) // 2, ptb.at[i % 2])

    @pl.when(jnp.logical_and(in_heads, i % 4 == 3))
    def _():
        grp = i // 4
        wcols = pl.ds(pl.multiple_of(grp * 128, 128), 128)
        acc = None
        for m in range(3):
            grad = dqkv[m]
            dw = dot_nt(xt[...], grad)
            emit(
                2 * n_ff + n_out + 3 * grp + m, 3 * ((n_ff + 1 + grp) % 2) + m,
                [dw[:, :128]], [dw[:, 128:]],
            )
            w = jnp.concatenate([wqkv[0, m, :, wcols], wqkv[1, m, :, wcols]], axis=1)
            part = dot_nn(w, grad)
            acc = part if acc is None else acc + part
        gnat[...] += acc

    @pl.when(i == n_heads)
    def _():
        seg = seg_ref[...]
        start = x[...].astype(F32)
        back, gain_grad = norm_back(start, gain_a_ref[...], gnat[...].T)
        gstart = mid[...] + back
        picks = picks_t(seg)
        here = dot_tn(picks, (iota((128, 128), 0) < PROMPT).astype(F32).astype(BF16)) > 0.5
        for c in range(0, D, 128):
            gtok_ref[:, c : c + 128] = jnp.where(here, 0.0, gstart[:, c : c + 128]).astype(BF16)
        high = gstart.astype(BF16)
        low = (gstart - high.astype(F32)).astype(BF16)
        gprompt = dot_nn(picks, high) + dot_nn(picks, low)
        opicks = offset_picks(128).astype(BF16)
        gv = gvec[...]
        g1 = gv.astype(BF16)
        g2 = (gv - g1.astype(F32)).astype(BF16)
        gtab = dot_nt(g1, opicks) + dot_nt(g2, opicks)
        row = iota((128, D), 0)
        small = jnp.where(row < PROMPT, gprompt, 0.0)
        small = jnp.where(row == PROMPT, gain_grad, small)
        small = jnp.where(row == PROMPT + 1, gains[0:1, :], small)
        blocks = lanes(small)
        wide = jnp.concatenate([jnp.zeros((104, 128), F32), gtab, jnp.zeros((8, 128), F32)], axis=0)
        blocks[0] = blocks[0] + wide
        last = n_ff + 1 + n_heads // 4
        emit(n_chunks - 1, 3 * (last % 2), blocks, blocks)
        t0 = n_ff + 2 * n_heads

        @pl.loop(t0, t0 + n_chunks - 1 + HOLES - t0)
        def _(t):
            tick(t)

        collect(n_chunks - 1, 3 * (last % 2))

        @pl.loop(n_chunks - 1 + HOLES, n_chunks + HOLES + n_stages)
        def _(t):
            tick(t)

        out_wait(0)
        out_wait(1)


def run_backward(
    n_rows, seg, gain_a, gain_f, win_own, win_oth, wout_own, wout_oth, pt_own, pt_oth, rest
):
    n_ff = win_own.shape[1] // FFC
    n_heads = 2 * pt_own.shape[0]
    cols = n_heads * DH // 2
    n_chunks = 2 * n_ff + 4 * (cols // 128) + 1
    first = n_ff + 1
    n_stages = 2 * (n_rows.bit_length() - 1)

    def ff(s):
        return jnp.minimum(s, n_ff - 1)

    blk_in = pl.BlockSpec((D, FFC), lambda s: (0, ff(s)))
    blk_out = pl.BlockSpec((FFC, D), lambda s: (ff(s), 0))
    anyspec = pl.BlockSpec(memory_space=pl.ANY)
    return pl.pallas_call(
        partial(backward, n_ff, n_heads, n_rows),
        grid=(first + n_heads + 1,),
        in_specs=[
            whole(seg.shape), whole(gain_a.shape), whole(gain_f.shape),
            blk_in, blk_in, blk_out, blk_out,
        ] + [anyspec] * (2 + len(rest)),
        out_specs=[whole((ROW, D)), whole((ROW, D))] + [anyspec] * 7,
        out_shape=[sds((ROW, D), BF16), sds((ROW, D), BF16)] + [
            sds(shape, BF16)
            for shape in (win_own.shape, wout_own.shape)
            + ((D, cols),) * 3 + ((cols, D), (128, D))
        ],
        scratch_shapes=[
            pltpu.VMEM((ROW, D), BF16),
            pltpu.VMEM((D, ROW), BF16),
            pltpu.VMEM((ROW, D), BF16),
            pltpu.VMEM((ROW, D), F32),
            pltpu.VMEM((2, 3, cols, ROW), BF16),
            pltpu.VMEM((2, cols, ROW), BF16),
            pltpu.VMEM((2, cols, ROW), BF16),
            pltpu.VMEM((2, 3, D, cols), BF16),
            pltpu.VMEM((2, cols, D), BF16),
            pltpu.VMEM((ROW, D), F32),
            pltpu.VMEM((ROW, D), F32),
            pltpu.VMEM((D, ROW), F32),
            pltpu.VMEM((ROW, ROW), BF16),
            pltpu.VMEM((3, 256, ROW), BF16),
            pltpu.VMEM((DH + 16, ROW), BF16),
            pltpu.VMEM((DH + 16, ROW), BF16),
            pltpu.VMEM((DH + 16, ROW), BF16),
            pltpu.VMEM((BT, 512), F32),
            pltpu.VMEM((16, 512), F32),
            pltpu.VMEM((8, D), F32),
            pltpu.VMEM((2, ROW, ROW), BF16),
            pltpu.VMEM((n_chunks, CH, 128), BF16),
            pltpu.VMEM((6, CH, 128), BF16),
            pltpu.VMEM((6, CH, 128), BF16),
            pltpu.VMEM((2, 2, ring_rows(n_rows), 128), BF16),
            pltpu.SemaphoreType.DMA((16,)),
            pltpu.SemaphoreType.DMA((2,)),
            pltpu.SemaphoreType.DMA((2,)),
            pltpu.SemaphoreType.DMA((2,)),
            pltpu.SemaphoreType.DMA((6,)),
            pltpu.SemaphoreType.DMA((6,)),
            pltpu.SemaphoreType.DMA((2, n_stages, 2)),
            pltpu.SemaphoreType.DMA((2, n_stages, 2)),
        ],
        compiler_params=pltpu.CompilerParams(
            vmem_limit_bytes=62 * 1024 * 1024, collective_id=0, has_side_effects=True
        ),
        name="backward",
    )(seg, gain_a, gain_f, win_own, win_oth, wout_own, wout_oth, pt_own, pt_oth, *rest)


def on_device(
    tokens, prompt, segment_ids, gain_attn, w_query, w_key, w_value, w_attn_out, bias_table,
    gain_ff, w_in, w_out, out_grad,
):
    me = lax.axis_index("heads")
    seg = lax.dynamic_slice_in_dim(segment_ids, me, 1, 0)
    prompt_ext = jnp.concatenate(
        [jnp.pad(prompt, ((0, 128 - PROMPT), (0, 0))), jnp.ones((128, 128), BF16)], axis=1
    )
    prompt_ext = jnp.where(jnp.arange(128)[:, None] < PROMPT, prompt_ext, 0)
    swap = [(0, 1), (1, 0)]
    heads_half = bias_table.shape[1]
    tab_own = jnp.pad(bias_table.T, ((0, 8 - heads_half), (0, 0)))

    def other(a):
        return lax.ppermute(a, "heads", swap)

    tab_oth, wq_oth, wk_oth, wv_oth = other(tab_own), other(w_query), other(w_key), other(w_value)
    wo_oth, win_oth, wout_oth = other(w_attn_out), other(w_in), other(w_out)
    gain_a, gain_f = gain_attn[None, :], gain_ff[None, :]
    start, yt, qkv_own, pt_own, mix_own = run_first(
        seg, tokens, prompt_ext, gain_a, w_query, w_key, w_value, tab_own
    )
    qkv_oth, pt_oth, mix_oth, middle, x, xt = run_second(
        seg, start, yt, gain_f, wq_oth, wk_oth, wv_oth, tab_oth, mix_own, w_attn_out, wo_oth
    )
    result, gtok, g_in, g_out, g_q, g_k, g_v, g_wo, small = run_backward(
        lax.axis_size("rows"),
        seg, gain_a, gain_f, w_in, win_oth, w_out, wout_oth, pt_own, pt_oth,
        [x, xt, out_grad, middle, start, yt, qkv_own, qkv_oth, mix_own, mix_oth,
         w_query, w_key, w_value, wq_oth, wk_oth, wv_oth, w_attn_out, wo_oth],
    )
    g_in, g_out, g_q, g_k, g_v, g_wo, small = (
        a.astype(F32) for a in (g_in, g_out, g_q, g_k, g_v, g_wo, small)
    )
    gtab = lax.dynamic_slice(small, (104 + me * heads_half, 0), (heads_half, NB)).T
    return (
        result, gtok, small[:PROMPT], small[PROMPT], g_q, g_k, g_v, g_wo, gtab,
        small[PROMPT + 1], g_in, g_out,
    )


def solution(mesh):
    both = P(("rows", "heads"), None)
    cols = P(None, "heads")
    rows = P("heads", None)
    in_specs = (
        both, P(), P("rows", None), P(), cols, cols, cols, rows, cols, P(), cols, rows, both,
    )
    out_specs = (both, both, P(), P(), cols, cols, cols, rows, cols, P(), cols, rows)
    return jax.shard_map(
        on_device, mesh=mesh, in_specs=in_specs, out_specs=out_specs, check_vma=False
    )
```

```python
from functools import partial
import math

import jax
import jax.numpy as jnp
from jax import lax
from jax.experimental import pallas as pl
from jax.experimental.pallas import tpu as pltpu
from jax.sharding import PartitionSpec as P

D = 768
DH = 64
NB = 32
ROW = 1024
PROMPT = 100
BIG = 1e30
EDGES = (12, 16, 23, 32, 46, 64, 91)
EPS = 1e-06
ROOT_HALF = 1.0 / math.sqrt(2.0)
DENSITY = 1.0 / math.sqrt(2.0 * math.pi)
F32 = jnp.float32
BF16 = jnp.bfloat16
FFC = 128
CH = 768
UNIT = CH
QB = 256
GROUP = 3
SIZES = (2, 3, 4, 5, 6, 8)
SPACING = 3
SLOTS = 7
BT = 128
NBLK = ROW // BT


def dot_nn(a, b):
    return lax.dot_general(a, b, (((1,), (0,)), ((), ())), preferred_element_type=F32)


def dot_nt(a, b):
    return lax.dot_general(a, b, (((1,), (1,)), ((), ())), preferred_element_type=F32)


def dot_tn(a, b):
    return lax.dot_general(a, b, (((0,), (0,)), ((), ())), preferred_element_type=F32)


def own_row(seg_ref):
    return jnp.where(lax.axis_index("heads") == 0, seg_ref[0:1, :], seg_ref[1:2, :])


def iota(shape, dim):
    return lax.broadcasted_iota(jnp.int32, shape, dim)


def bucket_of(offset):
    distance = jnp.abs(offset)
    far = jnp.full(distance.shape, 8, jnp.int32)
    for edge in EDGES:
        far = far + (distance >= edge).astype(jnp.int32)
    near = jnp.where(distance < 8, distance, far)
    return near + jnp.where(offset > 0, 16, 0)


def picks_t(seg):
    lane = iota((1, ROW), 1)
    first = jnp.zeros((1, ROW), jnp.int32)
    for s in range(1, 4):
        count = jnp.sum((seg < s).astype(F32), axis=1, keepdims=True).astype(jnp.int32)
        first = jnp.where(seg == s, count, first)
    pos = lane - first
    return (iota((128, ROW), 0) == pos).astype(F32).astype(BF16)


def offset_picks(rows):
    return (bucket_of(256 - iota((rows, 512), 1)) == iota((rows, 512), 0)).astype(F32)


def key_marks(seg):
    i = iota((16, ROW), 0)
    block = iota((16, ROW), 1) // BT
    return jnp.where(i < 8, (seg == i).astype(F32), (block == i - 8).astype(F32)).astype(BF16)


def query_marks(seg, left, right):
    i = iota((16, ROW), 0)
    block = iota((16, ROW), 1) // BT
    excluded = jnp.where(jnp.logical_or(seg == i, i >= 4), 0.0, -BIG)
    j = i - 8
    far = jnp.where(j <= block - 2, left, jnp.where(j >= block + 2, right, 0.0))
    return jnp.where(i < 8, excluded, far).astype(BF16)


def attend_block(n, q, lo, base, kn, qaug, vaug, strip, pt_ref, mixed_ref, inv_ref):
    lo = jnp.minimum(lo, NBLK - n)
    rows = pl.ds(pl.multiple_of(lo * BT, BT), n * BT)
    cols = pl.ds(pl.multiple_of(q * QB, QB), QB)
    near = pl.ds(pl.multiple_of((lo - q * (QB // BT) + ROW // BT - QB // BT) * BT, BT), n * BT)

    def mix(j):
        o = dot_nn(vaug[j, :, rows], pt_ref[j, rows, :])
        inv = 1.0 / o[DH : DH + 1]
        out = pl.ds(pl.multiple_of((base + j) * DH, DH), DH)
        mixed_ref[out, cols] = (o[:DH] * inv).astype(BF16)
        inv_ref[pl.ds(base + j, 1), cols] = inv

    scores, peaks = [], []
    for j in range(GROUP):
        s = dot_nn(kn[j, rows, :], qaug[j, :, cols]) + strip[j, near, :]
        scores.append(s)
        peaks.append(jnp.max(s, axis=0, keepdims=True))
    for j in range(GROUP):
        if n < NBLK:
            pt_ref[j] = jnp.zeros((ROW, QB), BF16)
        pt_ref[j, rows, :] = jnp.exp(scores[j] - peaks[j]).astype(BF16)
        if j:
            mix(j - 1)
    mix(GROUP - 1)


def attend_heads(
    step, q, seg, table_f, span, qkv_ref, kaug, qaug, vaug, kn, strip, pt_ref, mixed_ref, inv_ref
):
    base = step * GROUP
    per = QB // BT
    zero = (ROW // BT - per) * BT
    @pl.when(q == 0)
    def _():
        for j in range(GROUP):
            rows = pl.ds(pl.multiple_of((base + j) * DH, DH), DH)
            values = table_f[pl.ds(base + j, 1), :]
            near = pltpu.roll(jnp.broadcast_to(values, (BT, 512)), 0, 1, stride=1, stride_axis=0)
            for d in range(-1, per + 1):
                for u in range(per):
                    if abs(d - u) <= 1:
                        at = 256 - 128 * (d - u)
                        strip[j, zero + d * BT : zero + (d + 1) * BT, u * BT : (u + 1) * BT] = near[
                            :, at : at + 128
                        ]
            qaug[j, 0:DH, :] = qkv_ref[0, rows, :]
            kaug[0:DH, :] = qkv_ref[1, rows, :]
            vaug[j, 0:DH, :] = qkv_ref[2, rows, :]
            qaug[j, DH : DH + 16, :] = query_marks(seg, values[:, 511:512], values[:, 1:2])
            kn[j] = kaug[...].T

    lo, n = span[0, q], span[1, q]
    last = 0
    for size in SIZES:

        @pl.when(jnp.logical_and(n > last, n <= size))
        def _():
            attend_block(size, q, lo, base, kn, qaug, vaug, strip, pt_ref, mixed_ref, inv_ref)

        last = size


def project_t(w_refs, yt, qkv_ref):
    for m in range(3):
        qkv_ref[m] = dot_tn(w_refs[m][...], yt).astype(BF16)


def head_setup(seg, tab_ref, table_f, span, kaug, qaug, vaug, strip):
    picks = offset_picks(NB).astype(BF16)
    wide_tab = jnp.concatenate([tab_ref[...], jnp.zeros((NB, 128 - tab_ref.shape[1]), BF16)], axis=1)
    table_f[...] = dot_tn(wide_tab, picks)[0:8]
    kaug[DH:, :] = jnp.zeros((128 - DH, ROW), BF16)
    qaug[:, DH:, :] = jnp.zeros((GROUP, 128 - DH, ROW), BF16)
    kaug[DH : DH + 16, :] = key_marks(seg)
    vaug[:, DH:, :] = jnp.ones((GROUP, 16, ROW), BF16)
    strip[...] = jnp.zeros(strip.shape, F32)
    for q in range(ROW // QB):
        lowest = jnp.min(seg[:, q * QB : (q + 1) * QB].astype(F32))
        highest = jnp.max(seg[:, q * QB : (q + 1) * QB].astype(F32))
        wide = seg.astype(F32)
        begin = jnp.sum((wide < lowest).astype(F32)).astype(jnp.int32) // BT
        end = (jnp.sum((wide <= highest).astype(F32)).astype(jnp.int32) + BT - 1) // BT
        span[0, q] = begin
        span[1, q] = end - begin


def forward_first(
    seg_ref, tok_ref, prompt_ref, gain_ref, wq, wk, wv, tab_ref,
    start_ref, yt_ref, qkv_ref, pt_ref, mixed_ref, inv_ref,
    table_f, span, kaug, qaug, vaug, kn, strip, padded,
):
    step, q = pl.program_id(0), pl.program_id(1)
    first = jnp.logical_and(step == 0, q == 0)
    seg = own_row(seg_ref)

    @pl.when(first)
    def _():
        padded[...] = jnp.zeros(padded.shape, BF16)
        padded[0:PROMPT, :] = prompt_ref[...]
        picks = picks_t(seg)
        looked = dot_tn(picks, padded[...])
        here = dot_tn(picks, (iota((128, 128), 0) < PROMPT).astype(F32).astype(BF16)) > 0.5
        tok = tok_ref[...].astype(F32)
        start = jnp.concatenate(
            [
                jnp.where(here, looked[:, c : c + 128], tok[:, c : c + 128])
                for c in range(0, D, 128)
            ],
            axis=1,
        )
        start_ref[...] = start.astype(BF16)
        inv = lax.rsqrt(jnp.mean(start * start, axis=1, keepdims=True) + EPS)
        yt = (start * inv * gain_ref[...][None, :]).astype(BF16).T
        yt_ref[...] = yt
        project_t((wq, wk, wv), yt, qkv_ref)
        head_setup(seg, tab_ref, table_f, span, kaug, qaug, vaug, strip)

    attend_heads(
        step, q, seg, table_f, span, qkv_ref, kaug, qaug, vaug, kn, strip, pt_ref, mixed_ref, inv_ref
    )


def forward_second(
    seg_ref, start_ref, yt_ref, gain_ref, wq, wk, wv, tab_ref, mixed_own, wo_own, wo_oth,
    qkv_ref, pt_ref, mixed_ref, inv_ref, middle_ref, x_ref, xt_ref,
    table_f, span, kaug, qaug, vaug, kn, strip,
):
    step, q = pl.program_id(0), pl.program_id(1)
    first = jnp.logical_and(step == 0, q == 0)
    seg = own_row(seg_ref)

    @pl.when(first)
    def _():
        project_t((wq, wk, wv), yt_ref[...], qkv_ref)
        head_setup(seg, tab_ref, table_f, span, kaug, qaug, vaug, strip)

    attend_heads(
        step, q, seg, table_f, span, qkv_ref, kaug, qaug, vaug, kn, strip, pt_ref, mixed_ref, inv_ref
    )

    @pl.when(jnp.logical_and(step == pl.num_programs(0) - 1, q == pl.num_programs(1) - 1))
    def _():
        attn = dot_tn(mixed_own[...], wo_own[...]) + dot_tn(mixed_ref[...], wo_oth[...])
        middle = start_ref[...].astype(F32) + attn
        middle_ref[...] = middle
        inv = lax.rsqrt(jnp.mean(middle * middle, axis=1, keepdims=True) + EPS)
        x = (middle * inv * gain_ref[...][None, :]).astype(BF16)
        x_ref[...] = x
        xt_ref[...] = x.T


def plan_stages(n_rows):
    n_bits = n_rows.bit_length() - 1
    size, slot = UNIT, 0
    stages, halved = [], []
    for j in range(n_bits):
        if j < n_bits - 1 and size % 32 == 0:
            size = size // 2
            halved.append((j, size))
            stages.append(("halve", j, size, slot))
        else:
            stages.append(("swap", j, size, slot))
        slot += size
    for j, n in reversed(halved):
        stages.append(("gather", j, n, slot))
        slot += n
    return stages, len(halved), slot


def stage_order(n_rows, odd):
    n_bits = n_rows.bit_length() - 1
    me = lax.axis_index("rows")
    bits = [(me // (1 << b)) % 2 for b in range(n_bits)]
    peers = [me + (1 - 2 * bits[b]) * (1 << b) for b in range(n_bits)]
    even = [0, 2, 1] + list(range(3, n_bits))
    flip = [1, 2, 0] + list(range(3, n_bits))
    pick = [(bits[a] + odd * (bits[b] - bits[a])) for a, b in zip(even, flip)]
    peer = [(peers[a] + odd * (peers[b] - peers[a])) for a, b in zip(even, flip)]
    return pick, peer, peers


def whole(shape):
    n = len(shape)
    return pl.BlockSpec(shape, lambda *_: (0,) * n, pipeline_mode=pl.Buffered(1))


def whole_out(shape):
    n = len(shape)
    return pl.BlockSpec(shape, lambda *_: (0,) * n)


def sds(shape, dtype):
    return jax.ShapeDtypeStruct(shape, dtype)


def forward_scratch():
    return [
        pltpu.VMEM((8, 512), F32),
        pltpu.SMEM((2, ROW // QB), jnp.int32),
        pltpu.VMEM((128, ROW), BF16),
        pltpu.VMEM((GROUP, 128, ROW), BF16),
        pltpu.VMEM((GROUP, DH + 16, ROW), BF16),
        pltpu.VMEM((GROUP, ROW, 128), BF16),
        pltpu.VMEM((GROUP, 2 * ROW, QB), F32),
    ]


PARAMS = dict(vmem_limit_bytes=56 * 1024 * 1024)


def run_first(seg, tok, prompt, gain, wq, wk, wv, tab):
    cols = wq.shape[1]
    heads = cols // DH
    return pl.pallas_call(
        forward_first,
        grid=(heads // GROUP, ROW // QB),
        in_specs=[whole(a.shape) for a in (seg, tok, prompt, gain, wq, wk, wv, tab)],
        out_specs=[
            whole_out((ROW, D)),
            whole_out((D, ROW)),
            whole_out((3, cols, ROW)),
            pl.BlockSpec((GROUP, ROW, QB), lambda h, q: (h, 0, q)),
            whole_out((cols, ROW)),
            whole_out((8, ROW)),
        ],
        out_shape=[
            sds((ROW, D), BF16),
            sds((D, ROW), BF16),
            sds((3, cols, ROW), BF16),
            sds((heads, ROW, ROW), BF16),
            sds((cols, ROW), BF16),
            sds((8, ROW), F32),
        ],
        scratch_shapes=forward_scratch() + [pltpu.VMEM((128, D), BF16)],
        compiler_params=pltpu.CompilerParams(**PARAMS),
        cost_estimate=pl.CostEstimate(flops=2 * 10**10, bytes_accessed=10**7, transcendentals=0),
        name="attend_own",
    )(seg, tok, prompt, gain, wq, wk, wv, tab)


def run_second(seg, start, yt, gain, wq, wk, wv, tab, mixed_own, wo_own, wo_oth):
    cols = wq.shape[1]
    heads = cols // DH
    ins = (seg, start, yt, gain, wq, wk, wv, tab, mixed_own, wo_own, wo_oth)
    return pl.pallas_call(
        forward_second,
        grid=(heads // GROUP, ROW // QB),
        in_specs=[whole(a.shape) for a in ins],
        out_specs=[
            whole_out((3, cols, ROW)),
            pl.BlockSpec((GROUP, ROW, QB), lambda h, q: (h, 0, q)),
            whole_out((cols, ROW)),
            whole_out((8, ROW)),
            whole_out((ROW, D)),
            whole_out((ROW, D)),
            whole_out((D, ROW)),
        ],
        out_shape=[
            sds((3, cols, ROW), BF16),
            sds((heads, ROW, ROW), BF16),
            sds((cols, ROW), BF16),
            sds((8, ROW), F32),
            sds((ROW, D), F32),
            sds((ROW, D), BF16),
            sds((D, ROW), BF16),
        ],
        scratch_shapes=forward_scratch(),
        compiler_params=pltpu.CompilerParams(**PARAMS),
        cost_estimate=pl.CostEstimate(flops=2 * 10**10, bytes_accessed=10**7, transcendentals=0),
        name="attend_other",
    )(*ins)


def norm_back(value, gain, grad):
    inv = lax.rsqrt(jnp.mean(value * value, axis=1, keepdims=True) + EPS)
    scaled = grad * gain
    inner = jnp.mean(scaled * value, axis=1, keepdims=True)
    back = inv * scaled - value * (inv * inv * inv * inner)
    return back, jnp.sum(grad * (value * inv), axis=0, keepdims=True)


def backward(
    n_ff, n_heads, n_rows,
    seg_ref, gain_a_ref, gain_f_ref, win_own, win_oth, wout_own, wout_oth, pt_own, pt_oth,
    x_hbm, xt_hbm, og_hbm, mid_hbm, start_hbm, yt_hbm, qkv_own_hbm, qkv_oth_hbm,
    mix_own_hbm, mix_oth_hbm, inv_own_hbm, inv_oth_hbm, wq_own_hbm, wk_own_hbm, wv_own_hbm, wq_oth_hbm, wk_oth_hbm,
    wv_oth_hbm, wo_own_hbm, wo_oth_hbm,
    result_ref, gtok_ref, out_in, out_out, out_q, out_k, out_v, out_o, out_small,
    x, xt, og, mid, qkv, mix, inv, gmix, wqkv, wo, feed, gnf, dst, dqkv, kaug, vaug, doaug,
    tacc, gvec, gains, ptb, g, xsend, xrecv, ring, load_sem, late_sem, pt_sem, out_sem, xs_sem, xr_sem,
    send_sem, recv_sem,
):
    s = pl.program_id(0)
    heads_half = n_heads // 2
    cols = heads_half * DH
    me = lax.axis_index("heads")
    early = [(x_hbm, x), (xt_hbm, xt), (og_hbm, og)]
    later = [
        (mid_hbm, mid),
        (qkv_own_hbm, qkv.at[0]),
        (qkv_oth_hbm, qkv.at[1]),
        (mix_own_hbm, mix.at[0]),
        (mix_oth_hbm, mix.at[1]),
        (inv_own_hbm, inv.at[0]),
        (inv_oth_hbm, inv.at[1]),
        (wq_own_hbm, wqkv.at[0, 0]),
        (wk_own_hbm, wqkv.at[0, 1]),
        (wv_own_hbm, wqkv.at[0, 2]),
        (wq_oth_hbm, wqkv.at[1, 0]),
        (wk_oth_hbm, wqkv.at[1, 1]),
        (wv_oth_hbm, wqkv.at[1, 2]),
        (wo_own_hbm, wo.at[0]),
        (wo_oth_hbm, wo.at[1]),
    ]
    n_early = len(early)
    loads = [
        pltpu.make_async_copy(a, b, load_sem.at[i]) for i, (a, b) in enumerate(early + later)
    ]
    late = [
        pltpu.make_async_copy(start_hbm, x, late_sem.at[0]),
        pltpu.make_async_copy(yt_hbm, xt, late_sem.at[1]),
    ]

    def pt_start(i):
        hh = 2 * (i // 4) + i % 2
        for o, ref in enumerate((pt_own, pt_oth)):

            @pl.when((i % 4) // 2 == o)
            def _():
                pltpu.make_async_copy(ref.at[hh], ptb.at[i % 2], pt_sem.at[i % 2]).start()

    n_out = cols // 128
    n_chunks = 2 * n_ff + 4 * n_out + 1
    n_units = n_chunks
    stages, n_halved, _ = plan_stages(n_rows)
    n_stages = len(stages)
    peers = stage_order(n_rows, 0)[2]
    core = {"heads": 1 - me}

    def swap(slot):
        return pltpu.make_async_remote_copy(
            src_ref=xsend.at[slot],
            dst_ref=xrecv.at[slot],
            send_sem=xs_sem.at[slot],
            recv_sem=xr_sem.at[slot],
            device_id=core,
            device_id_type=pl.DeviceIdType.MESH,
        )

    def emit(c, slot, own, oth):
        for blocks, ref in ((own, g.at[c]), (oth, xsend.at[slot])):
            for b, block in enumerate(blocks):
                n = block.shape[0]
                ref[b * n : (b + 1) * n, :] = block.astype(BF16)
        swap(slot).start()

    def collect(c, slot):
        swap(slot).wait()
        g[c] = (g[c].astype(F32) + xrecv[slot].astype(F32)).astype(BF16)

    def stage_copy(k, c):
        kind, j, n, slot = stages[k]
        pick, peer, _ = stage_order(n_rows, c % 2)
        base, size = 0, UNIT
        for i in range(min(j, n_halved)):
            size = size // 2
            base = base + pick[i] * size
        keep = base + pick[j] * n
        give = base + (1 - pick[j]) * n
        src, dst = {"halve": (give, keep), "swap": (base, base), "gather": (keep, give)}[kind]
        src, dst = (pl.ds(pl.multiple_of(r, 16), n) for r in (src, dst))
        par = c % SLOTS
        copy = pltpu.make_async_remote_copy(
            src_ref=g.at[c, src, :],
            dst_ref=ring.at[par, slot : slot + n, :],
            send_sem=send_sem.at[k, par],
            recv_sem=recv_sem.at[k, par],
            device_id={"rows": peer[j]},
            device_id_type=pl.DeviceIdType.MESH,
        )
        return copy, dst

    def stage_end(k, c):
        kind, _, n, slot = stages[k]
        copy, dst = stage_copy(k, c)
        copy.wait()
        part = ring[c % SLOTS, slot : slot + n, :]
        if kind != "gather":
            part = (g[c, dst, :].astype(F32) + part.astype(F32)).astype(BF16)
        g[c, dst, :] = part

    def out_wait(par):
        pltpu.make_async_copy(g.at[0], out_in.at[:, 0:128], out_sem.at[par]).wait()

    def out_start(c):
        sem = out_sem.at[c % 2]

        @pl.when(c >= 2)
        def _():
            out_wait(c % 2)

        def wide(ref, col):
            dst = ref.at[:, pl.ds(pl.multiple_of(col * 128, 128), 128)]
            pltpu.make_async_copy(g.at[c], dst, sem).start()

        def tall(ref, row):
            for b in range(D // 128):
                dst = ref.at[
                    pl.ds(pl.multiple_of(row * 128, 128), 128), b * 128 : (b + 1) * 128
                ]
                pltpu.make_async_copy(g.at[c, b * 128 : (b + 1) * 128], dst, sem).start()

        base = 2 * n_ff + n_out

        @pl.when(jnp.logical_and(c < 2 * n_ff, c % 2 == 0))
        def _():
            wide(out_in, c // 2)

        @pl.when(jnp.logical_and(c < 2 * n_ff, c % 2 == 1))
        def _():
            tall(out_out, c // 2)

        @pl.when(jnp.logical_and(c >= 2 * n_ff, c < base))
        def _():
            tall(out_o, c - 2 * n_ff)

        for m, ref in enumerate((out_q, out_k, out_v)):
            at = jnp.logical_and(c >= base, c < n_chunks - 1)

            @pl.when(jnp.logical_and(at, (c - base) % 3 == m))
            def _():
                wide(ref, (c - base) // 3)

        @pl.when(c == n_chunks - 1)
        def _():
            tall(out_small, 0)

    wo_end = 2 * n_ff + n_out
    holes = ((wo_end, 2), (wo_end + 5, 1))

    def tick(t):
        for k in range(n_stages, -1, -1):
            v = t - SPACING * k
            c = v
            valid = v >= 0
            for at, length in holes:
                c = c - jnp.where(v >= at + length, length, 0)
                valid = jnp.logical_and(valid, jnp.logical_or(v < at, v >= at + length))
            valid = jnp.logical_and(valid, c < n_units)

            @pl.when(valid)
            def _():
                if k > 0:
                    stage_end(k - 1, c)
                if k < n_stages:
                    stage_copy(k, c)[0].start()
                if k == n_stages:
                    out_start(c)

    def collect_ff(e):
        for j in range(2):
            collect(2 * e + j, 2 * (e % 4) + j)

    def group_slot(e, m):
        return 3 + m if e % 2 == 0 else m

    def collect_group(e):
        for m in range(3):
            collect((2 * n_ff + n_out + 3 * e + m), group_slot(e, m))

    def lanes(a):
        return [a[:, k : k + 128] for k in range(0, a.shape[1], 128)]

    @pl.when(s == 0)
    def _():
        for copy in loads:
            copy.start()
        barrier = pltpu.get_barrier_semaphore()
        for peer in [{"rows": p} for p in peers] + [core]:
            pl.semaphore_signal(
                barrier, inc=1, device_id=peer, device_id_type=pl.DeviceIdType.MESH
            )
        pl.semaphore_wait(barrier, len(peers) + 1)
        for copy in loads[:n_early]:
            copy.wait()
        feed[...] = jnp.zeros(feed.shape, F32)
        gnf[...] = jnp.zeros(gnf.shape, F32)

    @pl.when(s < n_ff)
    def _():
        wi = jnp.concatenate([win_own[...], win_oth[...]], axis=1)
        wout = jnp.concatenate([wout_own[...], wout_oth[...]], axis=0)
        halves = [slice(0, ROW // 2), slice(ROW // 2, ROW)]
        pres = [dot_nn(x[r, :], wi) for r in halves]
        gacts = [dot_nt(og[r, :], wout) for r in halves]
        acts, gpres = [], []
        for pre, gact in zip(pres, gacts):
            cdf = 0.5 * (1.0 + lax.erf(pre * ROOT_HALF))
            acts.append((pre * cdf).astype(BF16))
            slope = cdf + pre * jnp.exp(-0.5 * pre * pre) * DENSITY
            gpres.append((gact * slope).astype(BF16))
        for r, act, gpre in zip(halves, acts, gpres):
            feed[r, :] += dot_nn(act, wout)
            gnf[r, :] += dot_nt(gpre, wi)
        active = jnp.concatenate(acts, axis=0)
        gpre = jnp.concatenate(gpres, axis=0)

        @pl.when(s >= 2)
        def _():
            collect_ff(s - 2)
            tick(2 * (s - 2))

        dwin = dot_nn(xt[...], gpre)
        dwout = dot_tn(active, og[...])

        emit(2 * s, 2 * (s % 4), [dwin[:, :FFC]], [dwin[:, FFC:]])
        emit(2 * s + 1, 2 * (s % 4) + 1, lanes(dwout[:FFC]), lanes(dwout[FFC:]))

        @pl.when(s >= 2)
        def _():
            tick(2 * (s - 2) + 1)

    @pl.when(s == n_ff)
    def _():
        for copy in late:
            copy.start()
        pt_start(0)
        for copy in loads[n_early:]:
            copy.wait()
        collect_ff(n_ff - 2)
        t0 = 2 * (n_ff - 2)
        tick(t0)
        middle = mid[...]
        result_ref[...] = (middle + feed[...]).astype(BF16)
        back, gain_grad = norm_back(middle, gain_f_ref[...][None, :], gnf[...])
        gmid = og[...].astype(F32) + back
        gains[0:1, :] = gain_grad
        mid[...] = gmid
        tick(t0 + 1)
        ga = gmid.astype(BF16)
        dwo = [dot_nn(mix[o], ga) for o in range(2)]
        collect_ff(n_ff - 1)
        for j in range(n_out):
            rows = slice(j * 128, (j + 1) * 128)
            emit((2 * n_ff + j), j, lanes(dwo[0][rows]), lanes(dwo[1][rows]))
        for o in range(2):
            grad = dot_nt(wo[o], ga)
            for k in range(heads_half):
                rows = slice(k * DH, (k + 1) * DH)
                gmix[o, rows, :] = (grad[rows] * inv[o, k : k + 1, :]).astype(BF16)
        tick(t0 + 2)
        gnf[...] = jnp.zeros(gnf.shape, F32)
        kaug[DH:, :] = key_marks(own_row(seg_ref))
        vaug[DH:, :] = (iota((16, ROW), 0) < 3).astype(F32).astype(BF16)
        gvec[...] = jnp.zeros(gvec.shape, F32)
        for copy in late:
            copy.wait()
        tick(t0 + 3)

    i = s - (n_ff + 1)

    def head_back(o, pt_ref):
        hh = 2 * (i // 4) + i % 2
        rows = pl.ds(pl.multiple_of(hh * DH, DH), DH)
        dot_ = gmix[o, rows, :]
        delta = jnp.sum(dot_.astype(F32) * mix[o, rows, :].astype(F32), axis=0, keepdims=True)
        d1 = delta.astype(BF16).astype(F32)
        d2 = (delta - d1).astype(BF16).astype(F32)
        d3 = delta - d1 - d2
        k = iota((16, ROW), 0)
        vaug[0:DH, :] = qkv[o, 2, rows, :]
        kaug[0:DH, :] = qkv[o, 1, rows, :]
        doaug[0:DH, :] = dot_
        doaug[DH:, :] = jnp.where(
            k == 0, -d1, jnp.where(k == 1, -d2, jnp.where(k == 2, -d3, 0.0))
        ).astype(BF16)
        va = vaug[...]
        ka = kaug[...]
        out_rows = pl.ds(pl.multiple_of(o * 128 + (i % 2) * DH, DH), DH)
        tacc[...] = jnp.zeros(tacc.shape, F32)
        left = jnp.zeros((1, QB), F32)
        right = jnp.zeros((1, QB), F32)
        n_blocks = ROW // QB

        def grad_probs(b):
            return dot_tn(va, doaug[:, b * QB : (b + 1) * QB])

        dp = grad_probs(0)
        dqkv[2, out_rows, :] = dot_nt(dot_, pt_ref[...]).astype(BF16)
        for b in range(n_blocks):
            qs = slice(b * QB, (b + 1) * QB)
            ahead = grad_probs(b + 1) if b + 1 < n_blocks else None
            ds = pt_ref[:, qs].astype(F32) * dp
            for u in range(QB // BT):
                qb = b * (QB // BT) + u
                for d in (-1, 0, 1):
                    kb = qb + d
                    if 0 <= kb < NBLK:
                        tacc[:, 256 - 128 * d : 384 - 128 * d] += ds[
                            kb * BT : (kb + 1) * BT, u * BT : (u + 1) * BT
                        ]
            dst[:, qs] = ds.astype(BF16)
            dp = ahead
        for b in range(n_blocks):
            qs = slice(b * QB, (b + 1) * QB)
            r = dot_nn(ka, dst[:, qs])
            dqkv[0, out_rows, qs] = r[:DH].astype(BF16)
            sums = r[DH + 8 :]
            j = iota((8, QB), 0)
            block = b * (QB // BT) + iota((8, QB), 1) // BT
            left = left + jnp.sum(jnp.where(j <= block - 2, sums, 0.0), axis=0, keepdims=True)
            right = right + jnp.sum(jnp.where(j >= block + 2, sums, 0.0), axis=0, keepdims=True)
        dqkv[1, out_rows, :] = dot_nt(qkv[o, 0, rows, :], dst[...]).astype(BF16)
        flip = (iota((BT, BT), 0) + iota((BT, BT), 1) == BT - 1).astype(F32).astype(BF16)
        near = tacc[...]
        high = near.astype(BF16)
        low = (near - high.astype(F32)).astype(BF16)
        turned = dot_nn(flip, high) + dot_nn(flip, low)
        skew = pltpu.roll(turned, 0, 1, stride=1, stride_axis=0)
        vec = pltpu.roll(jnp.sum(skew, axis=0, keepdims=True), 512 - (BT - 1), 1)
        lane = iota((1, 512), 1)
        vec = vec + jnp.where(lane == 511, jnp.sum(left, axis=1, keepdims=True), 0.0)
        vec = vec + jnp.where(lane == 1, jnp.sum(right, axis=1, keepdims=True), 0.0)
        owner = me + o * (1 - 2 * me)
        gvec[pl.ds(owner * heads_half + hh, 1), :] = vec

    in_heads = jnp.logical_and(i >= 0, i < n_heads)

    @pl.when(in_heads)
    def _():
        @pl.when(i + 1 < n_heads)
        def _():
            pt_start(i + 1)

        pltpu.make_async_copy(pt_own.at[0], ptb.at[i % 2], pt_sem.at[i % 2]).wait()
        head_back((i % 4) // 2, ptb.at[i % 2])

        @pl.when(i == 0)
        def _():
            for j in range(n_out):
                collect((2 * n_ff + j), j)

        for e in range(n_heads // 4 - 1):

            @pl.when(i == 4 * (e + 1) + 1)
            def _():
                collect_group(e)

        tick(2 * n_ff + i)

    def group_back(grp):
        for m in range(3):
            grad = dqkv[m]
            dw = dot_nt(xt[...], grad)
            emit(
                (2 * n_ff + n_out + 3 * grp + m), group_slot(grp, m),
                [dw[:, :128]], [dw[:, 128:]],
            )
            cols_g = slice(grp * 128, (grp + 1) * 128)
            w = jnp.concatenate([wqkv[0, m, :, cols_g], wqkv[1, m, :, cols_g]], axis=1)
            part = lax.dot_general(grad, w, (((0,), (1,)), ((), ())), preferred_element_type=F32)
            gnf[...] += part

    for grp in range(n_heads // 4):

        @pl.when(i == 4 * grp + 3)
        def _():
            group_back(grp)

    @pl.when(i == n_heads)
    def _():
        seg = own_row(seg_ref)
        start = x[...].astype(F32)
        back, gain_grad = norm_back(start, gain_a_ref[...][None, :], gnf[...])
        gstart = mid[...] + back
        n_groups = n_heads // 4
        collect_group(n_groups - 1)
        t0 = 2 * n_ff + n_heads
        tick(t0)
        picks = picks_t(seg)
        here = dot_tn(picks, (iota((128, 128), 0) < PROMPT).astype(F32).astype(BF16)) > 0.5
        for c in range(0, D, 128):
            gtok_ref[:, c : c + 128] = jnp.where(here, 0.0, gstart[:, c : c + 128]).astype(BF16)
        high = gstart.astype(BF16)
        low = (gstart - high.astype(F32)).astype(BF16)
        tick(t0 + 1)
        gprompt = dot_nn(picks, high) + dot_nn(picks, low)
        opicks = offset_picks(128).astype(BF16)
        gv = gvec[...]
        g1 = gv.astype(BF16)
        g2 = (gv - g1.astype(F32)).astype(BF16)
        gtab = dot_nt(g1, opicks) + dot_nt(g2, opicks)
        row = iota((128, D), 0)
        small = jnp.where(row < PROMPT, gprompt, 0.0)
        small = jnp.where(row == PROMPT, gain_grad, small)
        small = jnp.where(row == PROMPT + 1, gains[0:1, :], small)
        blocks = lanes(small)
        wide = jnp.concatenate([jnp.zeros((104, 128), F32), gtab, jnp.zeros((8, 128), F32)], axis=0)
        blocks[0] = blocks[0] + wide
        slot = group_slot(n_groups, 0)
        emit((n_chunks - 1), slot, blocks, blocks)
        tick(t0 + 2)
        collect((n_chunks - 1), slot)

        @pl.loop(t0 + 3, n_units + sum(h[1] for h in holes) + SPACING * n_stages)
        def _(t):
            tick(t)

        out_wait(0)
        out_wait(1)


def run_backward(
    n_rows, seg, gain_a, gain_f, win_own, win_oth, wout_own, wout_oth, pt_own, pt_oth, rest
):
    n_ff = win_own.shape[1] // FFC
    n_heads = 2 * pt_own.shape[0]
    cols = n_heads * DH // 2
    n_chunks = 2 * n_ff + 4 * (cols // 128) + 1
    first = n_ff + 1
    stages, _, ring_rows = plan_stages(n_rows)
    n_stages = len(stages)

    def ff(s):
        return jnp.minimum(s, n_ff - 1)

    blk_in = pl.BlockSpec((D, FFC), lambda s: (0, ff(s)))
    blk_out = pl.BlockSpec((FFC, D), lambda s: (ff(s), 0))
    anyspec = pl.BlockSpec(memory_space=pl.ANY)
    return pl.pallas_call(
        partial(backward, n_ff, n_heads, n_rows),
        grid=(first + n_heads + 1,),
        in_specs=[
            whole(seg.shape), whole(gain_a.shape), whole(gain_f.shape),
            blk_in, blk_in, blk_out, blk_out,
        ] + [anyspec] * (2 + len(rest)),
        out_specs=[whole((ROW, D)), whole((ROW, D))] + [anyspec] * 7,
        out_shape=[sds((ROW, D), BF16), sds((ROW, D), BF16)] + [
            sds(shape, BF16)
            for shape in (win_own.shape, wout_own.shape)
            + ((D, cols),) * 3 + ((cols, D), (128, D))
        ],
        scratch_shapes=[
            pltpu.VMEM((ROW, D), BF16),
            pltpu.VMEM((D, ROW), BF16),
            pltpu.VMEM((ROW, D), BF16),
            pltpu.VMEM((ROW, D), F32),
            pltpu.VMEM((2, 3, cols, ROW), BF16),
            pltpu.VMEM((2, cols, ROW), BF16),
            pltpu.VMEM((2, 8, ROW), F32),
            pltpu.VMEM((2, cols, ROW), BF16),
            pltpu.VMEM((2, 3, D, cols), BF16),
            pltpu.VMEM((2, cols, D), BF16),
            pltpu.VMEM((ROW, D), F32),
            pltpu.VMEM((ROW, D), F32),
            pltpu.VMEM((ROW, ROW), BF16),
            pltpu.VMEM((3, 256, ROW), BF16),
            pltpu.VMEM((DH + 16, ROW), BF16),
            pltpu.VMEM((DH + 16, ROW), BF16),
            pltpu.VMEM((DH + 16, ROW), BF16),
            pltpu.VMEM((BT, 512), F32),
            pltpu.VMEM((16, 512), F32),
            pltpu.VMEM((8, D), F32),
            pltpu.VMEM((2, ROW, ROW), BF16),
            pltpu.VMEM((n_chunks, UNIT, 128), BF16),
            pltpu.VMEM((8, CH, 128), BF16),
            pltpu.VMEM((8, CH, 128), BF16),
            pltpu.VMEM((SLOTS, ring_rows, 128), BF16),
            pltpu.SemaphoreType.DMA((18,)),
            pltpu.SemaphoreType.DMA((2,)),
            pltpu.SemaphoreType.DMA((2,)),
            pltpu.SemaphoreType.DMA((2,)),
            pltpu.SemaphoreType.DMA((8,)),
            pltpu.SemaphoreType.DMA((8,)),
            pltpu.SemaphoreType.DMA((n_stages, SLOTS)),
            pltpu.SemaphoreType.DMA((n_stages, SLOTS)),
        ],
        compiler_params=pltpu.CompilerParams(
            vmem_limit_bytes=62 * 1024 * 1024, collective_id=0, has_side_effects=True
        ),
        name="backward",
    )(seg, gain_a, gain_f, win_own, win_oth, wout_own, wout_oth, pt_own, pt_oth, *rest)


def finish(
    heads, result, gtok, small, g_q, g_k, g_v, g_wo, g_in, g_out,
    o_result, o_gtok, o_prompt, o_gain_a, o_q, o_k, o_v, o_wo, o_tab, o_gain_f, o_in, o_out, rows,
):
    o_result[...] = result[...]
    o_gtok[...] = gtok[...]
    for src, dst in ((g_q, o_q), (g_k, o_k), (g_v, o_v), (g_wo, o_wo), (g_in, o_in), (g_out, o_out)):
        dst[...] = src[...].astype(F32)

    @pl.when(pl.program_id(0) == 0)
    def _():
        rows[...] = small[...].astype(F32)
        o_prompt[...] = rows[0:PROMPT, :]
        o_gain_a[...] = rows[PROMPT, :]
        o_gain_f[...] = rows[PROMPT + 1, :]
        low = lax.axis_index("heads") == 0
        at = 104
        tab = [
            jnp.where(low, rows[at + k : at + k + 1, 0:128], rows[at + heads + k : at + heads + k + 1, 0:128])
            for k in range(heads)
        ]
        tab.append(jnp.zeros((8 - heads, 128), F32))
        o_tab[...] = jnp.concatenate(tab, axis=0).T[0:NB, 0:heads]


def run_finish(heads, result, gtok, small, *grads):
    steps = 8

    def part(a):
        return pl.BlockSpec((a.shape[0] // steps, a.shape[1]), lambda i: (i, 0))

    g_q, g_k, g_v, g_wo, g_in, g_out = grads
    whole_1d = pl.BlockSpec((D,), lambda i: (0,))
    return pl.pallas_call(
        partial(finish, heads),
        grid=(steps,),
        in_specs=[part(result), part(gtok), whole(small.shape)] + [part(a) for a in grads],
        out_specs=[part(result), part(gtok), whole_out((PROMPT, D)), whole_1d]
        + [part(a) for a in (g_q, g_k, g_v, g_wo)]
        + [whole_out((NB, heads)), whole_1d, part(g_in), part(g_out)],
        out_shape=[sds(result.shape, BF16), sds(gtok.shape, BF16), sds((PROMPT, D), F32), sds((D,), F32)]
        + [sds(a.shape, F32) for a in (g_q, g_k, g_v, g_wo)]
        + [sds((NB, heads), F32), sds((D,), F32), sds(g_in.shape, F32), sds(g_out.shape, F32)],
        scratch_shapes=[pltpu.VMEM((128, D), F32)],
        compiler_params=pltpu.CompilerParams(vmem_limit_bytes=62 * 1024 * 1024),
        name="finish",
    )(result, gtok, small, *grads)


def on_device(
    tokens, prompt, segment_ids, gain_attn, w_query, w_key, w_value, w_attn_out, bias_table,
    gain_ff, w_in, w_out, out_grad,
):
    seg = segment_ids
    swap = [(0, 1), (1, 0)]

    def other(a):
        return lax.ppermute(a, "heads", swap)

    tab_oth, wq_oth, wk_oth, wv_oth = (other(a) for a in (bias_table, w_query, w_key, w_value))
    wo_oth, win_oth, wout_oth = other(w_attn_out), other(w_in), other(w_out)
    gain_a, gain_f = gain_attn, gain_ff
    start, yt, qkv_own, pt_own, mix_own, inv_own = run_first(
        seg, tokens, prompt, gain_a, w_query, w_key, w_value, bias_table
    )
    qkv_oth, pt_oth, mix_oth, inv_oth, middle, x, xt = run_second(
        seg, start, yt, gain_f, wq_oth, wk_oth, wv_oth, tab_oth, mix_own, w_attn_out, wo_oth
    )
    result, gtok, g_in, g_out, g_q, g_k, g_v, g_wo, small = run_backward(
        lax.axis_size("rows"),
        seg, gain_a, gain_f, w_in, win_oth, w_out, wout_oth, pt_own, pt_oth,
        [x, xt, out_grad, middle, start, yt, qkv_own, qkv_oth, mix_own, mix_oth,
         inv_own, inv_oth,
         w_query, w_key, w_value, wq_oth, wk_oth, wv_oth, w_attn_out, wo_oth],
    )
    (
        result, gtok, g_prompt, g_gain_a, g_q, g_k, g_v, g_wo, g_tab, g_gain_f, g_in, g_out,
    ) = run_finish(bias_table.shape[1], result, gtok, small, g_q, g_k, g_v, g_wo, g_in, g_out)
    return (
        result, gtok, g_prompt, g_gain_a, g_q, g_k, g_v, g_wo, g_tab, g_gain_f, g_in, g_out,
    )


def solution(mesh):
    both = P(("rows", "heads"), None)
    cols = P(None, "heads")
    rows = P("heads", None)
    in_specs = (
        both, P(), P("rows", None), P(), cols, cols, cols, rows, cols, P(), cols, rows, both,
    )
    out_specs = (both, both, P(), P(), cols, cols, cols, rows, cols, P(), cols, rows)
    return jax.shard_map(
        on_device, mesh=mesh, in_specs=in_specs, out_specs=out_specs, check_vma=False
    )
```

```python
from functools import partial
import math

import jax
import jax.numpy as jnp
from jax import lax
from jax.experimental import pallas as pl
from jax.experimental.pallas import tpu as pltpu
from jax.sharding import PartitionSpec as P

D = 768
DH = 64
NB = 32
ROW = 1024
PROMPT = 100
BIG = 1e30
EDGES = (12, 16, 23, 32, 46, 64, 91)
EPS = 1e-06
ROOT_HALF = 1.0 / math.sqrt(2.0)
DENSITY = 1.0 / math.sqrt(2.0 * math.pi)
F32 = jnp.float32
BF16 = jnp.bfloat16
FFC = 128
CH = 768
UNIT = CH
QB = 256
LONGEST = ROW - 3 * 128
GROUP = 3
SIZES = (2, 3, 4, 5, 6, 8)
SPACING = 3
SLOTS = 8
BT = 128
NBLK = ROW // BT


def dot_nn(a, b):
    return lax.dot_general(a, b, (((1,), (0,)), ((), ())), preferred_element_type=F32)


def dot_nt(a, b):
    return lax.dot_general(a, b, (((1,), (1,)), ((), ())), preferred_element_type=F32)


def dot_tn(a, b):
    return lax.dot_general(a, b, (((0,), (0,)), ((), ())), preferred_element_type=F32)


def own_row(seg_ref):
    return jnp.where(lax.axis_index("heads") == 0, seg_ref[0:1, :], seg_ref[1:2, :])


def iota(shape, dim):
    return lax.broadcasted_iota(jnp.int32, shape, dim)


def bucket_of(offset):
    distance = jnp.abs(offset)
    far = jnp.full(distance.shape, 8, jnp.int32)
    for edge in EDGES:
        far = far + (distance >= edge).astype(jnp.int32)
    near = jnp.where(distance < 8, distance, far)
    return near + jnp.where(offset > 0, 16, 0)


def picks_t(seg):
    lane = iota((1, ROW), 1)
    first = jnp.zeros((1, ROW), jnp.int32)
    for s in range(1, 4):
        count = jnp.sum((seg < s).astype(F32), axis=1, keepdims=True).astype(jnp.int32)
        first = jnp.where(seg == s, count, first)
    pos = lane - first
    return (iota((128, ROW), 0) == pos).astype(F32).astype(BF16)


def offset_picks(rows):
    return (bucket_of(256 - iota((rows, 512), 1)) == iota((rows, 512), 0)).astype(F32)


def key_marks(seg):
    i = iota((16, ROW), 0)
    block = iota((16, ROW), 1) // BT
    return jnp.where(i < 8, (seg == i).astype(F32), (block == i - 8).astype(F32)).astype(BF16)


def query_marks(seg, left, right):
    i = iota((16, ROW), 0)
    block = iota((16, ROW), 1) // BT
    excluded = jnp.where(jnp.logical_or(seg == i, i >= 4), 0.0, -BIG)
    j = i - 8
    far = jnp.where(j <= block - 2, left, jnp.where(j >= block + 2, right, 0.0))
    return jnp.where(i < 8, excluded, far).astype(BF16)


def attend_block(n, q, lo, base, kn, qaug, vaug, strip, pt_ref, mixed_ref, inv_ref):
    lo = jnp.minimum(lo, NBLK - n)
    rows = pl.ds(pl.multiple_of(lo * BT, BT), n * BT)
    cols = pl.ds(pl.multiple_of(q * QB, QB), QB)
    near = pl.ds(pl.multiple_of((lo - q * (QB // BT) + ROW // BT - QB // BT) * BT, BT), n * BT)

    def mix(j):
        o = dot_nn(vaug[j, :, rows], pt_ref[j, rows, :])
        inv = 1.0 / o[DH : DH + 1]
        out = pl.ds(pl.multiple_of((base + j) * DH, DH), DH)
        mixed_ref[out, cols] = (o[:DH] * inv).astype(BF16)
        inv_ref[pl.ds(base + j, 1), cols] = inv

    scores, peaks = [], []
    for j in range(GROUP):
        s = dot_nn(kn[j, rows, :], qaug[j, :, cols]) + strip[j, near, :]
        scores.append(s)
        peaks.append(jnp.max(s, axis=0, keepdims=True))
    for j in range(GROUP):
        if n < NBLK:
            pt_ref[j] = jnp.zeros((ROW, QB), BF16)
        pt_ref[j, rows, :] = jnp.exp(scores[j] - peaks[j]).astype(BF16)
        if j:
            mix(j - 1)
    mix(GROUP - 1)


def attend_heads(
    step, q, seg, table_f, span, qkv_ref, kaug, qaug, vaug, kn, strip, pt_ref, mixed_ref, inv_ref
):
    base = step * GROUP
    per = QB // BT
    zero = (ROW // BT - per) * BT
    @pl.when(q == 0)
    def _():
        for j in range(GROUP):
            rows = pl.ds(pl.multiple_of((base + j) * DH, DH), DH)
            values = table_f[pl.ds(base + j, 1), :]
            near = pltpu.roll(jnp.broadcast_to(values, (BT, 512)), 0, 1, stride=1, stride_axis=0)
            for d in range(-1, per + 1):
                for u in range(per):
                    if abs(d - u) <= 1:
                        at = 256 - 128 * (d - u)
                        strip[j, zero + d * BT : zero + (d + 1) * BT, u * BT : (u + 1) * BT] = near[
                            :, at : at + 128
                        ]
            qaug[j, 0:DH, :] = qkv_ref[0, rows, :]
            kaug[0:DH, :] = qkv_ref[1, rows, :]
            vaug[j, 0:DH, :] = qkv_ref[2, rows, :]
            qaug[j, DH : DH + 16, :] = query_marks(seg, values[:, 511:512], values[:, 1:2])
            kn[j] = kaug[...].T

    lo, n = span[0, q], span[1, q]
    last = 0
    for size in SIZES:

        @pl.when(jnp.logical_and(n > last, n <= size))
        def _():
            attend_block(size, q, lo, base, kn, qaug, vaug, strip, pt_ref, mixed_ref, inv_ref)

        last = size


def project_t(w_refs, yt, qkv_ref):
    for m in range(3):
        qkv_ref[m] = dot_tn(w_refs[m][...], yt).astype(BF16)


def head_setup(seg, tab_ref, table_f, span, kaug, qaug, vaug, strip):
    picks = offset_picks(NB).astype(BF16)
    heads = tab_ref.shape[0]
    table_f[0:heads, :] = dot_nn(tab_ref[...], picks)
    kaug[DH:, :] = jnp.zeros((128 - DH, ROW), BF16)
    qaug[:, DH:, :] = jnp.zeros((GROUP, 128 - DH, ROW), BF16)
    kaug[DH : DH + 16, :] = key_marks(seg)
    vaug[:, DH:, :] = jnp.ones((GROUP, 16, ROW), BF16)
    strip[...] = jnp.zeros(strip.shape, F32)
    for q in range(ROW // QB):
        lowest = jnp.min(seg[:, q * QB : (q + 1) * QB].astype(F32))
        highest = jnp.max(seg[:, q * QB : (q + 1) * QB].astype(F32))
        wide = seg.astype(F32)
        begin = jnp.sum((wide < lowest).astype(F32)).astype(jnp.int32) // BT
        end = (jnp.sum((wide <= highest).astype(F32)).astype(jnp.int32) + BT - 1) // BT
        span[0, q] = begin
        span[1, q] = end - begin


def forward_first(
    seg_ref, tok_ref, prompt_ref, gain_ref, wq, wk, wv, tab_ref,
    start_ref, yt_ref, qkv_ref, pt_ref, mixed_ref, inv_ref,
    table_f, span, kaug, qaug, vaug, kn, strip, padded, start_s, yt_s, qkv_s, sem,
):
    copies = [
        pltpu.make_async_copy(a, b, sem.at[k])
        for k, (a, b) in enumerate(((start_s, start_ref), (yt_s, yt_ref), (qkv_s, qkv_ref)))
    ]
    step, q = pl.program_id(0), pl.program_id(1)
    first = jnp.logical_and(step == 0, q == 0)
    seg = own_row(seg_ref)

    @pl.when(first)
    def _():
        padded[...] = jnp.zeros(padded.shape, BF16)
        padded[0:PROMPT, :] = prompt_ref[...]
        picks = picks_t(seg)
        looked = dot_tn(picks, padded[...])
        here = dot_tn(picks, (iota((128, 128), 0) < PROMPT).astype(F32).astype(BF16)) > 0.5
        tok = tok_ref[...].astype(F32)
        start = jnp.concatenate(
            [
                jnp.where(here, looked[:, c : c + 128], tok[:, c : c + 128])
                for c in range(0, D, 128)
            ],
            axis=1,
        )
        start_s[...] = start.astype(BF16)
        copies[0].start()
        inv = lax.rsqrt(jnp.mean(start * start, axis=1, keepdims=True) + EPS)
        yt = (start * inv * gain_ref[...][None, :]).astype(BF16).T
        yt_s[...] = yt
        copies[1].start()
        project_t((wq, wk, wv), yt, qkv_s)
        copies[2].start()
        head_setup(seg, tab_ref, table_f, span, kaug, qaug, vaug, strip)

    attend_heads(
        step, q, seg, table_f, span, qkv_s, kaug, qaug, vaug, kn, strip, pt_ref, mixed_ref, inv_ref
    )

    @pl.when(jnp.logical_and(step == pl.num_programs(0) - 1, q == pl.num_programs(1) - 1))
    def _():
        for copy in copies:
            copy.wait()


def forward_second(
    seg_ref, start_ref, yt_ref, gain_ref, wq, wk, wv, tab_ref, mixed_own, wo_own, wo_oth,
    qkv_ref, pt_ref, mixed_ref, inv_ref, middle_ref, x_ref, xt_ref,
    table_f, span, kaug, qaug, vaug, kn, strip, qkv_s, middle_s, x_s, xt_s, sem,
):
    qkv_copy = pltpu.make_async_copy(qkv_s, qkv_ref, sem.at[0])
    step, q = pl.program_id(0), pl.program_id(1)
    first = jnp.logical_and(step == 0, q == 0)
    seg = own_row(seg_ref)

    @pl.when(first)
    def _():
        project_t((wq, wk, wv), yt_ref[...], qkv_s)
        qkv_copy.start()
        head_setup(seg, tab_ref, table_f, span, kaug, qaug, vaug, strip)

    attend_heads(
        step, q, seg, table_f, span, qkv_s, kaug, qaug, vaug, kn, strip, pt_ref, mixed_ref, inv_ref
    )

    @pl.when(jnp.logical_and(step == pl.num_programs(0) - 1, q == pl.num_programs(1) - 1))
    def _():
        copies = []
        for k in range(0, ROW, QB):
            r = slice(k, k + QB)
            attn = dot_tn(mixed_own[:, r], wo_own[...]) + dot_tn(mixed_ref[:, r], wo_oth[...])
            middle = start_ref[r, :].astype(F32) + attn
            middle_s[r, :] = middle
            inv = lax.rsqrt(jnp.mean(middle * middle, axis=1, keepdims=True) + EPS)
            x = (middle * inv * gain_ref[...][None, :]).astype(BF16)
            x_s[r, :] = x
            xt_s[:, r] = x.T
            for src, dst in ((middle_s, middle_ref), (x_s, x_ref)):
                copies.append((src.at[r, :], dst.at[r, :]))
            copies.append((xt_s.at[:, r], xt_ref.at[:, r]))
            for m in range(3):
                at = 3 * (k // QB) + m
                pltpu.make_async_copy(*copies[at], sem.at[1 + at]).start()
        qkv_copy.wait()
        for at, pair in enumerate(copies):
            pltpu.make_async_copy(*pair, sem.at[1 + at]).wait()


def plan_stages(n_rows):
    n_bits = n_rows.bit_length() - 1
    size, slot = UNIT, 0
    stages, halved = [], []
    for j in range(n_bits):
        if j < n_bits - 1 and size % 32 == 0:
            size = size // 2
            halved.append((j, size))
            stages.append(("halve", j, size, slot))
        else:
            stages.append(("swap", j, size, slot))
        slot += size
    for j, n in reversed(halved):
        stages.append(("gather", j, n, slot))
        slot += n
    return stages, len(halved), slot


def stage_table(n_rows):
    stages, n_halved, _ = plan_stages(n_rows)
    n_bits = n_rows.bit_length() - 1
    me = lax.axis_index("rows")
    bits = [(me // (1 << b)) % 2 for b in range(n_bits)]
    peers = [me + (1 - 2 * bits[b]) * (1 << b) for b in range(n_bits)]
    rest = list(range(3, n_bits))
    sides = []
    for order in ([0, 2, 1] + rest, [1, 2, 0] + rest):
        bases, base, size = [], 0, UNIT
        for j in range(n_bits):
            bases.append(base)
            if j < n_halved:
                size = size // 2
                base = base + bits[order[j]] * size
        side = []
        for kind, j, n, _ in stages:
            keep = bases[j] + bits[order[j]] * n
            give = bases[j] + (1 - bits[order[j]]) * n
            src, dst = {
                "halve": (give, keep), "swap": (bases[j], bases[j]), "gather": (keep, give)
            }[kind]
            side.append((src, dst, peers[order[j]]))
        sides.append(side)
    table = [(kind, n, slot, sides[0][k], sides[1][k]) for k, (kind, _, n, slot) in enumerate(stages)]
    return table, peers


def whole(shape):
    n = len(shape)
    return pl.BlockSpec(shape, lambda *_: (0,) * n, pipeline_mode=pl.Buffered(1))


def whole_out(shape):
    n = len(shape)
    return pl.BlockSpec(shape, lambda *_: (0,) * n)


def sds(shape, dtype):
    return jax.ShapeDtypeStruct(shape, dtype)


def forward_scratch():
    return [
        pltpu.VMEM((8, 512), F32),
        pltpu.SMEM((2, ROW // QB), jnp.int32),
        pltpu.VMEM((128, ROW), BF16),
        pltpu.VMEM((GROUP, 128, ROW), BF16),
        pltpu.VMEM((GROUP, DH + 16, ROW), BF16),
        pltpu.VMEM((GROUP, ROW, 128), BF16),
        pltpu.VMEM((GROUP, 2 * ROW, QB), F32),
    ]


PARAMS = dict(vmem_limit_bytes=56 * 1024 * 1024)


def run_first(seg, tok, prompt, gain, wq, wk, wv, tab):
    cols = wq.shape[1]
    heads = cols // DH
    return pl.pallas_call(
        forward_first,
        grid=(heads // GROUP, ROW // QB),
        in_specs=[whole(a.shape) for a in (seg, tok, prompt, gain, wq, wk, wv, tab)],
        out_specs=[
            pl.BlockSpec(memory_space=pl.ANY),
            pl.BlockSpec(memory_space=pl.ANY),
            pl.BlockSpec(memory_space=pl.ANY),
            pl.BlockSpec((GROUP, ROW, QB), lambda h, q: (h, 0, q)),
            whole_out((cols, ROW)),
            whole_out((8, ROW)),
        ],
        out_shape=[
            sds((ROW, D), BF16),
            sds((D, ROW), BF16),
            sds((3, cols, ROW), BF16),
            sds((heads, ROW, ROW), BF16),
            sds((cols, ROW), BF16),
            sds((8, ROW), F32),
        ],
        scratch_shapes=forward_scratch() + [
            pltpu.VMEM((128, D), BF16),
            pltpu.VMEM((ROW, D), BF16),
            pltpu.VMEM((D, ROW), BF16),
            pltpu.VMEM((3, cols, ROW), BF16),
            pltpu.SemaphoreType.DMA((3,)),
        ],
        compiler_params=pltpu.CompilerParams(**PARAMS),
        cost_estimate=pl.CostEstimate(flops=2 * 10**10, bytes_accessed=10**7, transcendentals=0),
        name="attend_own",
    )(seg, tok, prompt, gain, wq, wk, wv, tab)


def run_second(seg, start, yt, gain, wq, wk, wv, tab, mixed_own, wo_own, wo_oth):
    cols = wq.shape[1]
    heads = cols // DH
    ins = (seg, start, yt, gain, wq, wk, wv, tab, mixed_own, wo_own, wo_oth)
    return pl.pallas_call(
        forward_second,
        grid=(heads // GROUP, ROW // QB),
        in_specs=[whole(a.shape) for a in ins],
        out_specs=[
            pl.BlockSpec(memory_space=pl.ANY),
            pl.BlockSpec((GROUP, ROW, QB), lambda h, q: (h, 0, q)),
            whole_out((cols, ROW)),
            whole_out((8, ROW)),
            pl.BlockSpec(memory_space=pl.ANY),
            pl.BlockSpec(memory_space=pl.ANY),
            pl.BlockSpec(memory_space=pl.ANY),
        ],
        out_shape=[
            sds((3, cols, ROW), BF16),
            sds((heads, ROW, ROW), BF16),
            sds((cols, ROW), BF16),
            sds((8, ROW), F32),
            sds((ROW, D), F32),
            sds((ROW, D), BF16),
            sds((D, ROW), BF16),
        ],
        scratch_shapes=forward_scratch() + [
            pltpu.VMEM((3, cols, ROW), BF16),
            pltpu.VMEM((ROW, D), F32),
            pltpu.VMEM((ROW, D), BF16),
            pltpu.VMEM((D, ROW), BF16),
            pltpu.SemaphoreType.DMA((1 + 3 * (ROW // QB),)),
        ],
        compiler_params=pltpu.CompilerParams(**PARAMS),
        cost_estimate=pl.CostEstimate(flops=2 * 10**10, bytes_accessed=10**7, transcendentals=0),
        name="attend_other",
    )(*ins)


def norm_back(value, gain, grad):
    inv = lax.rsqrt(jnp.mean(value * value, axis=1, keepdims=True) + EPS)
    scaled = grad * gain
    inner = jnp.mean(scaled * value, axis=1, keepdims=True)
    back = inv * scaled - value * (inv * inv * inv * inner)
    return back, jnp.sum(grad * (value * inv), axis=0, keepdims=True)


def backward(
    n_ff, n_heads, n_rows,
    seg_ref, gain_a_ref, gain_f_ref, win_own, win_oth, wout_own, wout_oth, pt_own, pt_oth,
    x_hbm, xt_hbm, og_hbm, mid_hbm, start_hbm, yt_hbm, qkv_own_hbm, qkv_oth_hbm,
    mix_own_hbm, mix_oth_hbm, inv_own_hbm, inv_oth_hbm, wq_own_hbm, wk_own_hbm, wv_own_hbm, wq_oth_hbm, wk_oth_hbm,
    wv_oth_hbm, wo_own_hbm, wo_oth_hbm,
    result_hbm, gtok_hbm, out_in, out_out, out_q, out_k, out_v, out_o, out_small,
    x, xt, og, mid, qkv, mix, inv, gmix, wqkv, wo, feed, gnf, dst, dqkv, kaug, vaug, doaug,
    tacc, gvec, gains, ptb, g, xsend, xrecv, ring, load_sem, late_sem, pt_sem, out_sem, xs_sem, xr_sem,
    send_sem, recv_sem,
):
    s = pl.program_id(0)
    heads_half = n_heads // 2
    cols = heads_half * DH
    me = lax.axis_index("heads")
    early = [(x_hbm, x), (xt_hbm, xt), (og_hbm, og)]
    later = [
        (mid_hbm, mid),
        (qkv_own_hbm, qkv.at[0]),
        (qkv_oth_hbm, qkv.at[1]),
        (mix_own_hbm, mix.at[0]),
        (mix_oth_hbm, mix.at[1]),
        (inv_own_hbm, inv.at[0]),
        (inv_oth_hbm, inv.at[1]),
        (wq_own_hbm, wqkv.at[0, 0]),
        (wk_own_hbm, wqkv.at[0, 1]),
        (wv_own_hbm, wqkv.at[0, 2]),
        (wq_oth_hbm, wqkv.at[1, 0]),
        (wk_oth_hbm, wqkv.at[1, 1]),
        (wv_oth_hbm, wqkv.at[1, 2]),
        (wo_own_hbm, wo.at[0]),
        (wo_oth_hbm, wo.at[1]),
    ]
    n_early = len(early)
    loads = [
        pltpu.make_async_copy(a, b, load_sem.at[i]) for i, (a, b) in enumerate(early + later)
    ]
    late = [
        pltpu.make_async_copy(start_hbm, x, late_sem.at[0]),
        pltpu.make_async_copy(yt_hbm, xt, late_sem.at[1]),
    ]

    def pt_start(i):
        hh = 2 * (i // 4) + i % 2
        for o, ref in enumerate((pt_own, pt_oth)):

            @pl.when((i % 4) // 2 == o)
            def _():
                pltpu.make_async_copy(ref.at[hh], ptb.at[i % 2], pt_sem.at[i % 2]).start()

    n_out = cols // 128
    n_chunks = 2 * n_ff + 4 * n_out + 1
    n_units = n_chunks
    table, peers = stage_table(n_rows)
    n_stages = len(table)
    core = {"heads": 1 - me}

    def swap(slot):
        return pltpu.make_async_remote_copy(
            src_ref=xsend.at[slot],
            dst_ref=xrecv.at[slot],
            send_sem=xs_sem.at[slot],
            recv_sem=xr_sem.at[slot],
            device_id=core,
            device_id_type=pl.DeviceIdType.MESH,
        )

    def emit(c, slot, own, oth):
        for blocks, ref in ((own, g.at[c]), (oth, xsend.at[slot])):
            for b, block in enumerate(blocks):
                n = block.shape[0]
                ref[b * n : (b + 1) * n, :] = block.astype(BF16)
        swap(slot).start()

    def collect(c, slot):
        swap(slot).wait()
        g[c] = (g[c].astype(F32) + xrecv[slot].astype(F32)).astype(BF16)

    def stage_copy(k, c, par, odd):
        kind, n, slot, even_side, odd_side = table[k]
        src, dst, peer = (p + odd * (q - p) for p, q in zip(even_side, odd_side))
        copy = pltpu.make_async_remote_copy(
            src_ref=g.at[c, pl.ds(pl.multiple_of(src, 16), n), :],
            dst_ref=ring.at[par, slot : slot + n, :],
            send_sem=send_sem.at[k, par],
            recv_sem=recv_sem.at[k, par],
            device_id={"rows": peer},
            device_id_type=pl.DeviceIdType.MESH,
        )
        return copy, pl.ds(pl.multiple_of(dst, 16), n)

    def stage_end(k, c, par, odd):
        kind, n, slot = table[k][:3]
        copy, dst = stage_copy(k, c, par, odd)
        copy.wait()
        part = ring[par, slot : slot + n, :]
        if kind != "gather":
            part = (g[c, dst, :].astype(F32) + part.astype(F32)).astype(BF16)
        g[c, dst, :] = part

    def out_wait(par):
        pltpu.make_async_copy(g.at[0], out_in.at[:, 0:128], out_sem.at[par]).wait()

    def out_start(c, odd):
        sem = out_sem.at[odd]

        @pl.when(c >= 2)
        def _():
            out_wait(odd)

        def wide(ref, col):
            dst = ref.at[:, pl.ds(pl.multiple_of(col * 128, 128), 128)]
            pltpu.make_async_copy(g.at[c], dst, sem).start()

        def tall(ref, row):
            pltpu.make_async_copy(g.at[c], ref.at[row], sem).start()

        base = 2 * n_ff + n_out

        @pl.when(jnp.logical_and(c < 2 * n_ff, odd == 0))
        def _():
            wide(out_in, c // 2)

        @pl.when(jnp.logical_and(c < 2 * n_ff, odd == 1))
        def _():
            tall(out_out, c // 2)

        @pl.when(c >= 2 * n_ff)
        def _():
            @pl.when(c < base)
            def _():
                tall(out_o, c - 2 * n_ff)

            for m, ref in enumerate((out_q, out_k, out_v)):
                at = jnp.logical_and(c >= base, c < n_chunks - 1)

                @pl.when(jnp.logical_and(at, (c - base) % 3 == m))
                def _():
                    wide(ref, (c - base) // 3)

            @pl.when(c == n_chunks - 1)
            def _():
                tall(out_small, 0)

    wo_end = 2 * n_ff + n_out
    holes = ((wo_end, 2), (wo_end + 5, 1))

    def tick(t):
        turn = lax.rem(t, SLOTS)
        parity = lax.rem(t, 2)
        for k in range(n_stages, -1, -1):
            v = t - SPACING * k
            c = v
            live_unit = v >= 0
            for at, length in holes:
                c = c - jnp.where(v >= at + length, length, 0)
                live_unit = jnp.logical_and(live_unit, jnp.logical_or(v < at, v >= at + length))
            par = turn + (-SPACING * k) % SLOTS
            par = par - jnp.where(par >= SLOTS, SLOTS, 0)
            odd = parity if SPACING * k % 2 == 0 else 1 - parity

            def step(k=k, c=c, par=par, odd=odd):
                if k > 0:
                    stage_end(k - 1, c, par, odd)
                if k < n_stages:
                    stage_copy(k, c, par, odd)[0].start()
                else:
                    out_start(c, odd)

            pl.when(jnp.logical_and(live_unit, c < n_units))(step)

    def collect_ff(e):
        for j in range(2):
            collect(2 * e + j, 2 * (e % 4) + j)

    def group_slot(e, m):
        return 3 + m if e % 2 == 0 else m

    def collect_group(e):
        for m in range(3):
            collect((2 * n_ff + n_out + 3 * e + m), group_slot(e, m))

    def lanes(a):
        return [a[:, k : k + 128] for k in range(0, a.shape[1], 128)]

    @pl.when(s == 0)
    def _():
        for copy in loads:
            copy.start()
        barrier = pltpu.get_barrier_semaphore()
        for peer in [{"rows": p} for p in peers] + [core]:
            pl.semaphore_signal(
                barrier, inc=1, device_id=peer, device_id_type=pl.DeviceIdType.MESH
            )
        pl.semaphore_wait(barrier, len(peers) + 1)
        feed[...] = jnp.zeros(feed.shape, F32)
        gnf[...] = jnp.zeros(gnf.shape, F32)
        for copy in loads[:n_early]:
            copy.wait()

    @pl.when(s < n_ff)
    def _():
        wi = jnp.concatenate([win_own[...], win_oth[...]], axis=1)
        wout = jnp.concatenate([wout_own[...], wout_oth[...]], axis=0)
        halves = [slice(0, ROW // 2), slice(ROW // 2, ROW)]
        pres = [dot_nn(x[r, :], wi) for r in halves]
        gacts = [dot_nt(og[r, :], wout) for r in halves]
        acts, gpres = [], []
        for pre, gact in zip(pres, gacts):
            cdf = 0.5 * (1.0 + lax.erf(pre * ROOT_HALF))
            acts.append((pre * cdf).astype(BF16))
            slope = cdf + pre * jnp.exp(-0.5 * pre * pre) * DENSITY
            gpres.append((gact * slope).astype(BF16))
        for r, act, gpre in zip(halves, acts, gpres):
            feed[r, :] += dot_nn(act, wout)
            gnf[r, :] += dot_nt(gpre, wi)
        active = jnp.concatenate(acts, axis=0)
        gpre = jnp.concatenate(gpres, axis=0)

        @pl.when(s >= 2)
        def _():
            collect_ff(s - 2)
            tick(2 * (s - 2))

        dwin = dot_nn(xt[...], gpre)
        dwout = dot_tn(active, og[...])

        emit(2 * s, 2 * (s % 4), [dwin[:, :FFC]], [dwin[:, FFC:]])
        emit(2 * s + 1, 2 * (s % 4) + 1, lanes(dwout[:FFC]), lanes(dwout[FFC:]))

        @pl.when(s >= 2)
        def _():
            tick(2 * (s - 2) + 1)

    @pl.when(s == n_ff)
    def _():
        for copy in late:
            copy.start()
        pt_start(0)
        for copy in loads[n_early:]:
            copy.wait()
        collect_ff(n_ff - 2)
        t0 = 2 * (n_ff - 2)
        tick(t0)
        middle = mid[...]
        dst[:, 0:D] = (middle + feed[...]).astype(BF16)
        to_result = pltpu.make_async_copy(dst.at[:, 0:D], result_hbm, late_sem.at[2])
        to_result.start()
        back, gain_grad = norm_back(middle, gain_f_ref[...][None, :], gnf[...])
        gmid = og[...].astype(F32) + back
        gains[0:1, :] = gain_grad
        mid[...] = gmid
        tick(t0 + 1)
        ga = gmid.astype(BF16)
        dwo = [dot_nn(mix[o], ga) for o in range(2)]
        collect_ff(n_ff - 1)
        for j in range(n_out):
            rows = slice(j * 128, (j + 1) * 128)
            emit((2 * n_ff + j), j, lanes(dwo[0][rows]), lanes(dwo[1][rows]))
        for o in range(2):
            grad = dot_nt(wo[o], ga)
            for k in range(heads_half):
                rows = slice(k * DH, (k + 1) * DH)
                gmix[o, rows, :] = (grad[rows] * inv[o, k : k + 1, :]).astype(BF16)
        tick(t0 + 2)
        gnf[...] = jnp.zeros(gnf.shape, F32)
        kaug[DH:, :] = key_marks(own_row(seg_ref))
        vaug[DH:, :] = (iota((16, ROW), 0) < 3).astype(F32).astype(BF16)
        gvec[...] = jnp.zeros(gvec.shape, F32)
        to_result.wait()
        dst[...] = jnp.zeros(dst.shape, BF16)
        for copy in late:
            copy.wait()
        tick(t0 + 3)

    i = s - (n_ff + 1)

    def head_back(o, pt_ref):
        hh = 2 * (i // 4) + i % 2
        rows = pl.ds(pl.multiple_of(hh * DH, DH), DH)
        dot_ = gmix[o, rows, :]
        delta = jnp.sum(dot_.astype(F32) * mix[o, rows, :].astype(F32), axis=0, keepdims=True)
        d1 = delta.astype(BF16).astype(F32)
        d2 = (delta - d1).astype(BF16).astype(F32)
        d3 = delta - d1 - d2
        k = iota((16, ROW), 0)
        vaug[0:DH, :] = qkv[o, 2, rows, :]
        kaug[0:DH, :] = qkv[o, 1, rows, :]
        doaug[0:DH, :] = dot_
        doaug[DH:, :] = jnp.where(
            k == 0, -d1, jnp.where(k == 1, -d2, jnp.where(k == 2, -d3, 0.0))
        ).astype(BF16)
        va = vaug[...]
        ka = kaug[...]
        out_rows = pl.ds(pl.multiple_of(o * 128 + (i % 2) * DH, DH), DH)
        tacc[...] = jnp.zeros(tacc.shape, F32)
        left = jnp.zeros((1, QB), F32)
        right = jnp.zeros((1, QB), F32)
        n_blocks = ROW // QB

        def live(b):
            ks = [
                kb for kb in range(NBLK)
                if max(kb * BT - (b + 1) * QB, b * QB - (kb + 1) * BT) + 1 < LONGEST
            ]
            return slice(ks[0] * BT, (ks[-1] + 1) * BT)

        def grad_probs(b):
            return dot_tn(va[:, live(b)], doaug[:, b * QB : (b + 1) * QB])

        dp = grad_probs(0)
        dqkv[2, out_rows, :] = dot_nt(dot_, pt_ref[...]).astype(BF16)
        for b in range(n_blocks):
            qs = slice(b * QB, (b + 1) * QB)
            ahead = grad_probs(b + 1) if b + 1 < n_blocks else None
            ks = live(b)
            ds = pt_ref[ks, qs].astype(F32) * dp
            for u in range(QB // BT):
                qb = b * (QB // BT) + u
                for d in (-1, 0, 1):
                    kb = qb + d
                    if 0 <= kb < NBLK:
                        at = kb * BT - ks.start
                        tacc[:, 256 - 128 * d : 384 - 128 * d] += ds[
                            at : at + BT, u * BT : (u + 1) * BT
                        ]
            dst[ks, qs] = ds.astype(BF16)
            dp = ahead
        for b in range(n_blocks):
            qs = slice(b * QB, (b + 1) * QB)
            r = dot_nn(ka[:, live(b)], dst[live(b), qs])
            dqkv[0, out_rows, qs] = r[:DH].astype(BF16)
            sums = r[DH + 8 :]
            j = iota((8, QB), 0)
            block = b * (QB // BT) + iota((8, QB), 1) // BT
            left = left + jnp.sum(jnp.where(j <= block - 2, sums, 0.0), axis=0, keepdims=True)
            right = right + jnp.sum(jnp.where(j >= block + 2, sums, 0.0), axis=0, keepdims=True)
        dqkv[1, out_rows, :] = dot_nt(qkv[o, 0, rows, :], dst[...]).astype(BF16)
        flip = (iota((BT, BT), 0) + iota((BT, BT), 1) == BT - 1).astype(F32).astype(BF16)
        near = tacc[...]
        high = near.astype(BF16)
        low = (near - high.astype(F32)).astype(BF16)
        turned = dot_nn(flip, high) + dot_nn(flip, low)
        skew = pltpu.roll(turned, 0, 1, stride=1, stride_axis=0)
        vec = pltpu.roll(jnp.sum(skew, axis=0, keepdims=True), 512 - (BT - 1), 1)
        lane = iota((1, 512), 1)
        vec = vec + jnp.where(lane == 511, jnp.sum(left, axis=1, keepdims=True), 0.0)
        vec = vec + jnp.where(lane == 1, jnp.sum(right, axis=1, keepdims=True), 0.0)
        owner = me + o * (1 - 2 * me)
        gvec[pl.ds(owner * heads_half + hh, 1), :] = vec

    in_heads = jnp.logical_and(i >= 0, i < n_heads)

    @pl.when(in_heads)
    def _():
        @pl.when(i + 1 < n_heads)
        def _():
            pt_start(i + 1)

        pltpu.make_async_copy(pt_own.at[0], ptb.at[i % 2], pt_sem.at[i % 2]).wait()
        head_back((i % 4) // 2, ptb.at[i % 2])

        @pl.when(i == 0)
        def _():
            for j in range(n_out):
                collect((2 * n_ff + j), j)

        for e in range(n_heads // 4 - 1):

            @pl.when(i == 4 * (e + 1) + 1)
            def _():
                collect_group(e)

        tick(2 * n_ff + i)

    def group_back(grp):
        for m in range(3):
            dw = dot_nt(xt[...], dqkv[m])
            emit(
                2 * n_ff + n_out + 3 * grp + m, group_slot(grp, m),
                [dw[:, :128]], [dw[:, 128:]],
            )
        cols_g = slice(grp * 128, (grp + 1) * 128)
        for m in range(3):
            w = jnp.concatenate([wqkv[0, m, :, cols_g], wqkv[1, m, :, cols_g]], axis=1)
            gnf[...] += lax.dot_general(
                dqkv[m], w, (((0,), (1,)), ((), ())), preferred_element_type=F32
            )

    for grp in range(n_heads // 4):

        @pl.when(i == 4 * grp + 3)
        def _():
            group_back(grp)

    @pl.when(i == n_heads)
    def _():
        seg = own_row(seg_ref)
        start = x[...].astype(F32)
        back, gain_grad = norm_back(start, gain_a_ref[...][None, :], gnf[...])
        gstart = mid[...] + back
        n_groups = n_heads // 4
        collect_group(n_groups - 1)
        t0 = 2 * n_ff + n_heads
        tick(t0)
        picks = picks_t(seg)
        here = dot_tn(picks, (iota((128, 128), 0) < PROMPT).astype(F32).astype(BF16)) > 0.5
        for c in range(0, D, 128):
            og[:, c : c + 128] = jnp.where(here, 0.0, gstart[:, c : c + 128]).astype(BF16)
        to_gtok = pltpu.make_async_copy(og, gtok_hbm, late_sem.at[0])
        to_gtok.start()
        high = gstart.astype(BF16)
        low = (gstart - high.astype(F32)).astype(BF16)
        tick(t0 + 1)
        gprompt = dot_nn(picks, high) + dot_nn(picks, low)
        opicks = offset_picks(128).astype(BF16)
        gv = gvec[...]
        g1 = gv.astype(BF16)
        g2 = (gv - g1.astype(F32)).astype(BF16)
        gtab = dot_nt(g1, opicks) + dot_nt(g2, opicks)
        row = iota((128, D), 0)
        small = jnp.where(row < PROMPT, gprompt, 0.0)
        small = jnp.where(row == PROMPT, gain_grad, small)
        small = jnp.where(row == PROMPT + 1, gains[0:1, :], small)
        blocks = lanes(small)
        wide = jnp.concatenate([jnp.zeros((104, 128), F32), gtab, jnp.zeros((8, 128), F32)], axis=0)
        blocks[0] = blocks[0] + wide
        slot = group_slot(n_groups, 0)
        emit((n_chunks - 1), slot, blocks, blocks)
        tick(t0 + 2)
        collect((n_chunks - 1), slot)

        @pl.loop(t0 + 3, n_units + sum(h[1] for h in holes) + SPACING * n_stages)
        def _(t):
            tick(t)

        to_gtok.wait()
        out_wait(0)
        out_wait(1)


def run_backward(
    n_rows, seg, gain_a, gain_f, win_own, win_oth, wout_own, wout_oth, pt_own, pt_oth, rest
):
    n_ff = win_own.shape[1] // FFC
    n_heads = 2 * pt_own.shape[0]
    cols = n_heads * DH // 2
    n_chunks = 2 * n_ff + 4 * (cols // 128) + 1
    first = n_ff + 1
    stages, _, ring_rows = plan_stages(n_rows)
    n_stages = len(stages)

    def ff(s):
        return jnp.minimum(s, n_ff - 1)

    blk_in = pl.BlockSpec((D, FFC), lambda s: (0, ff(s)))
    blk_out = pl.BlockSpec((FFC, D), lambda s: (ff(s), 0))
    anyspec = pl.BlockSpec(memory_space=pl.ANY)
    return pl.pallas_call(
        partial(backward, n_ff, n_heads, n_rows),
        grid=(first + n_heads + 1,),
        in_specs=[
            whole(seg.shape), whole(gain_a.shape), whole(gain_f.shape),
            blk_in, blk_in, blk_out, blk_out,
        ] + [anyspec] * (2 + len(rest)),
        out_specs=[anyspec] * 9,
        out_shape=[sds((ROW, D), BF16), sds((ROW, D), BF16)] + [
            sds(shape, BF16)
            for shape in (win_own.shape, (n_ff, CH, 128))
            + ((D, cols),) * 3 + ((cols // 128, CH, 128), (1, CH, 128))
        ],
        scratch_shapes=[
            pltpu.VMEM((ROW, D), BF16),
            pltpu.VMEM((D, ROW), BF16),
            pltpu.VMEM((ROW, D), BF16),
            pltpu.VMEM((ROW, D), F32),
            pltpu.VMEM((2, 3, cols, ROW), BF16),
            pltpu.VMEM((2, cols, ROW), BF16),
            pltpu.VMEM((2, 8, ROW), F32),
            pltpu.VMEM((2, cols, ROW), BF16),
            pltpu.VMEM((2, 3, D, cols), BF16),
            pltpu.VMEM((2, cols, D), BF16),
            pltpu.VMEM((ROW, D), F32),
            pltpu.VMEM((ROW, D), F32),
            pltpu.VMEM((ROW, ROW), BF16),
            pltpu.VMEM((3, 256, ROW), BF16),
            pltpu.VMEM((DH + 16, ROW), BF16),
            pltpu.VMEM((DH + 16, ROW), BF16),
            pltpu.VMEM((DH + 16, ROW), BF16),
            pltpu.VMEM((BT, 512), F32),
            pltpu.VMEM((16, 512), F32),
            pltpu.VMEM((8, D), F32),
            pltpu.VMEM((2, ROW, ROW), BF16),
            pltpu.VMEM((n_chunks, UNIT, 128), BF16),
            pltpu.VMEM((8, CH, 128), BF16),
            pltpu.VMEM((8, CH, 128), BF16),
            pltpu.VMEM((SLOTS, ring_rows, 128), BF16),
            pltpu.SemaphoreType.DMA((18,)),
            pltpu.SemaphoreType.DMA((3,)),
            pltpu.SemaphoreType.DMA((2,)),
            pltpu.SemaphoreType.DMA((2,)),
            pltpu.SemaphoreType.DMA((8,)),
            pltpu.SemaphoreType.DMA((8,)),
            pltpu.SemaphoreType.DMA((n_stages, SLOTS)),
            pltpu.SemaphoreType.DMA((n_stages, SLOTS)),
        ],
        compiler_params=pltpu.CompilerParams(
            vmem_limit_bytes=62 * 1024 * 1024, collective_id=0, has_side_effects=True
        ),
        name="backward",
    )(seg, gain_a, gain_f, win_own, win_oth, wout_own, wout_oth, pt_own, pt_oth, *rest)


def untile(src, dst):
    for c in range(src.shape[0]):
        for b in range(D // 128):
            dst[c * 128 : (c + 1) * 128, b * 128 : (b + 1) * 128] = src[
                c, b * 128 : (b + 1) * 128, :
            ].astype(F32)


def finish(
    heads, result, gtok, small, g_q, g_k, g_v, g_wo, g_in, g_out,
    o_result, o_gtok, o_prompt, o_gain_a, o_q, o_k, o_v, o_wo, o_tab, o_gain_f, o_in, o_out, rows,
):
    o_result[...] = result[...]
    o_gtok[...] = gtok[...]
    for src, dst in ((g_q, o_q), (g_k, o_k), (g_v, o_v), (g_in, o_in)):
        dst[...] = src[...].astype(F32)
    untile(g_out, o_out)

    @pl.when(pl.program_id(0) == 0)
    def _():
        untile(small, rows)
        untile(g_wo, o_wo)
        o_prompt[...] = rows[0:PROMPT, :]
        o_gain_a[...] = rows[PROMPT, :]
        o_gain_f[...] = rows[PROMPT + 1, :]
        low = lax.axis_index("heads") == 0
        at = 104
        tab = [
            jnp.where(low, rows[at + k : at + k + 1, 0:128], rows[at + heads + k : at + heads + k + 1, 0:128])
            for k in range(heads)
        ]
        tab.append(jnp.zeros((8 - heads, 128), F32))
        o_tab[...] = jnp.concatenate(tab, axis=0)[0:heads, 0:NB]


def run_finish(heads, result, gtok, small, *grads):
    steps = 2

    def part(shape):
        zeros = (0,) * (len(shape) - 1)
        return pl.BlockSpec((shape[0] // steps,) + shape[1:], lambda i: (i,) + zeros)

    g_q, g_k, g_v, g_wo, g_in, g_out = grads
    wo_shape, out_shape = ((a.shape[0] * 128, D) for a in (g_wo, g_out))
    whole_1d = pl.BlockSpec((D,), lambda i: (0,))
    return pl.pallas_call(
        partial(finish, heads),
        grid=(steps,),
        in_specs=[part(result.shape), part(gtok.shape), whole(small.shape)]
        + [part(a.shape) for a in (g_q, g_k, g_v)]
        + [whole(g_wo.shape), part(g_in.shape), part(g_out.shape)],
        out_specs=[part(result.shape), part(gtok.shape), whole_out((PROMPT, D)), whole_1d]
        + [part(a.shape) for a in (g_q, g_k, g_v)]
        + [whole_out(wo_shape), whole_out((heads, NB)), whole_1d, part(g_in.shape), part(out_shape)],
        out_shape=[sds(result.shape, BF16), sds(gtok.shape, BF16), sds((PROMPT, D), F32), sds((D,), F32)]
        + [sds(a.shape, F32) for a in (g_q, g_k, g_v)]
        + [sds(wo_shape, F32), sds((heads, NB), F32), sds((D,), F32)]
        + [sds(g_in.shape, F32), sds(out_shape, F32)],
        scratch_shapes=[pltpu.VMEM((128, D), F32)],
        compiler_params=pltpu.CompilerParams(vmem_limit_bytes=62 * 1024 * 1024),
        name="finish",
    )(result, gtok, small, *grads)


def on_device(
    tokens, prompt, segment_ids, gain_attn, w_query, w_key, w_value, w_attn_out, bias_table,
    gain_ff, w_in, w_out, out_grad,
):
    seg = segment_ids
    swap = [(0, 1), (1, 0)]

    def other(a):
        return lax.ppermute(a, "heads", swap)

    tab_oth, wq_oth, wk_oth, wv_oth = (other(a) for a in (bias_table.T, w_query, w_key, w_value))
    wo_oth, win_oth, wout_oth = other(w_attn_out), other(w_in), other(w_out)
    gain_a, gain_f = gain_attn, gain_ff
    start, yt, qkv_own, pt_own, mix_own, inv_own = run_first(
        seg, tokens, prompt, gain_a, w_query, w_key, w_value, bias_table.T
    )
    qkv_oth, pt_oth, mix_oth, inv_oth, middle, x, xt = run_second(
        seg, start, yt, gain_f, wq_oth, wk_oth, wv_oth, tab_oth, mix_own, w_attn_out, wo_oth
    )
    result, gtok, g_in, g_out, g_q, g_k, g_v, g_wo, small = run_backward(
        lax.axis_size("rows"),
        seg, gain_a, gain_f, w_in, win_oth, w_out, wout_oth, pt_own, pt_oth,
        [x, xt, out_grad, middle, start, yt, qkv_own, qkv_oth, mix_own, mix_oth,
         inv_own, inv_oth,
         w_query, w_key, w_value, wq_oth, wk_oth, wv_oth, w_attn_out, wo_oth],
    )
    (
        result, gtok, g_prompt, g_gain_a, g_q, g_k, g_v, g_wo, g_tab, g_gain_f, g_in, g_out,
    ) = run_finish(bias_table.shape[1], result, gtok, small, g_q, g_k, g_v, g_wo, g_in, g_out)
    return (
        result, gtok, g_prompt, g_gain_a, g_q, g_k, g_v, g_wo, g_tab.T, g_gain_f, g_in, g_out,
    )


def solution(mesh):
    both = P(("rows", "heads"), None)
    cols = P(None, "heads")
    rows = P("heads", None)
    in_specs = (
        both, P(), P("rows", None), P(), cols, cols, cols, rows, cols, P(), cols, rows, both,
    )
    out_specs = (both, both, P(), P(), cols, cols, cols, rows, cols, P(), cols, rows)
    return jax.shard_map(
        on_device, mesh=mesh, in_specs=in_specs, out_specs=out_specs, check_vma=False
    )
```

```python
from functools import partial
import math

import jax
import jax.numpy as jnp
from jax import lax
from jax.experimental import pallas as pl
from jax.experimental.pallas import tpu as pltpu
from jax.sharding import PartitionSpec as P

D = 768
DH = 64
NB = 32
ROW = 1024
PROMPT = 100
BIG = 1e30
EDGES = (12, 16, 23, 32, 46, 64, 91)
EPS = 1e-06
ROOT_HALF = 1.0 / math.sqrt(2.0)
DENSITY = 1.0 / math.sqrt(2.0 * math.pi)
F32 = jnp.float32
BF16 = jnp.bfloat16
FFC = 128
CH = 768
UNIT = CH
QB = 256
LONGEST = ROW - 3 * 128
GROUP = 3
SIZES = (2, 3, 4, 5, 6, 8)
SPACING = 3
SLOTS = 8
BT = 128
NBLK = ROW // BT


def dot_nn(a, b):
    return lax.dot_general(a, b, (((1,), (0,)), ((), ())), preferred_element_type=F32)


def dot_nt(a, b):
    return lax.dot_general(a, b, (((1,), (1,)), ((), ())), preferred_element_type=F32)


def dot_tn(a, b):
    return lax.dot_general(a, b, (((0,), (0,)), ((), ())), preferred_element_type=F32)


def own_row(seg_ref):
    return jnp.where(lax.axis_index("heads") == 0, seg_ref[0:1, :], seg_ref[1:2, :])


def iota(shape, dim):
    return lax.broadcasted_iota(jnp.int32, shape, dim)


def bucket_of(offset):
    distance = jnp.abs(offset)
    far = jnp.full(distance.shape, 8, jnp.int32)
    for edge in EDGES:
        far = far + (distance >= edge).astype(jnp.int32)
    near = jnp.where(distance < 8, distance, far)
    return near + jnp.where(offset > 0, 16, 0)


def picks_t(seg):
    lane = iota((1, ROW), 1)
    first = jnp.zeros((1, ROW), jnp.int32)
    for s in range(1, 4):
        count = jnp.sum((seg < s).astype(F32), axis=1, keepdims=True).astype(jnp.int32)
        first = jnp.where(seg == s, count, first)
    pos = lane - first
    return (iota((128, ROW), 0) == pos).astype(F32).astype(BF16)


def offset_picks(rows):
    return (bucket_of(256 - iota((rows, 512), 1)) == iota((rows, 512), 0)).astype(F32)


def key_marks(seg):
    i = iota((16, ROW), 0)
    block = iota((16, ROW), 1) // BT
    return jnp.where(i < 8, (seg == i).astype(F32), (block == i - 8).astype(F32)).astype(BF16)


def query_marks(seg, left, right):
    i = iota((16, ROW), 0)
    block = iota((16, ROW), 1) // BT
    excluded = jnp.where(jnp.logical_or(seg == i, i >= 4), 0.0, -BIG)
    j = i - 8
    far = jnp.where(j <= block - 2, left, jnp.where(j >= block + 2, right, 0.0))
    return jnp.where(i < 8, excluded, far).astype(BF16)


def attend_block(n, q, lo, base, kn, qaug, vaug, strip, pt_ref, mixed_ref, inv_ref):
    lo = jnp.minimum(lo, NBLK - n)
    rows = pl.ds(pl.multiple_of(lo * BT, BT), n * BT)
    cols = pl.ds(pl.multiple_of(q * QB, QB), QB)
    near = pl.ds(pl.multiple_of((lo - q * (QB // BT) + ROW // BT - QB // BT) * BT, BT), n * BT)

    def mix(j):
        o = dot_nn(vaug[j, :, rows], pt_ref[j, rows, :])
        inv = 1.0 / o[DH : DH + 1]
        out = pl.ds(pl.multiple_of((base + j) * DH, DH), DH)
        mixed_ref[out, cols] = (o[:DH] * inv).astype(BF16)
        inv_ref[pl.ds(base + j, 1), cols] = inv

    scores, peaks = [], []
    for j in range(GROUP):
        s = dot_nn(kn[j, rows, :], qaug[j, :, cols]) + strip[j, near, :]
        scores.append(s)
        peaks.append(jnp.max(s, axis=0, keepdims=True))
    for j in range(GROUP):
        if n < NBLK:
            pt_ref[j] = jnp.zeros((ROW, QB), BF16)
        pt_ref[j, rows, :] = jnp.exp(scores[j] - peaks[j]).astype(BF16)
        if j:
            mix(j - 1)
    mix(GROUP - 1)


def attend_heads(
    step, q, seg, table_f, span, qkv_ref, kaug, qaug, vaug, kn, strip, pt_ref, mixed_ref, inv_ref
):
    base = step * GROUP
    per = QB // BT
    zero = (ROW // BT - per) * BT
    @pl.when(q == 0)
    def _():
        for j in range(GROUP):
            rows = pl.ds(pl.multiple_of((base + j) * DH, DH), DH)
            values = table_f[pl.ds(base + j, 1), :]
            near = pltpu.roll(jnp.broadcast_to(values, (BT, 512)), 0, 1, stride=1, stride_axis=0)
            for d in range(-1, per + 1):
                for u in range(per):
                    if abs(d - u) <= 1:
                        at = 256 - 128 * (d - u)
                        strip[j, zero + d * BT : zero + (d + 1) * BT, u * BT : (u + 1) * BT] = near[
                            :, at : at + 128
                        ]
            qaug[j, 0:DH, :] = qkv_ref[0, rows, :]
            kaug[0:DH, :] = qkv_ref[1, rows, :]
            vaug[j, 0:DH, :] = qkv_ref[2, rows, :]
            qaug[j, DH : DH + 16, :] = query_marks(seg, values[:, 511:512], values[:, 1:2])
            kn[j] = kaug[...].T

    lo, n = span[0, q], span[1, q]
    last = 0
    for size in SIZES:

        @pl.when(jnp.logical_and(n > last, n <= size))
        def _():
            attend_block(size, q, lo, base, kn, qaug, vaug, strip, pt_ref, mixed_ref, inv_ref)

        last = size


def project_t(w_refs, yt, qkv_ref):
    for m in range(3):
        qkv_ref[m] = dot_tn(w_refs[m][...], yt).astype(BF16)


def head_setup(seg, tab_ref, table_f, span, kaug, qaug, vaug, strip):
    picks = offset_picks(NB).astype(BF16)
    heads = tab_ref.shape[0]
    table_f[0:heads, :] = dot_nn(tab_ref[...], picks)
    kaug[DH:, :] = jnp.zeros((128 - DH, ROW), BF16)
    qaug[:, DH:, :] = jnp.zeros((GROUP, 128 - DH, ROW), BF16)
    kaug[DH : DH + 16, :] = key_marks(seg)
    vaug[:, DH:, :] = jnp.ones((GROUP, 16, ROW), BF16)
    strip[...] = jnp.zeros(strip.shape, F32)
    for q in range(ROW // QB):
        lowest = jnp.min(seg[:, q * QB : (q + 1) * QB].astype(F32))
        highest = jnp.max(seg[:, q * QB : (q + 1) * QB].astype(F32))
        wide = seg.astype(F32)
        begin = jnp.sum((wide < lowest).astype(F32)).astype(jnp.int32) // BT
        end = (jnp.sum((wide <= highest).astype(F32)).astype(jnp.int32) + BT - 1) // BT
        span[0, q] = begin
        span[1, q] = end - begin


def forward_first(
    seg_ref, tok_ref, prompt_ref, gain_ref, wq, wk, wv, tab_ref,
    start_ref, yt_ref, qkv_ref, pt_ref, mixed_ref, inv_ref,
    table_f, span, kaug, qaug, vaug, kn, strip, padded, start_s, yt_s, qkv_s, sem, w_s, w_sem,
):
    loads = [
        pltpu.make_async_copy(w, w_s.at[m], w_sem.at[m]) for m, w in enumerate((wq, wk, wv))
    ]
    copies = [
        pltpu.make_async_copy(a, b, sem.at[k])
        for k, (a, b) in enumerate(((start_s, start_ref), (yt_s, yt_ref), (qkv_s, qkv_ref)))
    ]
    step, q = pl.program_id(0), pl.program_id(1)
    first = jnp.logical_and(step == 0, q == 0)
    seg = own_row(seg_ref)

    @pl.when(first)
    def _():
        for copy in loads:
            copy.start()
        padded[...] = jnp.zeros(padded.shape, BF16)
        padded[0:PROMPT, :] = prompt_ref[...]
        picks = picks_t(seg)
        looked = dot_tn(picks, padded[...])
        here = dot_tn(picks, (iota((128, 128), 0) < PROMPT).astype(F32).astype(BF16)) > 0.5
        tok = tok_ref[...].astype(F32)
        start = jnp.concatenate(
            [
                jnp.where(here, looked[:, c : c + 128], tok[:, c : c + 128])
                for c in range(0, D, 128)
            ],
            axis=1,
        )
        start_s[...] = start.astype(BF16)
        copies[0].start()
        inv = lax.rsqrt(jnp.mean(start * start, axis=1, keepdims=True) + EPS)
        yt = (start * inv * gain_ref[...][None, :]).astype(BF16).T
        yt_s[...] = yt
        copies[1].start()
        for copy in loads:
            copy.wait()
        project_t([w_s.at[m] for m in range(3)], yt, qkv_s)
        copies[2].start()
        head_setup(seg, tab_ref, table_f, span, kaug, qaug, vaug, strip)

    attend_heads(
        step, q, seg, table_f, span, qkv_s, kaug, qaug, vaug, kn, strip, pt_ref, mixed_ref, inv_ref
    )

    @pl.when(jnp.logical_and(step == pl.num_programs(0) - 1, q == pl.num_programs(1) - 1))
    def _():
        for copy in copies:
            copy.wait()


def forward_second(
    seg_ref, start_ref, yt_ref, gain_ref, wq, wk, wv, tab_ref, mixed_own, wo_own, wo_oth,
    qkv_ref, pt_ref, mixed_ref, inv_ref, middle_ref, x_ref, xt_ref,
    table_f, span, kaug, qaug, vaug, kn, strip, qkv_s, middle_s, x_s, xt_s, sem,
    w_s, yt_s, start_s, mixed_s, wo_s, w_sem,
):
    pairs = [(w, w_s.at[m]) for m, w in enumerate((wq, wk, wv))]
    pairs += [
        (yt_ref, yt_s), (start_ref, start_s), (mixed_own, mixed_s), (wo_own, wo_s.at[0]),
        (wo_oth, wo_s.at[1]),
    ]
    loads = [pltpu.make_async_copy(a, b, w_sem.at[k]) for k, (a, b) in enumerate(pairs)]
    qkv_copy = pltpu.make_async_copy(qkv_s, qkv_ref, sem.at[0])
    step, q = pl.program_id(0), pl.program_id(1)
    first = jnp.logical_and(step == 0, q == 0)
    seg = own_row(seg_ref)

    @pl.when(first)
    def _():
        for copy in loads:
            copy.start()
        head_setup(seg, tab_ref, table_f, span, kaug, qaug, vaug, strip)
        for copy in loads[:4]:
            copy.wait()
        project_t([w_s.at[m] for m in range(3)], yt_s[...], qkv_s)
        qkv_copy.start()

    attend_heads(
        step, q, seg, table_f, span, qkv_s, kaug, qaug, vaug, kn, strip, pt_ref, mixed_ref, inv_ref
    )

    @pl.when(jnp.logical_and(step == pl.num_programs(0) - 1, q == pl.num_programs(1) - 1))
    def _():
        for copy in loads[4:]:
            copy.wait()
        copies = []
        for k in range(0, ROW, QB):
            r = slice(k, k + QB)
            attn = dot_tn(mixed_s[:, r], wo_s[0]) + dot_tn(mixed_ref[:, r], wo_s[1])
            middle = start_s[r, :].astype(F32) + attn
            middle_s[r, :] = middle
            inv = lax.rsqrt(jnp.mean(middle * middle, axis=1, keepdims=True) + EPS)
            x = (middle * inv * gain_ref[...][None, :]).astype(BF16)
            x_s[r, :] = x
            xt_s[:, r] = x.T
            for src, dst in ((middle_s, middle_ref), (x_s, x_ref)):
                copies.append((src.at[r, :], dst.at[r, :]))
            copies.append((xt_s.at[:, r], xt_ref.at[:, r]))
            for m in range(3):
                at = 3 * (k // QB) + m
                pltpu.make_async_copy(*copies[at], sem.at[1 + at]).start()
        qkv_copy.wait()
        for at, pair in enumerate(copies):
            pltpu.make_async_copy(*pair, sem.at[1 + at]).wait()


def plan_stages(n_rows):
    n_bits = n_rows.bit_length() - 1
    size, slot = UNIT, 0
    stages, halved = [], []
    for j in range(n_bits):
        if j < n_bits - 1 and size % 32 == 0:
            size = size // 2
            halved.append((j, size))
            stages.append(("halve", j, size, slot))
        else:
            stages.append(("swap", j, size, slot))
        slot += size
    for j, n in reversed(halved):
        stages.append(("gather", j, n, slot))
        slot += n
    return stages, len(halved), slot


def stage_table(n_rows):
    stages, n_halved, _ = plan_stages(n_rows)
    n_bits = n_rows.bit_length() - 1
    me = lax.axis_index("rows")
    bits = [(me // (1 << b)) % 2 for b in range(n_bits)]
    peers = [me + (1 - 2 * bits[b]) * (1 << b) for b in range(n_bits)]
    rest = list(range(3, n_bits))
    sides = []
    for order in ([0, 2, 1] + rest, [1, 2, 0] + rest):
        bases, base, size = [], 0, UNIT
        for j in range(n_bits):
            bases.append(base)
            if j < n_halved:
                size = size // 2
                base = base + bits[order[j]] * size
        side = []
        for kind, j, n, _ in stages:
            keep = bases[j] + bits[order[j]] * n
            give = bases[j] + (1 - bits[order[j]]) * n
            src, dst = {
                "halve": (give, keep), "swap": (bases[j], bases[j]), "gather": (keep, give)
            }[kind]
            side.append((src, dst, peers[order[j]]))
        sides.append(side)
    table = [(kind, n, slot, sides[0][k], sides[1][k]) for k, (kind, _, n, slot) in enumerate(stages)]
    return table, peers


def whole(shape):
    n = len(shape)
    return pl.BlockSpec(shape, lambda *_: (0,) * n, pipeline_mode=pl.Buffered(1))


def whole_out(shape):
    n = len(shape)
    return pl.BlockSpec(shape, lambda *_: (0,) * n)


def sds(shape, dtype):
    return jax.ShapeDtypeStruct(shape, dtype)


def forward_scratch():
    return [
        pltpu.VMEM((8, 512), F32),
        pltpu.SMEM((2, ROW // QB), jnp.int32),
        pltpu.VMEM((128, ROW), BF16),
        pltpu.VMEM((GROUP, 128, ROW), BF16),
        pltpu.VMEM((GROUP, DH + 16, ROW), BF16),
        pltpu.VMEM((GROUP, ROW, 128), BF16),
        pltpu.VMEM((GROUP, 2 * ROW, QB), F32),
    ]


PARAMS = dict(vmem_limit_bytes=56 * 1024 * 1024)


def run_first(seg, tok, prompt, gain, wq, wk, wv, tab):
    cols = wq.shape[1]
    heads = cols // DH
    return pl.pallas_call(
        forward_first,
        grid=(heads // GROUP, ROW // QB),
        in_specs=[whole(a.shape) for a in (seg, tok, prompt, gain)]
        + [pl.BlockSpec(memory_space=pl.ANY)] * 3
        + [whole(tab.shape)],
        out_specs=[
            pl.BlockSpec(memory_space=pl.ANY),
            pl.BlockSpec(memory_space=pl.ANY),
            pl.BlockSpec(memory_space=pl.ANY),
            pl.BlockSpec((GROUP, ROW, QB), lambda h, q: (h, 0, q)),
            whole_out((cols, ROW)),
            whole_out((8, ROW)),
        ],
        out_shape=[
            sds((ROW, D), BF16),
            sds((D, ROW), BF16),
            sds((3, cols, ROW), BF16),
            sds((heads, ROW, ROW), BF16),
            sds((cols, ROW), BF16),
            sds((8, ROW), F32),
        ],
        scratch_shapes=forward_scratch() + [
            pltpu.VMEM((128, D), BF16),
            pltpu.VMEM((ROW, D), BF16),
            pltpu.VMEM((D, ROW), BF16),
            pltpu.VMEM((3, cols, ROW), BF16),
            pltpu.SemaphoreType.DMA((3,)),
            pltpu.VMEM((3, D, cols), BF16),
            pltpu.SemaphoreType.DMA((3,)),
        ],
        compiler_params=pltpu.CompilerParams(**PARAMS),
        cost_estimate=pl.CostEstimate(flops=2 * 10**10, bytes_accessed=10**7, transcendentals=0),
        name="attend_own",
    )(seg, tok, prompt, gain, wq, wk, wv, tab)


def run_second(seg, start, yt, gain, wq, wk, wv, tab, mixed_own, wo_own, wo_oth):
    cols = wq.shape[1]
    heads = cols // DH
    ins = (seg, start, yt, gain, wq, wk, wv, tab, mixed_own, wo_own, wo_oth)
    return pl.pallas_call(
        forward_second,
        grid=(heads // GROUP, ROW // QB),
        in_specs=[
            whole(a.shape) if a is seg or a is gain or a is tab else pl.BlockSpec(memory_space=pl.ANY)
            for a in ins
        ],
        out_specs=[
            pl.BlockSpec(memory_space=pl.ANY),
            pl.BlockSpec((GROUP, ROW, QB), lambda h, q: (h, 0, q)),
            whole_out((cols, ROW)),
            whole_out((8, ROW)),
            pl.BlockSpec(memory_space=pl.ANY),
            pl.BlockSpec(memory_space=pl.ANY),
            pl.BlockSpec(memory_space=pl.ANY),
        ],
        out_shape=[
            sds((3, cols, ROW), BF16),
            sds((heads, ROW, ROW), BF16),
            sds((cols, ROW), BF16),
            sds((8, ROW), F32),
            sds((ROW, D), F32),
            sds((ROW, D), BF16),
            sds((D, ROW), BF16),
        ],
        scratch_shapes=forward_scratch() + [
            pltpu.VMEM((3, cols, ROW), BF16),
            pltpu.VMEM((ROW, D), F32),
            pltpu.VMEM((ROW, D), BF16),
            pltpu.VMEM((D, ROW), BF16),
            pltpu.SemaphoreType.DMA((1 + 3 * (ROW // QB),)),
            pltpu.VMEM((3, D, cols), BF16),
            pltpu.VMEM((D, ROW), BF16),
            pltpu.VMEM((ROW, D), BF16),
            pltpu.VMEM((cols, ROW), BF16),
            pltpu.VMEM((2, cols, D), BF16),
            pltpu.SemaphoreType.DMA((8,)),
        ],
        compiler_params=pltpu.CompilerParams(**PARAMS),
        cost_estimate=pl.CostEstimate(flops=2 * 10**10, bytes_accessed=10**7, transcendentals=0),
        name="attend_other",
    )(*ins)


def norm_back(value, gain, grad):
    inv = lax.rsqrt(jnp.mean(value * value, axis=1, keepdims=True) + EPS)
    scaled = grad * gain
    inner = jnp.mean(scaled * value, axis=1, keepdims=True)
    back = inv * scaled - value * (inv * inv * inv * inner)
    return back, jnp.sum(grad * (value * inv), axis=0, keepdims=True)


def backward(
    n_ff, n_heads, n_rows,
    seg_ref, gain_a_ref, gain_f_ref, win_own, win_oth, wout_own, wout_oth, pt_own, pt_oth,
    x_hbm, xt_hbm, og_hbm, mid_hbm, start_hbm, yt_hbm, qkv_own_hbm, qkv_oth_hbm,
    mix_own_hbm, mix_oth_hbm, inv_own_hbm, inv_oth_hbm, wq_own_hbm, wk_own_hbm, wv_own_hbm, wq_oth_hbm, wk_oth_hbm,
    wv_oth_hbm, wo_own_hbm, wo_oth_hbm,
    result_hbm, gtok_hbm, out_in, out_out, out_q, out_k, out_v, out_o, out_small,
    x, xt, og, mid, qkv, mix, inv, gmix, wqkv, wo, feed, gnf, dst, dqkv, kaug, vaug, doaug,
    tacc, gvec, gains, ptb, g, xsend, xrecv, ring, load_sem, late_sem, pt_sem, out_sem, xs_sem, xr_sem,
    send_sem, recv_sem,
):
    s = pl.program_id(0)
    heads_half = n_heads // 2
    cols = heads_half * DH
    me = lax.axis_index("heads")
    early = [(x_hbm, x), (xt_hbm, xt), (og_hbm, og)]
    later = [
        (mid_hbm, mid),
        (qkv_own_hbm, qkv.at[0]),
        (qkv_oth_hbm, qkv.at[1]),
        (mix_own_hbm, mix.at[0]),
        (mix_oth_hbm, mix.at[1]),
        (inv_own_hbm, inv.at[0]),
        (inv_oth_hbm, inv.at[1]),
        (wq_own_hbm, wqkv.at[0, 0]),
        (wk_own_hbm, wqkv.at[0, 1]),
        (wv_own_hbm, wqkv.at[0, 2]),
        (wq_oth_hbm, wqkv.at[1, 0]),
        (wk_oth_hbm, wqkv.at[1, 1]),
        (wv_oth_hbm, wqkv.at[1, 2]),
        (wo_own_hbm, wo.at[0]),
        (wo_oth_hbm, wo.at[1]),
    ]
    n_early = len(early)
    loads = [
        pltpu.make_async_copy(a, b, load_sem.at[i]) for i, (a, b) in enumerate(early + later)
    ]
    late = [
        pltpu.make_async_copy(start_hbm, x, late_sem.at[0]),
        pltpu.make_async_copy(yt_hbm, xt, late_sem.at[1]),
    ]

    def pt_start(i):
        hh = 2 * (i // 4) + i % 2
        for o, ref in enumerate((pt_own, pt_oth)):

            @pl.when((i % 4) // 2 == o)
            def _():
                pltpu.make_async_copy(ref.at[hh], ptb.at[i % 2], pt_sem.at[i % 2]).start()

    n_out = cols // 128
    n_chunks = 2 * n_ff + 4 * n_out + 1
    n_units = n_chunks
    table, peers = stage_table(n_rows)
    n_stages = len(table)
    core = {"heads": 1 - me}

    def swap(slot):
        return pltpu.make_async_remote_copy(
            src_ref=xsend.at[slot],
            dst_ref=xrecv.at[slot],
            send_sem=xs_sem.at[slot],
            recv_sem=xr_sem.at[slot],
            device_id=core,
            device_id_type=pl.DeviceIdType.MESH,
        )

    def emit(c, slot, own, oth):
        for blocks, ref in ((own, g.at[c]), (oth, xsend.at[slot])):
            for b, block in enumerate(blocks):
                n = block.shape[0]
                ref[b * n : (b + 1) * n, :] = block.astype(BF16)
        swap(slot).start()

    def collect(c, slot):
        swap(slot).wait()
        g[c] = (g[c].astype(F32) + xrecv[slot].astype(F32)).astype(BF16)

    def stage_copy(k, c, par, odd):
        kind, n, slot, even_side, odd_side = table[k]
        src, dst, peer = (p + odd * (q - p) for p, q in zip(even_side, odd_side))
        copy = pltpu.make_async_remote_copy(
            src_ref=g.at[c, pl.ds(pl.multiple_of(src, 16), n), :],
            dst_ref=ring.at[par, slot : slot + n, :],
            send_sem=send_sem.at[k, par],
            recv_sem=recv_sem.at[k, par],
            device_id={"rows": peer},
            device_id_type=pl.DeviceIdType.MESH,
        )
        return copy, pl.ds(pl.multiple_of(dst, 16), n)

    def stage_end(k, c, par, odd):
        kind, n, slot = table[k][:3]
        copy, dst = stage_copy(k, c, par, odd)
        copy.wait()
        part = ring[par, slot : slot + n, :]
        if kind != "gather":
            part = (g[c, dst, :].astype(F32) + part.astype(F32)).astype(BF16)
        g[c, dst, :] = part

    def out_wait(par):
        pltpu.make_async_copy(g.at[0], out_in.at[:, 0:128], out_sem.at[par]).wait()

    def out_start(c, odd):
        sem = out_sem.at[odd]

        @pl.when(c >= 2)
        def _():
            out_wait(odd)

        def wide(ref, col):
            dst = ref.at[:, pl.ds(pl.multiple_of(col * 128, 128), 128)]
            pltpu.make_async_copy(g.at[c], dst, sem).start()

        def tall(ref, row):
            pltpu.make_async_copy(g.at[c], ref.at[row], sem).start()

        base = 2 * n_ff + n_out

        @pl.when(jnp.logical_and(c < 2 * n_ff, odd == 0))
        def _():
            wide(out_in, c // 2)

        @pl.when(jnp.logical_and(c < 2 * n_ff, odd == 1))
        def _():
            tall(out_out, c // 2)

        @pl.when(c >= 2 * n_ff)
        def _():
            @pl.when(c < base)
            def _():
                tall(out_o, c - 2 * n_ff)

            for m, ref in enumerate((out_q, out_k, out_v)):
                at = jnp.logical_and(c >= base, c < n_chunks - 1)

                @pl.when(jnp.logical_and(at, (c - base) % 3 == m))
                def _():
                    wide(ref, (c - base) // 3)

            @pl.when(c == n_chunks - 1)
            def _():
                tall(out_small, 0)

    wo_end = 2 * n_ff + n_out
    holes = ((wo_end, 2), (wo_end + 5, 1))

    def tick(t):
        turn = lax.rem(t, SLOTS)
        parity = lax.rem(t, 2)
        for k in range(n_stages, -1, -1):
            v = t - SPACING * k
            c = v
            live_unit = v >= 0
            for at, length in holes:
                c = c - jnp.where(v >= at + length, length, 0)
                live_unit = jnp.logical_and(live_unit, jnp.logical_or(v < at, v >= at + length))
            par = turn + (-SPACING * k) % SLOTS
            par = par - jnp.where(par >= SLOTS, SLOTS, 0)
            odd = parity if SPACING * k % 2 == 0 else 1 - parity

            def step(k=k, c=c, par=par, odd=odd):
                if k > 0:
                    stage_end(k - 1, c, par, odd)
                if k < n_stages:
                    stage_copy(k, c, par, odd)[0].start()
                else:
                    out_start(c, odd)

            pl.when(jnp.logical_and(live_unit, c < n_units))(step)

    def collect_ff(e):
        for j in range(2):
            collect(2 * e + j, 2 * (e % 4) + j)

    def group_slot(e, m):
        return 3 + m if e % 2 == 0 else m

    def collect_group(e):
        for m in range(3):
            collect((2 * n_ff + n_out + 3 * e + m), group_slot(e, m))

    def lanes(a):
        return [a[:, k : k + 128] for k in range(0, a.shape[1], 128)]

    @pl.when(s == 0)
    def _():
        for copy in loads:
            copy.start()
        barrier = pltpu.get_barrier_semaphore()
        for peer in [{"rows": p} for p in peers] + [core]:
            pl.semaphore_signal(
                barrier, inc=1, device_id=peer, device_id_type=pl.DeviceIdType.MESH
            )
        pl.semaphore_wait(barrier, len(peers) + 1)
        feed[...] = jnp.zeros(feed.shape, F32)
        gnf[...] = jnp.zeros(gnf.shape, F32)
        for copy in loads[:n_early]:
            copy.wait()

    @pl.when(s < n_ff)
    def _():
        wi = jnp.concatenate([win_own[...], win_oth[...]], axis=1)
        wout = jnp.concatenate([wout_own[...], wout_oth[...]], axis=0)
        halves = [slice(0, ROW // 2), slice(ROW // 2, ROW)]
        pres = [dot_nn(x[r, :], wi) for r in halves]
        gacts = [dot_nt(og[r, :], wout) for r in halves]
        acts, gpres = [], []
        for pre, gact in zip(pres, gacts):
            cdf = 0.5 * (1.0 + lax.erf(pre * ROOT_HALF))
            acts.append((pre * cdf).astype(BF16))
            slope = cdf + pre * jnp.exp(-0.5 * pre * pre) * DENSITY
            gpres.append((gact * slope).astype(BF16))
        for r, act, gpre in zip(halves, acts, gpres):
            feed[r, :] += dot_nn(act, wout)
            gnf[r, :] += dot_nt(gpre, wi)
        active = jnp.concatenate(acts, axis=0)
        gpre = jnp.concatenate(gpres, axis=0)

        @pl.when(s >= 1)
        def _():
            collect_ff(s - 1)
            tick(2 * (s - 1))

        dwin = dot_nn(xt[...], gpre)
        dwout = dot_tn(active, og[...])

        emit(2 * s, 2 * (s % 4), [dwin[:, :FFC]], [dwin[:, FFC:]])
        emit(2 * s + 1, 2 * (s % 4) + 1, lanes(dwout[:FFC]), lanes(dwout[FFC:]))

        @pl.when(s >= 1)
        def _():
            tick(2 * (s - 1) + 1)

    @pl.when(s == n_ff)
    def _():
        for copy in late:
            copy.start()
        pt_start(0)
        for copy in loads[n_early:]:
            copy.wait()
        t0 = 2 * (n_ff - 2)
        middle = mid[...]
        dst[:, 0:D] = (middle + feed[...]).astype(BF16)
        to_result = pltpu.make_async_copy(dst.at[:, 0:D], result_hbm, late_sem.at[2])
        to_result.start()
        back, gain_grad = norm_back(middle, gain_f_ref[...][None, :], gnf[...])
        gmid = og[...].astype(F32) + back
        gains[0:1, :] = gain_grad
        mid[...] = gmid
        ga = gmid.astype(BF16)
        dwo = [dot_nn(mix[o], ga) for o in range(2)]
        collect_ff(n_ff - 1)
        for j in range(n_out):
            rows = slice(j * 128, (j + 1) * 128)
            emit((2 * n_ff + j), j, lanes(dwo[0][rows]), lanes(dwo[1][rows]))
        for o in range(2):
            grad = dot_nt(wo[o], ga)
            for k in range(heads_half):
                rows = slice(k * DH, (k + 1) * DH)
                gmix[o, rows, :] = (grad[rows] * inv[o, k : k + 1, :]).astype(BF16)
        tick(t0 + 2)
        gnf[...] = jnp.zeros(gnf.shape, F32)
        kaug[DH:, :] = key_marks(own_row(seg_ref))
        vaug[DH:, :] = (iota((16, ROW), 0) < 3).astype(F32).astype(BF16)
        gvec[...] = jnp.zeros(gvec.shape, F32)
        to_result.wait()
        dst[...] = jnp.zeros(dst.shape, BF16)
        for copy in late:
            copy.wait()
        tick(t0 + 3)

    i = s - (n_ff + 1)

    def head_back(o, pt_ref):
        hh = 2 * (i // 4) + i % 2
        rows = pl.ds(pl.multiple_of(hh * DH, DH), DH)
        dot_ = gmix[o, rows, :]
        delta = jnp.sum(dot_.astype(F32) * mix[o, rows, :].astype(F32), axis=0, keepdims=True)
        d1 = delta.astype(BF16).astype(F32)
        d2 = (delta - d1).astype(BF16).astype(F32)
        d3 = delta - d1 - d2
        k = iota((16, ROW), 0)
        vaug[0:DH, :] = qkv[o, 2, rows, :]
        kaug[0:DH, :] = qkv[o, 1, rows, :]
        doaug[0:DH, :] = dot_
        doaug[DH:, :] = jnp.where(
            k == 0, -d1, jnp.where(k == 1, -d2, jnp.where(k == 2, -d3, 0.0))
        ).astype(BF16)
        va = vaug[...]
        ka = kaug[...]
        out_rows = pl.ds(pl.multiple_of(o * 128 + (i % 2) * DH, DH), DH)
        tacc[...] = jnp.zeros(tacc.shape, F32)
        left = jnp.zeros((1, QB), F32)
        right = jnp.zeros((1, QB), F32)
        n_blocks = ROW // QB

        def live(b):
            ks = [
                kb for kb in range(NBLK)
                if max(kb * BT - (b + 1) * QB, b * QB - (kb + 1) * BT) + 1 < LONGEST
            ]
            return slice(ks[0] * BT, (ks[-1] + 1) * BT)

        def grad_probs(b):
            return dot_tn(va[:, live(b)], doaug[:, b * QB : (b + 1) * QB])

        dp = grad_probs(0)
        dqkv[2, out_rows, :] = dot_nt(dot_, pt_ref[...]).astype(BF16)
        for b in range(n_blocks):
            qs = slice(b * QB, (b + 1) * QB)
            ahead = grad_probs(b + 1) if b + 1 < n_blocks else None
            ks = live(b)
            ds = pt_ref[ks, qs].astype(F32) * dp
            for u in range(QB // BT):
                qb = b * (QB // BT) + u
                for d in (-1, 0, 1):
                    kb = qb + d
                    if 0 <= kb < NBLK:
                        at = kb * BT - ks.start
                        tacc[:, 256 - 128 * d : 384 - 128 * d] += ds[
                            at : at + BT, u * BT : (u + 1) * BT
                        ]
            dst[ks, qs] = ds.astype(BF16)
            dp = ahead
        for b in range(n_blocks):
            qs = slice(b * QB, (b + 1) * QB)
            r = dot_nn(ka[:, live(b)], dst[live(b), qs])
            dqkv[0, out_rows, qs] = r[:DH].astype(BF16)
            sums = r[DH + 8 :]
            j = iota((8, QB), 0)
            block = b * (QB // BT) + iota((8, QB), 1) // BT
            left = left + jnp.sum(jnp.where(j <= block - 2, sums, 0.0), axis=0, keepdims=True)
            right = right + jnp.sum(jnp.where(j >= block + 2, sums, 0.0), axis=0, keepdims=True)
        dqkv[1, out_rows, :] = dot_nt(qkv[o, 0, rows, :], dst[...]).astype(BF16)
        flip = (iota((BT, BT), 0) + iota((BT, BT), 1) == BT - 1).astype(F32).astype(BF16)
        near = tacc[...]
        high = near.astype(BF16)
        low = (near - high.astype(F32)).astype(BF16)
        turned = dot_nn(flip, high) + dot_nn(flip, low)
        skew = pltpu.roll(turned, 0, 1, stride=1, stride_axis=0)
        vec = pltpu.roll(jnp.sum(skew, axis=0, keepdims=True), 512 - (BT - 1), 1)
        lane = iota((1, 512), 1)
        vec = vec + jnp.where(lane == 511, jnp.sum(left, axis=1, keepdims=True), 0.0)
        vec = vec + jnp.where(lane == 1, jnp.sum(right, axis=1, keepdims=True), 0.0)
        owner = me + o * (1 - 2 * me)
        gvec[pl.ds(owner * heads_half + hh, 1), :] = vec

    in_heads = jnp.logical_and(i >= 0, i < n_heads)

    @pl.when(in_heads)
    def _():
        @pl.when(i + 1 < n_heads)
        def _():
            pt_start(i + 1)

        pltpu.make_async_copy(pt_own.at[0], ptb.at[i % 2], pt_sem.at[i % 2]).wait()
        head_back((i % 4) // 2, ptb.at[i % 2])

        @pl.when(i == 0)
        def _():
            for j in range(n_out):
                collect((2 * n_ff + j), j)

        for e in range(n_heads // 4 - 1):

            @pl.when(i == 4 * (e + 1) + 1)
            def _():
                collect_group(e)

        tick(2 * n_ff + i)

    def group_back(grp):
        for m in range(3):
            dw = dot_nt(xt[...], dqkv[m])
            emit(
                2 * n_ff + n_out + 3 * grp + m, group_slot(grp, m),
                [dw[:, :128]], [dw[:, 128:]],
            )
        cols_g = slice(grp * 128, (grp + 1) * 128)
        for m in range(3):
            w = jnp.concatenate([wqkv[0, m, :, cols_g], wqkv[1, m, :, cols_g]], axis=1)
            gnf[...] += lax.dot_general(
                dqkv[m], w, (((0,), (1,)), ((), ())), preferred_element_type=F32
            )

    for grp in range(n_heads // 4):

        @pl.when(i == 4 * grp + 3)
        def _():
            group_back(grp)

    @pl.when(i == n_heads)
    def _():
        seg = own_row(seg_ref)
        start = x[...].astype(F32)
        back, gain_grad = norm_back(start, gain_a_ref[...][None, :], gnf[...])
        gstart = mid[...] + back
        n_groups = n_heads // 4
        collect_group(n_groups - 1)
        t0 = 2 * n_ff + n_heads
        tick(t0)
        picks = picks_t(seg)
        here = dot_tn(picks, (iota((128, 128), 0) < PROMPT).astype(F32).astype(BF16)) > 0.5
        for c in range(0, D, 128):
            og[:, c : c + 128] = jnp.where(here, 0.0, gstart[:, c : c + 128]).astype(BF16)
        to_gtok = pltpu.make_async_copy(og, gtok_hbm, late_sem.at[0])
        to_gtok.start()
        high = gstart.astype(BF16)
        low = (gstart - high.astype(F32)).astype(BF16)
        tick(t0 + 1)
        gprompt = dot_nn(picks, high) + dot_nn(picks, low)
        opicks = offset_picks(128).astype(BF16)
        gv = gvec[...]
        g1 = gv.astype(BF16)
        g2 = (gv - g1.astype(F32)).astype(BF16)
        gtab = dot_nt(g1, opicks) + dot_nt(g2, opicks)
        row = iota((128, D), 0)
        small = jnp.where(row < PROMPT, gprompt, 0.0)
        small = jnp.where(row == PROMPT, gain_grad, small)
        small = jnp.where(row == PROMPT + 1, gains[0:1, :], small)
        blocks = lanes(small)
        wide = jnp.concatenate([jnp.zeros((104, 128), F32), gtab, jnp.zeros((8, 128), F32)], axis=0)
        blocks[0] = blocks[0] + wide
        slot = group_slot(n_groups, 0)
        emit((n_chunks - 1), slot, blocks, blocks)
        tick(t0 + 2)
        collect((n_chunks - 1), slot)

        @pl.loop(t0 + 3, n_units + sum(h[1] for h in holes) + SPACING * n_stages)
        def _(t):
            tick(t)

        to_gtok.wait()
        out_wait(0)
        out_wait(1)


def run_backward(
    n_rows, seg, gain_a, gain_f, win_own, win_oth, wout_own, wout_oth, pt_own, pt_oth, rest
):
    n_ff = win_own.shape[1] // FFC
    n_heads = 2 * pt_own.shape[0]
    cols = n_heads * DH // 2
    n_chunks = 2 * n_ff + 4 * (cols // 128) + 1
    first = n_ff + 1
    stages, _, ring_rows = plan_stages(n_rows)
    n_stages = len(stages)

    def ff(s):
        return jnp.minimum(s, n_ff - 1)

    blk_in = pl.BlockSpec((D, FFC), lambda s: (0, ff(s)))
    blk_out = pl.BlockSpec((FFC, D), lambda s: (ff(s), 0))
    anyspec = pl.BlockSpec(memory_space=pl.ANY)
    return pl.pallas_call(
        partial(backward, n_ff, n_heads, n_rows),
        grid=(first + n_heads + 1,),
        in_specs=[
            whole(seg.shape), whole(gain_a.shape), whole(gain_f.shape),
            blk_in, blk_in, blk_out, blk_out,
        ] + [anyspec] * (2 + len(rest)),
        out_specs=[anyspec] * 9,
        out_shape=[sds((ROW, D), BF16), sds((ROW, D), BF16)] + [
            sds(shape, BF16)
            for shape in (win_own.shape, (n_ff, CH, 128))
            + ((D, cols),) * 3 + ((cols // 128, CH, 128), (1, CH, 128))
        ],
        scratch_shapes=[
            pltpu.VMEM((ROW, D), BF16),
            pltpu.VMEM((D, ROW), BF16),
            pltpu.VMEM((ROW, D), BF16),
            pltpu.VMEM((ROW, D), F32),
            pltpu.VMEM((2, 3, cols, ROW), BF16),
            pltpu.VMEM((2, cols, ROW), BF16),
            pltpu.VMEM((2, 8, ROW), F32),
            pltpu.VMEM((2, cols, ROW), BF16),
            pltpu.VMEM((2, 3, D, cols), BF16),
            pltpu.VMEM((2, cols, D), BF16),
            pltpu.VMEM((ROW, D), F32),
            pltpu.VMEM((ROW, D), F32),
            pltpu.VMEM((ROW, ROW), BF16),
            pltpu.VMEM((3, 256, ROW), BF16),
            pltpu.VMEM((DH + 16, ROW), BF16),
            pltpu.VMEM((DH + 16, ROW), BF16),
            pltpu.VMEM((DH + 16, ROW), BF16),
            pltpu.VMEM((BT, 512), F32),
            pltpu.VMEM((16, 512), F32),
            pltpu.VMEM((8, D), F32),
            pltpu.VMEM((2, ROW, ROW), BF16),
            pltpu.VMEM((n_chunks, UNIT, 128), BF16),
            pltpu.VMEM((8, CH, 128), BF16),
            pltpu.VMEM((8, CH, 128), BF16),
            pltpu.VMEM((SLOTS, ring_rows, 128), BF16),
            pltpu.SemaphoreType.DMA((18,)),
            pltpu.SemaphoreType.DMA((3,)),
            pltpu.SemaphoreType.DMA((2,)),
            pltpu.SemaphoreType.DMA((2,)),
            pltpu.SemaphoreType.DMA((8,)),
            pltpu.SemaphoreType.DMA((8,)),
            pltpu.SemaphoreType.DMA((n_stages, SLOTS)),
            pltpu.SemaphoreType.DMA((n_stages, SLOTS)),
        ],
        compiler_params=pltpu.CompilerParams(
            vmem_limit_bytes=62 * 1024 * 1024, collective_id=0, has_side_effects=True
        ),
        name="backward",
    )(seg, gain_a, gain_f, win_own, win_oth, wout_own, wout_oth, pt_own, pt_oth, *rest)


def untile(src, dst):
    for c in range(src.shape[0]):
        for b in range(D // 128):
            dst[c * 128 : (c + 1) * 128, b * 128 : (b + 1) * 128] = src[
                c, b * 128 : (b + 1) * 128, :
            ].astype(F32)


def finish(
    heads, result, gtok, small, g_q, g_k, g_v, g_wo, g_in, g_out,
    o_result, o_gtok, o_prompt, o_gain_a, o_q, o_k, o_v, o_wo, o_tab, o_gain_f, o_in, o_out, rows,
):
    o_result[...] = result[...]
    o_gtok[...] = gtok[...]
    for src, dst in ((g_q, o_q), (g_k, o_k), (g_v, o_v), (g_in, o_in)):
        dst[...] = src[...].astype(F32)
    untile(g_out, o_out)

    @pl.when(pl.program_id(0) == 0)
    def _():
        untile(small, rows)
        untile(g_wo, o_wo)
        o_prompt[...] = rows[0:PROMPT, :]
        o_gain_a[...] = rows[PROMPT, :]
        o_gain_f[...] = rows[PROMPT + 1, :]
        low = lax.axis_index("heads") == 0
        at = 104
        tab = [
            jnp.where(low, rows[at + k : at + k + 1, 0:128], rows[at + heads + k : at + heads + k + 1, 0:128])
            for k in range(heads)
        ]
        tab.append(jnp.zeros((8 - heads, 128), F32))
        o_tab[...] = jnp.concatenate(tab, axis=0)[0:heads, 0:NB]


def run_finish(heads, result, gtok, small, *grads):
    steps = 2

    def part(shape):
        zeros = (0,) * (len(shape) - 1)
        return pl.BlockSpec((shape[0] // steps,) + shape[1:], lambda i: (i,) + zeros)

    g_q, g_k, g_v, g_wo, g_in, g_out = grads
    wo_shape, out_shape = ((a.shape[0] * 128, D) for a in (g_wo, g_out))
    whole_1d = pl.BlockSpec((D,), lambda i: (0,))
    return pl.pallas_call(
        partial(finish, heads),
        grid=(steps,),
        in_specs=[part(result.shape), part(gtok.shape), whole(small.shape)]
        + [part(a.shape) for a in (g_q, g_k, g_v)]
        + [whole(g_wo.shape), part(g_in.shape), part(g_out.shape)],
        out_specs=[part(result.shape), part(gtok.shape), whole_out((PROMPT, D)), whole_1d]
        + [part(a.shape) for a in (g_q, g_k, g_v)]
        + [whole_out(wo_shape), whole_out((heads, NB)), whole_1d, part(g_in.shape), part(out_shape)],
        out_shape=[sds(result.shape, BF16), sds(gtok.shape, BF16), sds((PROMPT, D), F32), sds((D,), F32)]
        + [sds(a.shape, F32) for a in (g_q, g_k, g_v)]
        + [sds(wo_shape, F32), sds((heads, NB), F32), sds((D,), F32)]
        + [sds(g_in.shape, F32), sds(out_shape, F32)],
        scratch_shapes=[pltpu.VMEM((128, D), F32)],
        compiler_params=pltpu.CompilerParams(vmem_limit_bytes=62 * 1024 * 1024),
        name="finish",
    )(result, gtok, small, *grads)


def on_device(
    tokens, prompt, segment_ids, gain_attn, w_query, w_key, w_value, w_attn_out, bias_table,
    gain_ff, w_in, w_out, out_grad,
):
    seg = segment_ids
    swap = [(0, 1), (1, 0)]

    def other(a):
        return lax.ppermute(a, "heads", swap)

    tab_oth, wq_oth, wk_oth, wv_oth = (other(a) for a in (bias_table.T, w_query, w_key, w_value))
    wo_oth, win_oth, wout_oth = other(w_attn_out), other(w_in), other(w_out)
    gain_a, gain_f = gain_attn, gain_ff
    start, yt, qkv_own, pt_own, mix_own, inv_own = run_first(
        seg, tokens, prompt, gain_a, w_query, w_key, w_value, bias_table.T
    )
    qkv_oth, pt_oth, mix_oth, inv_oth, middle, x, xt = run_second(
        seg, start, yt, gain_f, wq_oth, wk_oth, wv_oth, tab_oth, mix_own, w_attn_out, wo_oth
    )
    result, gtok, g_in, g_out, g_q, g_k, g_v, g_wo, small = run_backward(
        lax.axis_size("rows"),
        seg, gain_a, gain_f, w_in, win_oth, w_out, wout_oth, pt_own, pt_oth,
        [x, xt, out_grad, middle, start, yt, qkv_own, qkv_oth, mix_own, mix_oth,
         inv_own, inv_oth,
         w_query, w_key, w_value, wq_oth, wk_oth, wv_oth, w_attn_out, wo_oth],
    )
    (
        result, gtok, g_prompt, g_gain_a, g_q, g_k, g_v, g_wo, g_tab, g_gain_f, g_in, g_out,
    ) = run_finish(bias_table.shape[1], result, gtok, small, g_q, g_k, g_v, g_wo, g_in, g_out)
    return (
        result, gtok, g_prompt, g_gain_a, g_q, g_k, g_v, g_wo, g_tab.T, g_gain_f, g_in, g_out,
    )


def solution(mesh):
    both = P(("rows", "heads"), None)
    cols = P(None, "heads")
    rows = P("heads", None)
    in_specs = (
        both, P(), P("rows", None), P(), cols, cols, cols, rows, cols, P(), cols, rows, both,
    )
    out_specs = (both, both, P(), P(), cols, cols, cols, rows, cols, P(), cols, rows)
    return jax.shard_map(
        on_device, mesh=mesh, in_specs=in_specs, out_specs=out_specs, check_vma=False
    )
```

```python
from functools import partial
import math

import jax
import jax.numpy as jnp
from jax import lax
from jax.experimental import pallas as pl
from jax.experimental.pallas import tpu as pltpu
from jax.sharding import PartitionSpec as P

D = 768
DH = 64
NB = 32
ROW = 1024
PROMPT = 100
BIG = 1e30
EDGES = (12, 16, 23, 32, 46, 64, 91)
EPS = 1e-06
ROOT_HALF = 1.0 / math.sqrt(2.0)
DENSITY = 1.0 / math.sqrt(2.0 * math.pi)
F32 = jnp.float32
BF16 = jnp.bfloat16
FFC = 128
CH = 768
UNIT = CH
QB = 256
LONGEST = ROW - 3 * 128
GROUP = 3
SIZES = (2, 3, 4, 5, 6, 8)
SPACING = 3
SLOTS = 9
BT = 128
NBLK = ROW // BT


def dot_nn(a, b):
    return lax.dot_general(a, b, (((1,), (0,)), ((), ())), preferred_element_type=F32)


def dot_nt(a, b):
    return lax.dot_general(a, b, (((1,), (1,)), ((), ())), preferred_element_type=F32)


def dot_tn(a, b):
    return lax.dot_general(a, b, (((0,), (0,)), ((), ())), preferred_element_type=F32)


def own_row(seg_ref):
    return jnp.where(lax.axis_index("heads") == 0, seg_ref[0:1, :], seg_ref[1:2, :])


def iota(shape, dim):
    return lax.broadcasted_iota(jnp.int32, shape, dim)


def bucket_of(offset):
    distance = jnp.abs(offset)
    far = jnp.full(distance.shape, 8, jnp.int32)
    for edge in EDGES:
        far = far + (distance >= edge).astype(jnp.int32)
    near = jnp.where(distance < 8, distance, far)
    return near + jnp.where(offset > 0, 16, 0)


def picks_t(seg):
    lane = iota((1, ROW), 1)
    first = jnp.zeros((1, ROW), jnp.int32)
    for s in range(1, 4):
        count = jnp.sum((seg < s).astype(F32), axis=1, keepdims=True).astype(jnp.int32)
        first = jnp.where(seg == s, count, first)
    pos = lane - first
    return (iota((128, ROW), 0) == pos).astype(F32).astype(BF16)


def offset_picks(rows):
    return (bucket_of(256 - iota((rows, 512), 1)) == iota((rows, 512), 0)).astype(F32)


def key_marks(seg):
    i = iota((16, ROW), 0)
    block = iota((16, ROW), 1) // BT
    return jnp.where(i < 8, (seg == i).astype(F32), (block == i - 8).astype(F32)).astype(BF16)


def query_marks(seg, left, right):
    i = iota((16, ROW), 0)
    block = iota((16, ROW), 1) // BT
    excluded = jnp.where(jnp.logical_or(seg == i, i >= 4), 0.0, -BIG)
    j = i - 8
    far = jnp.where(j <= block - 2, left, jnp.where(j >= block + 2, right, 0.0))
    return jnp.where(i < 8, excluded, far).astype(BF16)


def attend_block(n, q, lo, base, kn, qaug, vaug, strip, pt_ref, mixed_ref, inv_ref):
    lo = jnp.minimum(lo, NBLK - n)
    rows = pl.ds(pl.multiple_of(lo * BT, BT), n * BT)
    cols = pl.ds(pl.multiple_of(q * QB, QB), QB)
    near = pl.ds(pl.multiple_of((lo - q * (QB // BT) + ROW // BT - QB // BT) * BT, BT), n * BT)

    def mix(j):
        o = dot_nn(vaug[j, :, rows], pt_ref[j, rows, :])
        inv = 1.0 / o[DH : DH + 1]
        out = pl.ds(pl.multiple_of((base + j) * DH, DH), DH)
        mixed_ref[out, cols] = (o[:DH] * inv).astype(BF16)
        inv_ref[pl.ds(base + j, 1), cols] = inv

    scores, peaks = [], []
    for j in range(GROUP):
        s = dot_nn(kn[j, rows, :], qaug[j, :, cols]) + strip[j, near, :]
        scores.append(s)
        peaks.append(jnp.max(s, axis=0, keepdims=True))
    for j in range(GROUP):
        if n < NBLK:
            pt_ref[j] = jnp.zeros((ROW, QB), BF16)
        pt_ref[j, rows, :] = jnp.exp(scores[j] - peaks[j]).astype(BF16)
        if j:
            mix(j - 1)
    mix(GROUP - 1)


def attend_heads(
    step, q, seg, table_f, span, qkv_ref, kaug, qaug, vaug, kn, strip, pt_ref, mixed_ref, inv_ref
):
    base = step * GROUP
    per = QB // BT
    zero = (ROW // BT - per) * BT
    @pl.when(q == 0)
    def _():
        for j in range(GROUP):
            rows = pl.ds(pl.multiple_of((base + j) * DH, DH), DH)
            values = table_f[pl.ds(base + j, 1), :]
            near = pltpu.roll(jnp.broadcast_to(values, (BT, 512)), 0, 1, stride=1, stride_axis=0)
            for d in range(-1, per + 1):
                for u in range(per):
                    if abs(d - u) <= 1:
                        at = 256 - 128 * (d - u)
                        strip[j, zero + d * BT : zero + (d + 1) * BT, u * BT : (u + 1) * BT] = near[
                            :, at : at + 128
                        ]
            qaug[j, 0:DH, :] = qkv_ref[0, rows, :]
            kaug[0:DH, :] = qkv_ref[1, rows, :]
            vaug[j, 0:DH, :] = qkv_ref[2, rows, :]
            qaug[j, DH : DH + 16, :] = query_marks(seg, values[:, 511:512], values[:, 1:2])
            kn[j] = kaug[...].T

    lo, n = span[0, q], span[1, q]
    last = 0
    for size in SIZES:

        @pl.when(jnp.logical_and(n > last, n <= size))
        def _():
            attend_block(size, q, lo, base, kn, qaug, vaug, strip, pt_ref, mixed_ref, inv_ref)

        last = size


def project_t(w_refs, yt, qkv_ref):
    for m in range(3):
        qkv_ref[m] = dot_tn(w_refs[m][...], yt).astype(BF16)


def head_setup(seg, tab_ref, table_f, span, kaug, qaug, vaug, strip):
    picks = offset_picks(NB).astype(BF16)
    heads = tab_ref.shape[0]
    table_f[0:heads, :] = dot_nn(tab_ref[...], picks)
    kaug[DH:, :] = jnp.zeros((128 - DH, ROW), BF16)
    qaug[:, DH:, :] = jnp.zeros((GROUP, 128 - DH, ROW), BF16)
    kaug[DH : DH + 16, :] = key_marks(seg)
    vaug[:, DH:, :] = jnp.ones((GROUP, 16, ROW), BF16)
    strip[...] = jnp.zeros(strip.shape, F32)
    for q in range(ROW // QB):
        lowest = jnp.min(seg[:, q * QB : (q + 1) * QB].astype(F32))
        highest = jnp.max(seg[:, q * QB : (q + 1) * QB].astype(F32))
        wide = seg.astype(F32)
        begin = jnp.sum((wide < lowest).astype(F32)).astype(jnp.int32) // BT
        end = (jnp.sum((wide <= highest).astype(F32)).astype(jnp.int32) + BT - 1) // BT
        span[0, q] = begin
        span[1, q] = end - begin


def forward_first(
    seg_ref, tok_ref, prompt_ref, gain_ref, wq, wk, wv, tab_ref,
    start_ref, yt_ref, qkv_ref, pt_ref, mixed_ref, inv_ref,
    table_f, span, kaug, qaug, vaug, kn, strip, padded, start_s, yt_s, qkv_s, sem, w_s, w_sem,
):
    loads = [
        pltpu.make_async_copy(w, w_s.at[m], w_sem.at[m]) for m, w in enumerate((wq, wk, wv))
    ]
    copies = [
        pltpu.make_async_copy(a, b, sem.at[k])
        for k, (a, b) in enumerate(((start_s, start_ref), (yt_s, yt_ref), (qkv_s, qkv_ref)))
    ]
    step, q = pl.program_id(0), pl.program_id(1)
    first = jnp.logical_and(step == 0, q == 0)
    seg = own_row(seg_ref)

    @pl.when(first)
    def _():
        for copy in loads:
            copy.start()
        padded[...] = jnp.zeros(padded.shape, BF16)
        padded[0:PROMPT, :] = prompt_ref[...]
        picks = picks_t(seg)
        looked = dot_tn(picks, padded[...])
        here = dot_tn(picks, (iota((128, 128), 0) < PROMPT).astype(F32).astype(BF16)) > 0.5
        tok = tok_ref[...].astype(F32)
        start = jnp.concatenate(
            [
                jnp.where(here, looked[:, c : c + 128], tok[:, c : c + 128])
                for c in range(0, D, 128)
            ],
            axis=1,
        )
        start_s[...] = start.astype(BF16)
        copies[0].start()
        inv = lax.rsqrt(jnp.mean(start * start, axis=1, keepdims=True) + EPS)
        yt = (start * inv * gain_ref[...][None, :]).astype(BF16).T
        yt_s[...] = yt
        copies[1].start()
        for copy in loads:
            copy.wait()
        project_t([w_s.at[m] for m in range(3)], yt, qkv_s)
        copies[2].start()
        head_setup(seg, tab_ref, table_f, span, kaug, qaug, vaug, strip)

    attend_heads(
        step, q, seg, table_f, span, qkv_s, kaug, qaug, vaug, kn, strip, pt_ref, mixed_ref, inv_ref
    )

    @pl.when(jnp.logical_and(step == pl.num_programs(0) - 1, q == pl.num_programs(1) - 1))
    def _():
        for copy in copies:
            copy.wait()


def forward_second(
    seg_ref, start_ref, yt_ref, gain_ref, wq, wk, wv, tab_ref, mixed_own, wo_own, wo_oth,
    qkv_ref, pt_ref, mixed_ref, inv_ref, middle_ref, x_ref, xt_ref,
    table_f, span, kaug, qaug, vaug, kn, strip, qkv_s, middle_s, x_s, xt_s, sem,
    w_s, yt_s, start_s, mixed_s, wo_s, w_sem,
):
    pairs = [(w, w_s.at[m]) for m, w in enumerate((wq, wk, wv))]
    pairs += [
        (yt_ref, yt_s), (start_ref, start_s), (mixed_own, mixed_s), (wo_own, wo_s.at[0]),
        (wo_oth, wo_s.at[1]),
    ]
    loads = [pltpu.make_async_copy(a, b, w_sem.at[k]) for k, (a, b) in enumerate(pairs)]
    qkv_copy = pltpu.make_async_copy(qkv_s, qkv_ref, sem.at[0])
    step, q = pl.program_id(0), pl.program_id(1)
    first = jnp.logical_and(step == 0, q == 0)
    seg = own_row(seg_ref)

    @pl.when(first)
    def _():
        for copy in loads:
            copy.start()
        head_setup(seg, tab_ref, table_f, span, kaug, qaug, vaug, strip)
        for copy in loads[:4]:
            copy.wait()
        project_t([w_s.at[m] for m in range(3)], yt_s[...], qkv_s)
        qkv_copy.start()

    attend_heads(
        step, q, seg, table_f, span, qkv_s, kaug, qaug, vaug, kn, strip, pt_ref, mixed_ref, inv_ref
    )

    @pl.when(jnp.logical_and(step == pl.num_programs(0) - 1, q == pl.num_programs(1) - 1))
    def _():
        for copy in loads[4:]:
            copy.wait()
        copies = []
        for k in range(0, ROW, QB):
            r = slice(k, k + QB)
            attn = dot_tn(mixed_s[:, r], wo_s[0]) + dot_tn(mixed_ref[:, r], wo_s[1])
            middle = start_s[r, :].astype(F32) + attn
            middle_s[r, :] = middle
            inv = lax.rsqrt(jnp.mean(middle * middle, axis=1, keepdims=True) + EPS)
            x = (middle * inv * gain_ref[...][None, :]).astype(BF16)
            x_s[r, :] = x
            xt_s[:, r] = x.T
            for src, dst in ((middle_s, middle_ref), (x_s, x_ref)):
                copies.append((src.at[r, :], dst.at[r, :]))
            copies.append((xt_s.at[:, r], xt_ref.at[:, r]))
            for m in range(3):
                at = 3 * (k // QB) + m
                pltpu.make_async_copy(*copies[at], sem.at[1 + at]).start()
        qkv_copy.wait()
        for at, pair in enumerate(copies):
            pltpu.make_async_copy(*pair, sem.at[1 + at]).wait()


def plan_stages(n_rows):
    n_bits = n_rows.bit_length() - 1
    size, slot = UNIT, 0
    stages, halved = [], []
    for j in range(n_bits):
        if j < n_bits - 1 and size % 32 == 0:
            size = size // 2
            halved.append((j, size))
            stages.append(("halve", j, size, slot))
        else:
            stages.append(("swap", j, size, slot))
        slot += size
    for j, n in reversed(halved):
        stages.append(("gather", j, n, slot))
        slot += n
    return stages, len(halved), slot


def stage_table(n_rows):
    stages, n_halved, _ = plan_stages(n_rows)
    n_bits = n_rows.bit_length() - 1
    me = lax.axis_index("rows")
    bits = [(me // (1 << b)) % 2 for b in range(n_bits)]
    peers = [me + (1 - 2 * bits[b]) * (1 << b) for b in range(n_bits)]
    rest = list(range(3, n_bits))
    sides = []
    for order in ([0, 2, 1] + rest, [1, 2, 0] + rest):
        bases, base, size = [], 0, UNIT
        for j in range(n_bits):
            bases.append(base)
            if j < n_halved:
                size = size // 2
                base = base + bits[order[j]] * size
        side = []
        for kind, j, n, _ in stages:
            keep = bases[j] + bits[order[j]] * n
            give = bases[j] + (1 - bits[order[j]]) * n
            src, dst = {
                "halve": (give, keep), "swap": (bases[j], bases[j]), "gather": (keep, give)
            }[kind]
            side.append((src, dst, peers[order[j]]))
        sides.append(side)
    table = [(kind, n, slot, sides[0][k], sides[1][k]) for k, (kind, _, n, slot) in enumerate(stages)]
    return table, peers


def whole(shape):
    n = len(shape)
    return pl.BlockSpec(shape, lambda *_: (0,) * n, pipeline_mode=pl.Buffered(1))


def whole_out(shape):
    n = len(shape)
    return pl.BlockSpec(shape, lambda *_: (0,) * n)


def sds(shape, dtype):
    return jax.ShapeDtypeStruct(shape, dtype)


def forward_scratch():
    return [
        pltpu.VMEM((8, 512), F32),
        pltpu.SMEM((2, ROW // QB), jnp.int32),
        pltpu.VMEM((128, ROW), BF16),
        pltpu.VMEM((GROUP, 128, ROW), BF16),
        pltpu.VMEM((GROUP, DH + 16, ROW), BF16),
        pltpu.VMEM((GROUP, ROW, 128), BF16),
        pltpu.VMEM((GROUP, 2 * ROW, QB), F32),
    ]


PARAMS = dict(vmem_limit_bytes=56 * 1024 * 1024)


def run_first(seg, tok, prompt, gain, wq, wk, wv, tab):
    cols = wq.shape[1]
    heads = cols // DH
    return pl.pallas_call(
        forward_first,
        grid=(heads // GROUP, ROW // QB),
        in_specs=[whole(a.shape) for a in (seg, tok, prompt, gain)]
        + [pl.BlockSpec(memory_space=pl.ANY)] * 3
        + [whole(tab.shape)],
        out_specs=[
            pl.BlockSpec(memory_space=pl.ANY),
            pl.BlockSpec(memory_space=pl.ANY),
            pl.BlockSpec(memory_space=pl.ANY),
            pl.BlockSpec((GROUP, ROW, QB), lambda h, q: (h, 0, q)),
            whole_out((cols, ROW)),
            whole_out((8, ROW)),
        ],
        out_shape=[
            sds((ROW, D), BF16),
            sds((D, ROW), BF16),
            sds((3, cols, ROW), BF16),
            sds((heads, ROW, ROW), BF16),
            sds((cols, ROW), BF16),
            sds((8, ROW), F32),
        ],
        scratch_shapes=forward_scratch() + [
            pltpu.VMEM((128, D), BF16),
            pltpu.VMEM((ROW, D), BF16),
            pltpu.VMEM((D, ROW), BF16),
            pltpu.VMEM((3, cols, ROW), BF16),
            pltpu.SemaphoreType.DMA((3,)),
            pltpu.VMEM((3, D, cols), BF16),
            pltpu.SemaphoreType.DMA((3,)),
        ],
        compiler_params=pltpu.CompilerParams(**PARAMS),
        cost_estimate=pl.CostEstimate(flops=2 * 10**10, bytes_accessed=10**7, transcendentals=0),
        name="attend_own",
    )(seg, tok, prompt, gain, wq, wk, wv, tab)


def run_second(seg, start, yt, gain, wq, wk, wv, tab, mixed_own, wo_own, wo_oth):
    cols = wq.shape[1]
    heads = cols // DH
    ins = (seg, start, yt, gain, wq, wk, wv, tab, mixed_own, wo_own, wo_oth)
    return pl.pallas_call(
        forward_second,
        grid=(heads // GROUP, ROW // QB),
        in_specs=[
            whole(a.shape) if a is seg or a is gain or a is tab else pl.BlockSpec(memory_space=pl.ANY)
            for a in ins
        ],
        out_specs=[
            pl.BlockSpec(memory_space=pl.ANY),
            pl.BlockSpec((GROUP, ROW, QB), lambda h, q: (h, 0, q)),
            whole_out((cols, ROW)),
            whole_out((8, ROW)),
            pl.BlockSpec(memory_space=pl.ANY),
            pl.BlockSpec(memory_space=pl.ANY),
            pl.BlockSpec(memory_space=pl.ANY),
        ],
        out_shape=[
            sds((3, cols, ROW), BF16),
            sds((heads, ROW, ROW), BF16),
            sds((cols, ROW), BF16),
            sds((8, ROW), F32),
            sds((ROW, D), F32),
            sds((ROW, D), BF16),
            sds((D, ROW), BF16),
        ],
        scratch_shapes=forward_scratch() + [
            pltpu.VMEM((3, cols, ROW), BF16),
            pltpu.VMEM((ROW, D), F32),
            pltpu.VMEM((ROW, D), BF16),
            pltpu.VMEM((D, ROW), BF16),
            pltpu.SemaphoreType.DMA((1 + 3 * (ROW // QB),)),
            pltpu.VMEM((3, D, cols), BF16),
            pltpu.VMEM((D, ROW), BF16),
            pltpu.VMEM((ROW, D), BF16),
            pltpu.VMEM((cols, ROW), BF16),
            pltpu.VMEM((2, cols, D), BF16),
            pltpu.SemaphoreType.DMA((8,)),
        ],
        compiler_params=pltpu.CompilerParams(**PARAMS),
        cost_estimate=pl.CostEstimate(flops=2 * 10**10, bytes_accessed=10**7, transcendentals=0),
        name="attend_other",
    )(*ins)


def norm_back(value, gain, grad):
    inv = lax.rsqrt(jnp.mean(value * value, axis=1, keepdims=True) + EPS)
    scaled = grad * gain
    inner = jnp.mean(scaled * value, axis=1, keepdims=True)
    back = inv * scaled - value * (inv * inv * inv * inner)
    return back, jnp.sum(grad * (value * inv), axis=0, keepdims=True)


def backward(
    n_ff, n_heads, n_rows,
    seg_ref, gain_a_ref, gain_f_ref, win_own, win_oth, wout_own, wout_oth, pt_own, pt_oth,
    x_hbm, xt_hbm, og_hbm, mid_hbm, start_hbm, yt_hbm, qkv_own_hbm, qkv_oth_hbm,
    mix_own_hbm, mix_oth_hbm, inv_own_hbm, inv_oth_hbm, wq_own_hbm, wk_own_hbm, wv_own_hbm, wq_oth_hbm, wk_oth_hbm,
    wv_oth_hbm, wo_own_hbm, wo_oth_hbm,
    result_hbm, gtok_hbm, out_in, out_out, out_q, out_k, out_v, out_o, out_small,
    x, xt, og, mid, qkv, mix, inv, gmix, wqkv, wo, feed, gnf, dst, dqkv, kaug, vaug, doaug,
    tacc, gvec, gains, ptb, g, xsend, xrecv, ring, load_sem, late_sem, pt_sem, out_sem, xs_sem, xr_sem,
    send_sem, recv_sem,
):
    s = pl.program_id(0)
    heads_half = n_heads // 2
    cols = heads_half * DH
    me = lax.axis_index("heads")
    early = [(x_hbm, x), (xt_hbm, xt), (og_hbm, og)]
    later = [
        (mid_hbm, mid),
        (qkv_own_hbm, qkv.at[0]),
        (qkv_oth_hbm, qkv.at[1]),
        (mix_own_hbm, mix.at[0]),
        (mix_oth_hbm, mix.at[1]),
        (inv_own_hbm, inv.at[0]),
        (inv_oth_hbm, inv.at[1]),
        (wq_own_hbm, wqkv.at[0, 0]),
        (wk_own_hbm, wqkv.at[0, 1]),
        (wv_own_hbm, wqkv.at[0, 2]),
        (wq_oth_hbm, wqkv.at[1, 0]),
        (wk_oth_hbm, wqkv.at[1, 1]),
        (wv_oth_hbm, wqkv.at[1, 2]),
        (wo_own_hbm, wo.at[0]),
        (wo_oth_hbm, wo.at[1]),
    ]
    n_early = len(early)
    loads = [
        pltpu.make_async_copy(a, b, load_sem.at[i]) for i, (a, b) in enumerate(early + later)
    ]
    late = [
        pltpu.make_async_copy(start_hbm, x, late_sem.at[0]),
        pltpu.make_async_copy(yt_hbm, xt, late_sem.at[1]),
    ]

    def pt_start(i):
        hh = 2 * (i // 4) + i % 2
        for o, ref in enumerate((pt_own, pt_oth)):

            @pl.when((i % 4) // 2 == o)
            def _():
                pltpu.make_async_copy(ref.at[hh], ptb.at[i % 2], pt_sem.at[i % 2]).start()

    n_out = cols // 128
    n_chunks = 2 * n_ff + 4 * n_out + 1
    n_units = n_chunks
    table, peers = stage_table(n_rows)
    n_stages = len(table)
    core = {"heads": 1 - me}

    def swap(slot):
        return pltpu.make_async_remote_copy(
            src_ref=xsend.at[slot],
            dst_ref=xrecv.at[slot],
            send_sem=xs_sem.at[slot],
            recv_sem=xr_sem.at[slot],
            device_id=core,
            device_id_type=pl.DeviceIdType.MESH,
        )

    def emit(c, slot, own, oth):
        for blocks, ref in ((own, g.at[c]), (oth, xsend.at[slot])):
            for b, block in enumerate(blocks):
                n = block.shape[0]
                ref[b * n : (b + 1) * n, :] = block.astype(BF16)
        swap(slot).start()

    def collect(c, slot):
        swap(slot).wait()
        g[c] = (g[c].astype(F32) + xrecv[slot].astype(F32)).astype(BF16)

    def stage_copy(k, c, par, odd):
        kind, n, slot, even_side, odd_side = table[k]
        src, dst, peer = (p + odd * (q - p) for p, q in zip(even_side, odd_side))
        copy = pltpu.make_async_remote_copy(
            src_ref=g.at[c, pl.ds(pl.multiple_of(src, 16), n), :],
            dst_ref=ring.at[par, slot : slot + n, :],
            send_sem=send_sem.at[k, par],
            recv_sem=recv_sem.at[k, par],
            device_id={"rows": peer},
            device_id_type=pl.DeviceIdType.MESH,
        )
        return copy, pl.ds(pl.multiple_of(dst, 16), n)

    def stage_end(k, c, par, odd):
        kind, n, slot = table[k][:3]
        copy, dst = stage_copy(k, c, par, odd)
        copy.wait()
        part = ring[par, slot : slot + n, :]
        if kind != "gather":
            part = (g[c, dst, :].astype(F32) + part.astype(F32)).astype(BF16)
        g[c, dst, :] = part

    def out_wait(par):
        pltpu.make_async_copy(g.at[0], out_in.at[:, 0:128], out_sem.at[par]).wait()

    def out_start(c, odd):
        sem = out_sem.at[odd]

        @pl.when(c >= 2)
        def _():
            out_wait(odd)

        def wide(ref, col):
            dst = ref.at[:, pl.ds(pl.multiple_of(col * 128, 128), 128)]
            pltpu.make_async_copy(g.at[c], dst, sem).start()

        def tall(ref, row):
            pltpu.make_async_copy(g.at[c], ref.at[row], sem).start()

        base = 2 * n_ff + n_out

        @pl.when(jnp.logical_and(c < 2 * n_ff, odd == 0))
        def _():
            wide(out_in, c // 2)

        @pl.when(jnp.logical_and(c < 2 * n_ff, odd == 1))
        def _():
            tall(out_out, c // 2)

        @pl.when(c >= 2 * n_ff)
        def _():
            @pl.when(c < base)
            def _():
                tall(out_o, c - 2 * n_ff)

            for m, ref in enumerate((out_q, out_k, out_v)):
                at = jnp.logical_and(c >= base, c < n_chunks - 1)

                @pl.when(jnp.logical_and(at, (c - base) % 3 == m))
                def _():
                    wide(ref, (c - base) // 3)

            @pl.when(c == n_chunks - 1)
            def _():
                tall(out_small, 0)

    wo_end = 2 * n_ff + n_out
    holes = ((wo_end, 3), (wo_end + 6, 2))

    def tick(t):
        turn = lax.rem(t, SLOTS)
        parity = lax.rem(t, 2)
        for k in range(n_stages, -1, -1):
            v = t - SPACING * k
            c = v
            live_unit = v >= 0
            for at, length in holes:
                c = c - jnp.where(v >= at + length, length, 0)
                live_unit = jnp.logical_and(live_unit, jnp.logical_or(v < at, v >= at + length))
            par = turn + (-SPACING * k) % SLOTS
            par = par - jnp.where(par >= SLOTS, SLOTS, 0)
            odd = parity if SPACING * k % 2 == 0 else 1 - parity

            def step(k=k, c=c, par=par, odd=odd):
                if k > 0:
                    stage_end(k - 1, c, par, odd)
                if k < n_stages:
                    stage_copy(k, c, par, odd)[0].start()
                else:
                    out_start(c, odd)

            pl.when(jnp.logical_and(live_unit, c < n_units))(step)

    def collect_ff(e):
        for j in range(2):
            collect(2 * e + j, 2 * (e % 4) + j)

    def group_slot(e, m):
        return 3 + m if e % 2 == 0 else m

    def collect_group(e):
        for m in range(3):
            collect((2 * n_ff + n_out + 3 * e + m), group_slot(e, m))

    def lanes(a):
        return [a[:, k : k + 128] for k in range(0, a.shape[1], 128)]

    @pl.when(s == 0)
    def _():
        for copy in loads:
            copy.start()
        barrier = pltpu.get_barrier_semaphore()
        for peer in [{"rows": p} for p in peers] + [core]:
            pl.semaphore_signal(
                barrier, inc=1, device_id=peer, device_id_type=pl.DeviceIdType.MESH
            )
        pl.semaphore_wait(barrier, len(peers) + 1)
        feed[...] = jnp.zeros(feed.shape, F32)
        gnf[...] = jnp.zeros(gnf.shape, F32)
        for copy in loads[:n_early]:
            copy.wait()

    @pl.when(s < n_ff)
    def _():
        wi = jnp.concatenate([win_own[...], win_oth[...]], axis=1)
        wout = jnp.concatenate([wout_own[...], wout_oth[...]], axis=0)
        halves = [slice(0, ROW // 2), slice(ROW // 2, ROW)]
        pres = [dot_nn(x[r, :], wi) for r in halves]
        gacts = [dot_nt(og[r, :], wout) for r in halves]
        acts, gpres = [], []
        for pre, gact in zip(pres, gacts):
            cdf = 0.5 * (1.0 + lax.erf(pre * ROOT_HALF))
            acts.append((pre * cdf).astype(BF16))
            slope = cdf + pre * jnp.exp(-0.5 * pre * pre) * DENSITY
            gpres.append((gact * slope).astype(BF16))
        for r, act, gpre in zip(halves, acts, gpres):
            feed[r, :] += dot_nn(act, wout)
            gnf[r, :] += dot_nt(gpre, wi)
        active = jnp.concatenate(acts, axis=0)
        gpre = jnp.concatenate(gpres, axis=0)

        @pl.when(s >= 1)
        def _():
            collect_ff(s - 1)
            tick(2 * (s - 1))

        dwin = dot_nn(xt[...], gpre)
        dwout = dot_tn(active, og[...])

        emit(2 * s, 2 * (s % 4), [dwin[:, :FFC]], [dwin[:, FFC:]])
        emit(2 * s + 1, 2 * (s % 4) + 1, lanes(dwout[:FFC]), lanes(dwout[FFC:]))

        @pl.when(s >= 1)
        def _():
            tick(2 * (s - 1) + 1)

    @pl.when(s == n_ff)
    def _():
        for copy in late:
            copy.start()
        pt_start(0)
        for copy in loads[n_early:]:
            copy.wait()
        t0 = 2 * (n_ff - 2)
        middle = mid[...]
        dst[:, 0:D] = (middle + feed[...]).astype(BF16)
        to_result = pltpu.make_async_copy(dst.at[:, 0:D], result_hbm, late_sem.at[2])
        to_result.start()
        back, gain_grad = norm_back(middle, gain_f_ref[...][None, :], gnf[...])
        gmid = og[...].astype(F32) + back
        gains[0:1, :] = gain_grad
        mid[...] = gmid
        ga = gmid.astype(BF16)
        dwo = [dot_nn(mix[o], ga) for o in range(2)]
        collect_ff(n_ff - 1)
        for j in range(n_out):
            rows = slice(j * 128, (j + 1) * 128)
            emit((2 * n_ff + j), j, lanes(dwo[0][rows]), lanes(dwo[1][rows]))
        for o in range(2):
            grad = dot_nt(wo[o], ga)
            for k in range(heads_half):
                rows = slice(k * DH, (k + 1) * DH)
                gmix[o, rows, :] = (grad[rows] * inv[o, k : k + 1, :]).astype(BF16)
        tick(t0 + 2)
        gnf[...] = jnp.zeros(gnf.shape, F32)
        kaug[DH:, :] = key_marks(own_row(seg_ref))
        vaug[DH:, :] = (iota((16, ROW), 0) < 3).astype(F32).astype(BF16)
        gvec[...] = jnp.zeros(gvec.shape, F32)
        to_result.wait()
        dst[...] = jnp.zeros(dst.shape, BF16)
        for copy in late:
            copy.wait()
        tick(t0 + 3)

    i = s - (n_ff + 1)

    def head_back(o, pt_ref):
        hh = 2 * (i // 4) + i % 2
        rows = pl.ds(pl.multiple_of(hh * DH, DH), DH)
        dot_ = gmix[o, rows, :]
        delta = jnp.sum(dot_.astype(F32) * mix[o, rows, :].astype(F32), axis=0, keepdims=True)
        d1 = delta.astype(BF16).astype(F32)
        d2 = (delta - d1).astype(BF16).astype(F32)
        d3 = delta - d1 - d2
        k = iota((16, ROW), 0)
        vaug[0:DH, :] = qkv[o, 2, rows, :]
        kaug[0:DH, :] = qkv[o, 1, rows, :]
        doaug[0:DH, :] = dot_
        doaug[DH:, :] = jnp.where(
            k == 0, -d1, jnp.where(k == 1, -d2, jnp.where(k == 2, -d3, 0.0))
        ).astype(BF16)
        va = vaug[...]
        ka = kaug[...]
        out_rows = pl.ds(pl.multiple_of(o * 128 + (i % 2) * DH, DH), DH)
        tacc[...] = jnp.zeros(tacc.shape, F32)
        left = jnp.zeros((1, QB), F32)
        right = jnp.zeros((1, QB), F32)
        n_blocks = ROW // QB

        def live(b):
            ks = [
                kb for kb in range(NBLK)
                if max(kb * BT - (b + 1) * QB, b * QB - (kb + 1) * BT) + 1 < LONGEST
            ]
            return slice(ks[0] * BT, (ks[-1] + 1) * BT)

        def grad_probs(b):
            return dot_tn(va[:, live(b)], doaug[:, b * QB : (b + 1) * QB])

        dp = grad_probs(0)
        dqkv[2, out_rows, :] = dot_nt(dot_, pt_ref[...]).astype(BF16)
        for b in range(n_blocks):
            qs = slice(b * QB, (b + 1) * QB)
            ahead = grad_probs(b + 1) if b + 1 < n_blocks else None
            ks = live(b)
            ds = pt_ref[ks, qs].astype(F32) * dp
            for u in range(QB // BT):
                qb = b * (QB // BT) + u
                for d in (-1, 0, 1):
                    kb = qb + d
                    if 0 <= kb < NBLK:
                        at = kb * BT - ks.start
                        tacc[:, 256 - 128 * d : 384 - 128 * d] += ds[
                            at : at + BT, u * BT : (u + 1) * BT
                        ]
            dst[ks, qs] = ds.astype(BF16)
            dp = ahead
        for b in range(n_blocks):
            qs = slice(b * QB, (b + 1) * QB)
            r = dot_nn(ka[:, live(b)], dst[live(b), qs])
            dqkv[0, out_rows, qs] = r[:DH].astype(BF16)
            sums = r[DH + 8 :]
            j = iota((8, QB), 0)
            block = b * (QB // BT) + iota((8, QB), 1) // BT
            left = left + jnp.sum(jnp.where(j <= block - 2, sums, 0.0), axis=0, keepdims=True)
            right = right + jnp.sum(jnp.where(j >= block + 2, sums, 0.0), axis=0, keepdims=True)
        dqkv[1, out_rows, :] = dot_nt(qkv[o, 0, rows, :], dst[...]).astype(BF16)
        flip = (iota((BT, BT), 0) + iota((BT, BT), 1) == BT - 1).astype(F32).astype(BF16)
        near = tacc[...]
        high = near.astype(BF16)
        low = (near - high.astype(F32)).astype(BF16)
        turned = dot_nn(flip, high) + dot_nn(flip, low)
        skew = pltpu.roll(turned, 0, 1, stride=1, stride_axis=0)
        vec = pltpu.roll(jnp.sum(skew, axis=0, keepdims=True), 512 - (BT - 1), 1)
        lane = iota((1, 512), 1)
        vec = vec + jnp.where(lane == 511, jnp.sum(left, axis=1, keepdims=True), 0.0)
        vec = vec + jnp.where(lane == 1, jnp.sum(right, axis=1, keepdims=True), 0.0)
        owner = me + o * (1 - 2 * me)
        gvec[pl.ds(owner * heads_half + hh, 1), :] = vec

    in_heads = jnp.logical_and(i >= 0, i < n_heads)

    @pl.when(in_heads)
    def _():
        @pl.when(i + 1 < n_heads)
        def _():
            pt_start(i + 1)

        pltpu.make_async_copy(pt_own.at[0], ptb.at[i % 2], pt_sem.at[i % 2]).wait()
        head_back((i % 4) // 2, ptb.at[i % 2])

        @pl.when(i == 0)
        def _():
            for j in range(n_out):
                collect((2 * n_ff + j), j)

        for e in range(n_heads // 4 - 1):

            @pl.when(i == 4 * (e + 1) + 1)
            def _():
                collect_group(e)

        tick(2 * n_ff + i + i // 4)

    def group_back(grp):
        for m in range(3):
            dw = dot_nt(xt[...], dqkv[m])
            emit(
                2 * n_ff + n_out + 3 * grp + m, group_slot(grp, m),
                [dw[:, :128]], [dw[:, 128:]],
            )
        cols_g = slice(grp * 128, (grp + 1) * 128)
        for m in range(3):
            w = jnp.concatenate([wqkv[0, m, :, cols_g], wqkv[1, m, :, cols_g]], axis=1)
            gnf[...] += lax.dot_general(
                dqkv[m], w, (((0,), (1,)), ((), ())), preferred_element_type=F32
            )
        if grp < 2:
            tick(2 * n_ff + 5 * grp + 4)

    for grp in range(n_heads // 4):

        @pl.when(i == 4 * grp + 3)
        def _():
            group_back(grp)

    @pl.when(i == n_heads)
    def _():
        seg = own_row(seg_ref)
        start = x[...].astype(F32)
        back, gain_grad = norm_back(start, gain_a_ref[...][None, :], gnf[...])
        gstart = mid[...] + back
        n_groups = n_heads // 4
        collect_group(n_groups - 1)
        t0 = 2 * n_ff + n_heads + 2
        tick(t0)
        picks = picks_t(seg)
        here = dot_tn(picks, (iota((128, 128), 0) < PROMPT).astype(F32).astype(BF16)) > 0.5
        for c in range(0, D, 128):
            og[:, c : c + 128] = jnp.where(here, 0.0, gstart[:, c : c + 128]).astype(BF16)
        to_gtok = pltpu.make_async_copy(og, gtok_hbm, late_sem.at[0])
        to_gtok.start()
        high = gstart.astype(BF16)
        low = (gstart - high.astype(F32)).astype(BF16)
        tick(t0 + 1)
        gprompt = dot_nn(picks, high) + dot_nn(picks, low)
        opicks = offset_picks(128).astype(BF16)
        gv = gvec[...]
        g1 = gv.astype(BF16)
        g2 = (gv - g1.astype(F32)).astype(BF16)
        gtab = dot_nt(g1, opicks) + dot_nt(g2, opicks)
        row = iota((128, D), 0)
        small = jnp.where(row < PROMPT, gprompt, 0.0)
        small = jnp.where(row == PROMPT, gain_grad, small)
        small = jnp.where(row == PROMPT + 1, gains[0:1, :], small)
        blocks = lanes(small)
        wide = jnp.concatenate([jnp.zeros((104, 128), F32), gtab, jnp.zeros((8, 128), F32)], axis=0)
        blocks[0] = blocks[0] + wide
        slot = group_slot(n_groups, 0)
        emit((n_chunks - 1), slot, blocks, blocks)
        tick(t0 + 2)
        collect((n_chunks - 1), slot)

        @pl.loop(t0 + 3, n_units + sum(h[1] for h in holes) + SPACING * n_stages)
        def _(t):
            tick(t)

        to_gtok.wait()
        out_wait(0)
        out_wait(1)


def run_backward(
    n_rows, seg, gain_a, gain_f, win_own, win_oth, wout_own, wout_oth, pt_own, pt_oth, rest
):
    n_ff = win_own.shape[1] // FFC
    n_heads = 2 * pt_own.shape[0]
    cols = n_heads * DH // 2
    n_chunks = 2 * n_ff + 4 * (cols // 128) + 1
    first = n_ff + 1
    stages, _, ring_rows = plan_stages(n_rows)
    n_stages = len(stages)

    def ff(s):
        return jnp.minimum(s, n_ff - 1)

    blk_in = pl.BlockSpec((D, FFC), lambda s: (0, ff(s)))
    blk_out = pl.BlockSpec((FFC, D), lambda s: (ff(s), 0))
    anyspec = pl.BlockSpec(memory_space=pl.ANY)
    return pl.pallas_call(
        partial(backward, n_ff, n_heads, n_rows),
        grid=(first + n_heads + 1,),
        in_specs=[
            whole(seg.shape), whole(gain_a.shape), whole(gain_f.shape),
            blk_in, blk_in, blk_out, blk_out,
        ] + [anyspec] * (2 + len(rest)),
        out_specs=[anyspec] * 9,
        out_shape=[sds((ROW, D), BF16), sds((ROW, D), BF16)] + [
            sds(shape, BF16)
            for shape in (win_own.shape, (n_ff, CH, 128))
            + ((D, cols),) * 3 + ((cols // 128, CH, 128), (1, CH, 128))
        ],
        scratch_shapes=[
            pltpu.VMEM((ROW, D), BF16),
            pltpu.VMEM((D, ROW), BF16),
            pltpu.VMEM((ROW, D), BF16),
            pltpu.VMEM((ROW, D), F32),
            pltpu.VMEM((2, 3, cols, ROW), BF16),
            pltpu.VMEM((2, cols, ROW), BF16),
            pltpu.VMEM((2, 8, ROW), F32),
            pltpu.VMEM((2, cols, ROW), BF16),
            pltpu.VMEM((2, 3, D, cols), BF16),
            pltpu.VMEM((2, cols, D), BF16),
            pltpu.VMEM((ROW, D), F32),
            pltpu.VMEM((ROW, D), F32),
            pltpu.VMEM((ROW, ROW), BF16),
            pltpu.VMEM((3, 256, ROW), BF16),
            pltpu.VMEM((DH + 16, ROW), BF16),
            pltpu.VMEM((DH + 16, ROW), BF16),
            pltpu.VMEM((DH + 16, ROW), BF16),
            pltpu.VMEM((BT, 512), F32),
            pltpu.VMEM((16, 512), F32),
            pltpu.VMEM((8, D), F32),
            pltpu.VMEM((2, ROW, ROW), BF16),
            pltpu.VMEM((n_chunks, UNIT, 128), BF16),
            pltpu.VMEM((8, CH, 128), BF16),
            pltpu.VMEM((8, CH, 128), BF16),
            pltpu.VMEM((SLOTS, ring_rows, 128), BF16),
            pltpu.SemaphoreType.DMA((18,)),
            pltpu.SemaphoreType.DMA((3,)),
            pltpu.SemaphoreType.DMA((2,)),
            pltpu.SemaphoreType.DMA((2,)),
            pltpu.SemaphoreType.DMA((8,)),
            pltpu.SemaphoreType.DMA((8,)),
            pltpu.SemaphoreType.DMA((n_stages, SLOTS)),
            pltpu.SemaphoreType.DMA((n_stages, SLOTS)),
        ],
        compiler_params=pltpu.CompilerParams(
            vmem_limit_bytes=62 * 1024 * 1024, collective_id=0, has_side_effects=True
        ),
        name="backward",
    )(seg, gain_a, gain_f, win_own, win_oth, wout_own, wout_oth, pt_own, pt_oth, *rest)


def untile(src, dst):
    for c in range(src.shape[0]):
        for b in range(D // 128):
            dst[c * 128 : (c + 1) * 128, b * 128 : (b + 1) * 128] = src[
                c, b * 128 : (b + 1) * 128, :
            ].astype(F32)


def finish(
    heads, result, gtok, small, g_q, g_k, g_v, g_wo, g_in, g_out,
    o_result, o_gtok, o_prompt, o_gain_a, o_q, o_k, o_v, o_wo, o_tab, o_gain_f, o_in, o_out, rows,
):
    o_result[...] = result[...]
    o_gtok[...] = gtok[...]
    for src, dst in ((g_q, o_q), (g_k, o_k), (g_v, o_v), (g_in, o_in)):
        dst[...] = src[...].astype(F32)
    untile(g_out, o_out)

    @pl.when(pl.program_id(0) == 0)
    def _():
        untile(small, rows)
        untile(g_wo, o_wo)
        o_prompt[...] = rows[0:PROMPT, :]
        o_gain_a[...] = rows[PROMPT, :]
        o_gain_f[...] = rows[PROMPT + 1, :]
        low = lax.axis_index("heads") == 0
        at = 104
        tab = [
            jnp.where(low, rows[at + k : at + k + 1, 0:128], rows[at + heads + k : at + heads + k + 1, 0:128])
            for k in range(heads)
        ]
        tab.append(jnp.zeros((8 - heads, 128), F32))
        o_tab[...] = jnp.concatenate(tab, axis=0)[0:heads, 0:NB]


def run_finish(heads, result, gtok, small, *grads):
    steps = 2

    def part(shape):
        zeros = (0,) * (len(shape) - 1)
        return pl.BlockSpec((shape[0] // steps,) + shape[1:], lambda i: (i,) + zeros)

    g_q, g_k, g_v, g_wo, g_in, g_out = grads
    wo_shape, out_shape = ((a.shape[0] * 128, D) for a in (g_wo, g_out))
    whole_1d = pl.BlockSpec((D,), lambda i: (0,))
    return pl.pallas_call(
        partial(finish, heads),
        grid=(steps,),
        in_specs=[part(result.shape), part(gtok.shape), whole(small.shape)]
        + [part(a.shape) for a in (g_q, g_k, g_v)]
        + [whole(g_wo.shape), part(g_in.shape), part(g_out.shape)],
        out_specs=[part(result.shape), part(gtok.shape), whole_out((PROMPT, D)), whole_1d]
        + [part(a.shape) for a in (g_q, g_k, g_v)]
        + [whole_out(wo_shape), whole_out((heads, NB)), whole_1d, part(g_in.shape), part(out_shape)],
        out_shape=[sds(result.shape, BF16), sds(gtok.shape, BF16), sds((PROMPT, D), F32), sds((D,), F32)]
        + [sds(a.shape, F32) for a in (g_q, g_k, g_v)]
        + [sds(wo_shape, F32), sds((heads, NB), F32), sds((D,), F32)]
        + [sds(g_in.shape, F32), sds(out_shape, F32)],
        scratch_shapes=[pltpu.VMEM((128, D), F32)],
        compiler_params=pltpu.CompilerParams(vmem_limit_bytes=62 * 1024 * 1024),
        name="finish",
    )(result, gtok, small, *grads)


def on_device(
    tokens, prompt, segment_ids, gain_attn, w_query, w_key, w_value, w_attn_out, bias_table,
    gain_ff, w_in, w_out, out_grad,
):
    seg = segment_ids
    swap = [(0, 1), (1, 0)]

    def other(a):
        return lax.ppermute(a, "heads", swap)

    tab_oth, wq_oth, wk_oth, wv_oth = (other(a) for a in (bias_table.T, w_query, w_key, w_value))
    wo_oth, win_oth, wout_oth = other(w_attn_out), other(w_in), other(w_out)
    gain_a, gain_f = gain_attn, gain_ff
    start, yt, qkv_own, pt_own, mix_own, inv_own = run_first(
        seg, tokens, prompt, gain_a, w_query, w_key, w_value, bias_table.T
    )
    qkv_oth, pt_oth, mix_oth, inv_oth, middle, x, xt = run_second(
        seg, start, yt, gain_f, wq_oth, wk_oth, wv_oth, tab_oth, mix_own, w_attn_out, wo_oth
    )
    result, gtok, g_in, g_out, g_q, g_k, g_v, g_wo, small = run_backward(
        lax.axis_size("rows"),
        seg, gain_a, gain_f, w_in, win_oth, w_out, wout_oth, pt_own, pt_oth,
        [x, xt, out_grad, middle, start, yt, qkv_own, qkv_oth, mix_own, mix_oth,
         inv_own, inv_oth,
         w_query, w_key, w_value, wq_oth, wk_oth, wv_oth, w_attn_out, wo_oth],
    )
    (
        result, gtok, g_prompt, g_gain_a, g_q, g_k, g_v, g_wo, g_tab, g_gain_f, g_in, g_out,
    ) = run_finish(bias_table.shape[1], result, gtok, small, g_q, g_k, g_v, g_wo, g_in, g_out)
    return (
        result, gtok, g_prompt, g_gain_a, g_q, g_k, g_v, g_wo, g_tab.T, g_gain_f, g_in, g_out,
    )


def solution(mesh):
    both = P(("rows", "heads"), None)
    cols = P(None, "heads")
    rows = P("heads", None)
    in_specs = (
        both, P(), P("rows", None), P(), cols, cols, cols, rows, cols, P(), cols, rows, both,
    )
    out_specs = (both, both, P(), P(), cols, cols, cols, rows, cols, P(), cols, rows)
    return jax.shard_map(
        on_device, mesh=mesh, in_specs=in_specs, out_specs=out_specs, check_vma=False
    )
```
